32 devices in a mesh: dp: 8 (over z, y), blk: 4 (over x, core).
Axes of the slice: x: 2, y: 2, z: 4, core: 2. Of those that a mesh axis runs over, the one named last changes fastest.
Arguments:
- tokens: bfloat16 [8, 1024, 768], P('dp', 'blk'), may hold values from -6 to 6
- segment_ids: int32 [8, 1024], P('dp', 'blk'), may hold values from 0 to 510, as said below
- w_query: bfloat16 [768, 768], P(('dp', 'blk')), may hold values from -0.109375 to 0.109375
- w_key: bfloat16 [768, 768], P(('dp', 'blk')), may hold values from -0.109375 to 0.109375
- w_value: bfloat16 [768, 768], P(('dp', 'blk')), may hold values from -0.21875 to 0.21875
- w_attn_out: bfloat16 [768, 768], P(('dp', 'blk')), may hold values from -1.75 to 1.75
- attn_gain: bfloat16 [768], P(('dp', 'blk')), may hold values from 0.099609375 to 1.8984375
- rel_bias: bfloat16 [32, 12], replicated, may hold values from -4 to 4
- w_gate: bfloat16 [768, 2048], P(('dp', 'blk')), may hold values from -0.21875 to 0.21875
- w_up: bfloat16 [768, 2048], P(('dp', 'blk')), may hold values from -0.21875 to 0.21875
- w_down: bfloat16 [2048, 768], P(('dp', 'blk')), may hold values from -0.125 to 0.125
- ffn_gain: bfloat16 [768], P(('dp', 'blk')), may hold values from 0.099609375 to 1.8984375
- cotangent: bfloat16 [8, 1024, 768], P('dp', 'blk'), may hold values from -6 to 6
Outputs:
- layer_out: bfloat16 [8, 1024, 768], P('dp', 'blk')
- tokens_grad: float32 [8, 1024, 768], P('dp', 'blk')
- w_query_grad: float32 [768, 768], P(('dp', 'blk'))
- w_key_grad: float32 [768, 768], P(('dp', 'blk'))
- w_value_grad: float32 [768, 768], P(('dp', 'blk'))
- w_attn_out_grad: float32 [768, 768], P(('dp', 'blk'))
- attn_gain_grad: float32 [768], P(('dp', 'blk'))
- rel_bias_grad: float32 [32, 12], replicated
- w_gate_grad: float32 [768, 2048], P(('dp', 'blk'))
- w_up_grad: float32 [768, 2048], P(('dp', 'blk'))
- w_down_grad: float32 [2048, 768], P(('dp', 'blk'))
- ffn_gain_grad: float32 [768], P(('dp', 'blk'))
The draws below stay inside these ranges and needn't reach their ends.
Inputs may be any that keep to these rules, and one draw needn't show every extreme that they name: `segment_ids`: segment ids start at 0 in each row, never fall along it, and end at 510 in each row; ids need not be consecutive. Each row holds one document that begins within its first 256 tokens and ends within its last 256 tokens; every other document is shorter than 256 tokens.
All inputs are finite; a program needn't handle non-finite values.
Results may differ from the reference program's by a relative error of at most 0.02.
Values may be sent and summed in bfloat16 or wider, within the bound.
No kernel may reach another device: no remote copies, remote signals or barrier semaphores. Data moves between devices by JAX's collectives and lax.ppermute only.
A program may use at most 128 MiB of HBM per device.

```python
import math
import jax
import jax.numpy as jnp
from jax import lax

D = 768
H = 12
DH = 64
FF = 2048
NB = 32
TOK_DEV = 256
L = 1024
ROWS = 8


def draw_segment_ids(key, part):
    key = jax.random.fold_in(key, 11)
    first_key, last_key, cut_key = jax.random.split(key, 3)
    first = jax.random.randint(first_key, (ROWS, 1), 1, TOK_DEV)
    last = jax.random.randint(last_key, (ROWS, 1), L - TOK_DEV + 1, L)
    cuts = jax.random.randint(cut_key, (ROWS, L), 0, 24) == 0
    place = jnp.arange(L, dtype=jnp.int32)[None, :]
    inside = (place > first) & (place < last)
    starts = (jnp.where(inside, False, cuts) | (place == first) | (place == last)) & (place > 0)
    counted = jnp.cumsum(starts.astype(jnp.int32), axis=1).astype(jnp.int32)
    top = counted[:, -1:]
    spread = 2 * TOK_DEV - 2
    return (counted * spread // top).astype(jnp.int32)


def level_of(key, extent, cuts, least, largest):
    def one(axis_at, blocks):
        heights = jax.random.uniform(jax.random.fold_in(jax.random.fold_in(key, 6), axis_at), (blocks,), jnp.float32, least / len(cuts), largest / len(cuts))
        return jnp.repeat(jnp.exp(heights), extent[axis_at] // blocks).reshape((-1,) + (1,) * (len(extent) - axis_at - 1))

    factor_of = one(*cuts[0])
    for cut in cuts[1:]:
        factor_of = factor_of * one(*cut)
    return factor_of


def scatter_about(rng, extent, scale, reach, cuts=(), held_as=jnp.bfloat16):
    level = level_of(rng, extent, cuts, -0.22, 0.18) if cuts else 1.0
    entries = jax.random.normal(rng, extent, jnp.float32) * scale * level
    return jnp.minimum(jnp.maximum(entries, -reach), reach).astype(held_as)


def setup_inputs(seed: int = 0) -> dict:
    key_list = jax.random.split(jax.random.key(seed), 14)
    tokens = scatter_about(key_list[0], (ROWS, L, D), 1.0, 6.0, ((0, 8), (1, 4)))
    segment_ids = draw_segment_ids(jax.random.fold_in(key_list[13], 71), 0)
    w_query = scatter_about(key_list[2], (D, H * DH), (4 * D) ** -0.5, 0.109375, ((0, 32),))
    w_key = scatter_about(key_list[3], (D, H * DH), (4 * D) ** -0.5, 0.109375, ((0, 32),))
    w_value = scatter_about(key_list[4], (D, H * DH), D ** -0.5, 0.21875, ((0, 32),))
    w_attn_out = scatter_about(key_list[5], (H * DH, D), (D // 64) ** -0.5, 1.75, ((0, 32),))
    attn_gain = jnp.clip(1.0 + 0.18 * jax.random.normal(key_list[6], (D,), jnp.float32), 0.099609375, 1.8984375).astype(jnp.bfloat16)
    rel_bias = scatter_about(key_list[7], (NB, H), 1.0, 4.0)
    w_gate = scatter_about(key_list[8], (D, FF), D ** -0.5, 0.21875, ((0, 32),))
    w_up = scatter_about(key_list[9], (D, FF), D ** -0.5, 0.21875, ((0, 32),))
    w_down = scatter_about(key_list[10], (FF, D), FF ** -0.5, 0.125, ((0, 32),))
    ffn_gain = jnp.clip(1.0 + 0.18 * jax.random.normal(key_list[11], (D,), jnp.float32), 0.099609375, 1.8984375).astype(jnp.bfloat16)
    cotangent = scatter_about(key_list[12], (ROWS, L, D), 1.0, 6.0, ((0, 8), (1, 4)))
    return dict(tokens=tokens, segment_ids=segment_ids, w_query=w_query, w_key=w_key, w_value=w_value, w_attn_out=w_attn_out, attn_gain=attn_gain, rel_bias=rel_bias, w_gate=w_gate, w_up=w_up, w_down=w_down, ffn_gain=ffn_gain, cotangent=cotangent)


@jax.custom_vjp
def low(v):
    return lax.optimization_barrier(v.astype(jnp.bfloat16)).astype(jnp.float32)

@jax.custom_vjp
def low_back(v):
    return v

def low_keep(v):
    return (low(v), None)

def low_pass(kept, grad):
    return (grad,)

def back_keep(v):
    return (v, None)

def back_low(kept, grad):
    return (low(grad),)
low.defvjp(low_keep, low_pass)
low_back.defvjp(back_keep, back_low)
THRESHOLDS = (12, 16, 23, 32, 46, 64, 91)
HIGHEST = lax.Precision.HIGHEST
EPSILON = 1e-06
MASKED = -1e+30

def bucket_of(relative):
    distance = jnp.abs(relative)
    far_bucket = 8 + sum([(distance >= threshold).astype(jnp.int32) for threshold in THRESHOLDS])
    near_bucket = jnp.where(distance < 8, distance, far_bucket)
    return jnp.where(relative > 0, NB // 2, 0) + near_bucket

def rms_norm(values, gain):
    return values * lax.rsqrt(lax.optimization_barrier(jnp.mean(values * values, axis=-1, keepdims=True)) + EPSILON) * gain

def row_layer(inputs, row_segs, query_weight, key_weight, value_weight, out_weight, gain_one, bias_table, gate_weight, up_weight, down_weight, gain_two):
    length = inputs.shape[0]
    normed_one = low(rms_norm(inputs, gain_one))
    queries = low(low_back(jnp.dot(normed_one, query_weight, precision=HIGHEST))).reshape(length, H, DH)
    key_rows = low(low_back(jnp.dot(normed_one, key_weight, precision=HIGHEST))).reshape(length, H, DH)
    values = low(low_back(jnp.dot(normed_one, value_weight, precision=HIGHEST))).reshape(length, H, DH)
    block_rows = math.gcd(length, 512)
    key_index = jnp.arange(length, dtype=jnp.int32)

    def attend(start):
        query_block = lax.dynamic_slice_in_dim(queries, start, block_rows, 0)
        query_index = start + jnp.arange(block_rows, dtype=jnp.int32)
        query_seg = lax.dynamic_slice_in_dim(row_segs, start, block_rows, 0)
        raw_scores = low_back(jnp.einsum('qhd,khd->hqk', query_block, key_rows, precision=HIGHEST))
        buckets = bucket_of(key_index[None, :] - query_index[:, None])
        rel_term = jnp.transpose(bias_table[buckets], (2, 0, 1))
        allowed = (query_seg[:, None] == row_segs[None, :])[None]
        scores = jnp.where(allowed, raw_scores + rel_term, MASKED)
        prob_low = low(jax.nn.softmax(scores, axis=-1))
        return jnp.einsum('hqk,khd->qhd', prob_low, values, precision=HIGHEST)
    starts = jnp.arange(length // block_rows, dtype=jnp.int32) * block_rows
    attended = lax.map(jax.checkpoint(attend), starts).reshape(length, H * DH)
    attended = low(low_back(attended))
    mixed_in = inputs + low_back(jnp.dot(attended, out_weight, precision=HIGHEST))
    normed_two = low(rms_norm(mixed_in, gain_two))
    gate_act = low_back(jnp.dot(normed_two, gate_weight, precision=HIGHEST))
    up_act = low_back(jnp.dot(normed_two, up_weight, precision=HIGHEST))
    hidden = low(jax.nn.gelu(gate_act, approximate=True) * up_act)
    return mixed_in + low_back(jnp.dot(hidden, down_weight, precision=HIGHEST))

def reference(tokens, segment_ids, w_query, w_key, w_value, w_attn_out, attn_gain, rel_bias, w_gate, w_up, w_down, ffn_gain, cotangent):
    floats = tuple((source.astype(jnp.float32) for source in (tokens, w_query, w_key, w_value, w_attn_out, attn_gain, rel_bias, w_gate, w_up, w_down, ffn_gain)))

    def forward(inputs, query_weight, key_weight, value_weight, out_weight, gain_one, bias_table, gate_weight, up_weight, down_weight, gain_two):

        def one_row(row_pair):
            return row_layer(row_pair[0], row_pair[1], query_weight, key_weight, value_weight, out_weight, gain_one, bias_table, gate_weight, up_weight, down_weight, gain_two)
        return lax.map(one_row, (inputs, segment_ids))
    layer_out, pullback = jax.vjp(forward, *floats)
    gradients = pullback(cotangent.astype(jnp.float32))
    return (layer_out.astype(jnp.bfloat16), gradients[0], gradients[1], gradients[2], gradients[3], gradients[4], gradients[5], gradients[6], gradients[7], gradients[8], gradients[9], gradients[10])
```

```python
import functools
import math

import jax
import jax.numpy as jnp
from jax import lax
from jax.experimental import pallas as pl
from jax.experimental.pallas import tpu as pltpu
from jax.sharding import PartitionSpec as P

D = 768
H = 12
DH = 64
NB = 32
THRESHOLDS = (12, 16, 23, 32, 46, 64, 91)
MASKED = -1e30
EPSILON = 1e-06
TP = 4
T = 256
HT = 3
F32 = jnp.float32
BF16 = jnp.bfloat16
MIB = 1 << 20


def dot(a, b):
    return lax.dot_general(a, b, (((1,), (0,)), ((), ())), preferred_element_type=F32)


def dot_nt(a, b):
    return lax.dot_general(a, b, (((1,), (1,)), ((), ())), preferred_element_type=F32)


def dot_tn(a, b):
    return lax.dot_general(a, b, (((0,), (0,)), ((), ())), preferred_element_type=F32)


def bucket_of(relative):
    distance = jnp.abs(relative)
    far = jnp.full(relative.shape, 8, jnp.int32)
    for threshold in THRESHOLDS:
        far = far + (distance >= threshold).astype(jnp.int32)
    return jnp.where(relative > 0, NB // 2, 0) + jnp.where(distance < 8, distance, far)


def call(kernel, out_shape, *args, scratch=(), smem=(), vmem=48, flops=0, nbytes=0, name=None):
    vspec = pl.BlockSpec(memory_space=pltpu.VMEM)
    sspec = pl.BlockSpec(memory_space=pltpu.SMEM)
    return pl.pallas_call(
        kernel,
        out_shape=out_shape,
        in_specs=[sspec if n in smem else vspec for n in range(len(args))],
        out_specs=jax.tree.map(lambda _: vspec, out_shape),
        scratch_shapes=list(scratch),
        compiler_params=pltpu.CompilerParams(vmem_limit_bytes=vmem * MIB),
        cost_estimate=pl.CostEstimate(flops=flops, bytes_accessed=nbytes, transcendentals=0),
        name=name,
    )(*args)


def sds(shape, dtype):
    return jax.ShapeDtypeStruct(shape, dtype)


def low_half(rows):
    return lax.broadcasted_iota(jnp.int32, (rows, 128), 1) < 64


def prep_kernel(wq, wk, wv, wg, wu, g1, g2, s0, s1, s2, s3, slabs):
    j_me = lax.axis_index("blk")
    rows = wq.shape[0]
    low = low_half(rows)
    lane = lax.broadcasted_iota(jnp.int32, (rows, 128), 1)
    gains = jnp.where(lane == 64, g1[...], jnp.where(lane == 65, g2[...], 0.0))

    def tile(ref, index):
        return ref[:, 128 * index : 128 * index + 128].astype(F32)

    for j in range(TP):
        first, second = [], []
        for ref in (wq, wk, wv):
            at = 192 * j // 128
            a, b = tile(ref, at), tile(ref, at + 1)
            if j % 2:
                a, b = pltpu.roll(a, 64, 1), pltpu.roll(b, 64, 1)
                a = jnp.where(low, a, b)
            first.append(a)
            second.append(b)
        tiles = first + [
            jnp.where(low, second[0], pltpu.roll(second[1], 64, 1)),
            jnp.where(low, second[2], gains),
        ]
        for ref in (wg, wu):
            for t in range(4):
                a = tile(ref, 4 * t + j // 2)
                b = tile(ref, 4 * t + 2 + j // 2)
                if j % 2:
                    tiles.append(jnp.where(low, pltpu.roll(a, 64, 1), b))
                else:
                    tiles.append(jnp.where(low, a, pltpu.roll(b, 64, 1)))
        for n, v in enumerate(tiles):
            slabs[j ^ j_me, :, 128 * n : 128 * n + 128] = v.astype(BF16)
    for k, ref in enumerate((s0, s1, s2, s3)):
        ref[...] = slabs[k]


def pack_kernel(s0, s1, s2, s3, wd, first, second, whole):
    j = lax.axis_index("blk")
    rows = s0.shape[0]
    for k, ref in enumerate((s0, s1, s2, s3)):
        whole[pl.ds(pl.multiple_of(rows * (j ^ k), 8), rows)] = ref[...].astype(F32)
    first[...] = whole[:, 0:640].astype(BF16)
    for n in range(4):
        second[96 * n : 96 * n + 96] = whole[:, 640 + 256 * n : 896 + 256 * n].astype(BF16)
    for n in range(3):
        second[384 + 64 * n : 448 + 64 * n] = wd[:, 256 * n : 256 * n + 256]


def bias_kernel(table, out):
    j = lax.axis_index("blk")
    lane = lax.broadcasted_iota(jnp.int32, (8, 512), 1)
    for n in range(3):
        off = (n - 1) * T
        rel = jnp.where(lane < 256, off - lane, off + 512 - lane)
        bucket = bucket_of(rel)
        for h in range(HT):
            row = jnp.zeros((8, 512), F32)
            for b in range(NB):
                row = jnp.where(bucket == b, table[b, HT * j + h], row)
            wide = jnp.broadcast_to(row[0:1], (T, 512))
            out[h, n] = pltpu.roll(wide, 0, 1, stride=1, stride_axis=0)[:, :T]


def piece_at(n):
    return 2 * (n % 4) + n // 4


def qkv_kernel(t0, t1, t2, t3, p0, p1, p2, p3, p4, p5, p6, p7, tok, n1, qkv, w, gains):
    j = lax.axis_index("blk")
    dp = lax.axis_index("dp")
    for k, ref in enumerate((t0, t1, t2, t3)):
        tok[j ^ k] = ref[...]
    for n, ref in enumerate((p0, p1, p2, p3, p4, p5, p6, p7)):
        w[pl.ds(pl.multiple_of(96 * (dp ^ piece_at(n)), 32), 96)] = ref[...]
    turned = jnp.transpose(w[:, 512:640].astype(F32))
    gains[...] = turned[64:72]

    def body(b, carry):
        x = tok[b].astype(F32)
        rstd = lax.rsqrt(jnp.mean(x * x, axis=-1, keepdims=True) + EPSILON)
        n = (x * rstd * gains[0:1]).astype(BF16)
        n1[b] = n
        y = dot(n, w[...])
        for t in range(5):
            qkv[t, b] = y[:, 128 * t : 128 * t + 128].astype(BF16)
        return carry

    lax.fori_loop(0, TP, body, 0)


def attn_fwd_kernel(
    table, bias, qkv, s0, s1, s2, s3, prob, inv_tot, out_t, att, segq, segk, qtm, vt, sc
):
    j_me = lax.axis_index("blk")
    for k, ref in enumerate((s0, s1, s2, s3)):
        row = ref[...].astype(F32)
        segq[j_me ^ k] = jnp.broadcast_to(row, (8, T))
        col = jnp.transpose(jnp.broadcast_to(row, (128, T)))
        segk[j_me ^ k, :, 0:128] = col
        segk[j_me ^ k, :, 128:256] = col
    rows_low = lax.broadcasted_iota(jnp.int32, (128, T), 0) < 64
    for i in range(TP):
        q0 = jnp.transpose(qkv[0, i].astype(F32))
        q1 = jnp.transpose(pltpu.roll(qkv[3, i].astype(F32), 64, 1))
        qtm[0, i] = jnp.where(rows_low, q0, 0.0).astype(BF16)
        qtm[1, i] = jnp.where(rows_low, 0.0, q0).astype(BF16)
        qtm[2, i] = jnp.where(rows_low, 0.0, q1).astype(BF16)
        v0 = jnp.transpose(qkv[2, i].astype(F32)).astype(BF16)
        v1 = jnp.transpose(qkv[4, i].astype(F32)).astype(BF16)
        vt[0, :, T * i : T * i + T] = v0[0:64]
        vt[1, :, T * i : T * i + T] = v0[64:128]
        vt[2, :, T * i : T * i + T] = v1[0:64]

    def head(h, carry):
        tile = 1 + 2 * (h // 2)
        far = (table[15, HT * j_me + h], table[31, HT * j_me + h])
        for i in range(TP):
            peak = jnp.full((1, T), MASKED, F32)
            for j in range(TP):
                s = dot(qkv[tile, j], qtm[h, i])
                if abs(j - i) <= 1:
                    s = s + bias[h, j - i + 1]
                else:
                    s = s + far[j > i]
                if i in (0, TP - 1) or j in (0, TP - 1):
                    s = jnp.where(segk[j] == segq[i, 0:1], s, MASKED)
                sc[j] = s
                peak = jnp.maximum(peak, jnp.max(s, axis=0, keepdims=True))
            total = jnp.zeros((1, T), F32)
            for j in range(TP):
                p = jnp.exp(sc[j] - peak)
                total = total + jnp.sum(p, axis=0, keepdims=True)
                prob[h, i, j] = p.astype(BF16)
            inv = 1.0 / total
            inv_tot[h, i] = inv
            o = dot(vt[h], prob[h, i].reshape(TP * T, T))
            out_t[h, :, T * i : T * i + T] = o * inv
        return carry

    lax.fori_loop(0, HT, head, 0)
    for b in range(TP):
        both = jnp.concatenate(
            [out_t[0, :, T * b : T * b + T], out_t[1, :, T * b : T * b + T]], axis=0
        )
        att[T * b : T * b + T, :] = jnp.transpose(both).astype(BF16)
    for b in range(2):
        both = jnp.concatenate(
            [out_t[2, :, T * b : T * b + T], out_t[2, :, T * (b + 2) : T * (b + 2) + T]], axis=0
        )
        att[1024 + T * b : 1024 + T * b + T, :] = jnp.transpose(both).astype(BF16)


def put_pair(keep, give, k, value):
    @pl.when(k % 2 == 0)
    def _():
        keep[k // 2] = value

    @pl.when(k % 2 == 1)
    def _():
        give[k // 2] = value


def ffn_kernel(
    a0, a1, a2, a3, wo, gains, p0, p1, p2, p3, p4, p5, p6, p7, tok, c0, c1, c2, c3,
    attc, wop, cot, n2, hid, ggug, two_keep, two_give, lo_keep, lo_give, mixed_own, wgu, wd,
):
    j = lax.axis_index("blk")
    dp = lax.axis_index("dp")
    for n, ref in enumerate((p0, p1, p2, p3, p4, p5, p6, p7)):
        at = dp ^ piece_at(n)
        for m in range(4):
            wgu[pl.ds(pl.multiple_of(96 * at, 32), 96), 256 * m : 256 * m + 256] = ref[96 * m : 96 * m + 96]
        for m in range(3):
            wd[pl.ds(pl.multiple_of(64 * at, 64), 64), 256 * m : 256 * m + 256] = ref[384 + 64 * m : 448 + 64 * m]
    for k, ref in enumerate((c0, c1, c2, c3)):
        cot[j ^ k] = ref[...]
        at = pl.multiple_of(192 * (j ^ k), 64)
        wop[128 * k : 128 * k + 128] = wo[pl.ds(at, 128)]
        wop[512 + 64 * k : 512 + 64 * k + 64] = wo[pl.ds(at + 128, 64)]
    low = low_half(T)

    def body(k, carry):
        b = j ^ k
        half = b // 2
        refs = (a0, a1, a2, a3)
        for n, ref in enumerate(refs):
            attc[b, :, 128 * n : 128 * n + 128] = ref[pl.ds(pl.multiple_of(b * T, T), T)]
        rest = [
            ref[pl.ds(pl.multiple_of(1024 + (b % 2) * T, T), T)].astype(F32) for ref in refs
        ]
        for n in range(2):
            lo = pltpu.roll(rest[2 * n], 64 * half, 1)
            hi = pltpu.roll(rest[2 * n + 1], 64 * (1 - half), 1)
            attc[b, :, 512 + 128 * n : 640 + 128 * n] = jnp.where(low, lo, hi).astype(BF16)
        mixed = tok[b].astype(F32) + dot(attc[b], wop[...])

        @pl.when(k == 0)
        def _():
            mixed_own[...] = mixed

        rstd = lax.rsqrt(jnp.mean(mixed * mixed, axis=-1, keepdims=True) + EPSILON)
        n = (mixed * rstd * gains[1:2]).astype(BF16)
        n2[b] = n
        gate = dot(n, wgu[:, 0:512])
        up = dot(n, wgu[:, 512:1024])
        c = 0.7978845608028654
        sq = gate * gate
        th = jnp.tanh(c * gate * (1.0 + 0.044715 * sq))
        act = 0.5 * gate * (1.0 + th)
        slope = 0.5 * (1.0 + th) + 0.5 * gate * (1.0 - th * th) * (c * (1.0 + 3 * 0.044715 * sq))
        hidden = (act * up).astype(BF16)
        hid[b] = hidden
        hg = dot_nt(cot[b], wd[...])
        ggug[b, :, 0:512] = (hg * up * slope).astype(BF16)
        ggug[b, :, 512:1024] = (hg * act).astype(BF16)
        two = dot_nt(ggug[b], wgu[...]).astype(BF16)
        put_pair(two_keep, two_give, k, two)
        put_pair(lo_keep, lo_give, k, dot(hidden, wd[...]).astype(BF16))
        return carry

    lax.fori_loop(0, TP, body, 0)


def mid_kernel(keep, rc, rx, mixed_own, cot_own, attc, wop, gains, mixed_grad, g0, g1, g2, g3, wo_keep, wo_give, dw):
    j = lax.axis_index("blk")
    u = (keep[0].astype(F32) + rc[0].astype(F32) + rx[...].astype(F32)) * gains[1:2]
    mixed = mixed_own[...]
    rstd = lax.rsqrt(jnp.mean(mixed * mixed, axis=-1, keepdims=True) + EPSILON)
    n = mixed * rstd
    mg = cot_own[...].astype(F32) + rstd * (u - n * jnp.mean(u * n, axis=-1, keepdims=True))
    mixed_grad[...] = mg
    ml = mg.astype(BF16)
    ag = dot_nt(ml, wop[...])
    low = low_half(128)
    for k, ref in enumerate((g0, g1, g2, g3)):
        ref[0:256] = ag[:, 128 * k : 128 * k + 128].astype(BF16)
        rest = ag[:, 512 + 128 * (k // 2) : 640 + 128 * (k // 2)]
        top, bottom = rest[0:128], rest[128:256]
        if k % 2 == 0:
            v = jnp.where(low, top, pltpu.roll(bottom, 64, 1))
        else:
            v = jnp.where(low, pltpu.roll(top, 64, 1), bottom)
        ref[256:384] = v.astype(BF16)
    perm = dot_tn(attc[j], ml)
    for k in range(TP):
        at = pl.multiple_of(192 * (j ^ k), 64)
        dw[pl.ds(at, 128)] = perm[128 * k : 128 * k + 128]
        dw[pl.ds(at + 128, 64)] = perm[512 + 64 * k : 512 + 64 * k + 64]
    for k in range(TP):
        ref = wo_give if k % 2 else wo_keep
        for d in range(8):
            at = pl.multiple_of(24 * (TP * d + (j ^ k)), 8)
            ref[k // 2, d] = dw[pl.ds(at, 24)].astype(BF16)


SLOTS = (0, 2, 1, 3)
WO_ROWS = 32
CHUNK = 5 * 96 + 6 * WO_ROWS
TAIL = 64


def slots(body):
    dp = lax.axis_index("dp")
    for give in range(2):
        for slot, z in enumerate(SLOTS):
            body(give, slot, dp ^ (2 * z + give))


def ffn_dw_kernel(n2, ggug, hid, cot, keep, give, dwgu, dwd):
    for m in range(2):
        at = slice(512 * m, 512 * m + 512)
        dwgu[:, at] = dot_tn(n2[...], ggug[:, at])
    for m in range(3):
        at = slice(256 * m, 256 * m + 256)
        dwd[:, at] = dot_tn(hid[...], cot[:, at])

    def put(g, slot, owner):
        ref = give if g else keep
        a = pl.ds(pl.multiple_of(96 * owner, 32), 96)
        for m in range(4):
            ref[slot, 96 * m : 96 * m + 96] = dwgu[a, 256 * m : 256 * m + 256].astype(BF16)
        a = pl.ds(pl.multiple_of(64 * owner, 64), 64)
        for m in range(3):
            ref[slot, 384 + 64 * m : 448 + 64 * m] = dwd[a, 256 * m : 256 * m + 256].astype(BF16)

    slots(put)


def split(x):
    high = x.astype(BF16)
    return high, (x - high.astype(F32)).astype(BF16)


def attn_dw_kernel(n1, dqkv, wo_keep, wo_got, wo_along, table_grad, keep, give, dw, wo):
    for t in range(5):
        at = slice(128 * t, 128 * t + 128)
        dw[:, at] = dot_tn(n1[...], dqkv[:, at])
    for d in range(8):
        wo[d] = wo_keep[0, d].astype(F32) + wo_got[0, d].astype(F32) + wo_along[d].astype(F32)

    def put(g, slot, owner):
        ref = give if g else keep
        base = CHUNK * slot
        a = pl.ds(pl.multiple_of(96 * owner, 32), 96)
        for t in range(5):
            ref[base + 96 * t : base + 96 * t + 96] = dw[a, 128 * t : 128 * t + 128].astype(BF16)
        base = base + 480
        pad = jnp.zeros((WO_ROWS - 24, 128), F32)
        for t in range(6):
            part = wo[owner, :, 128 * t : 128 * t + 128]
            full = jnp.concatenate([part, pad], axis=0)
            ref[base + WO_ROWS * t : base + WO_ROWS * t + WO_ROWS] = full.astype(BF16)

    slots(put)
    for ref in (keep, give):
        for n, part in enumerate(split(table_grad[...])):
            ref[4 * CHUNK + 32 * n : 4 * CHUNK + 32 * n + 32] = part


def tail_of(ref, base):
    return ref[base : base + 32].astype(F32) + ref[base + 32 : base + 64].astype(F32)


def stage_kernel(n, keep, got, next_keep, next_give):
    half = n // 2 * CHUNK
    for at, ref in ((0, next_keep), (half, next_give)):
        here = slice(at, at + half)
        ref[0:half] = (keep[here].astype(F32) + got[here].astype(F32)).astype(BF16)
        parts = split(tail_of(keep, n * CHUNK) + tail_of(got, n * CHUNK))
        for m, part in enumerate(parts):
            ref[half + 32 * m : half + 32 * m + 32] = part


def back_kernel(keep, got, dwo, b0, b1, b2, b3, total):
    j = lax.axis_index("blk")
    total[...] = keep[0:CHUNK].astype(F32) + got[0:CHUNK].astype(F32)
    parts = split(tail_of(keep, CHUNK) + tail_of(got, CHUNK))
    for t in range(6):
        at = 480 + WO_ROWS * t
        dwo[:, 128 * t : 128 * t + 128] = total[at : at + 24]
    pad = jnp.zeros((8, 128), F32)
    for k, ref in enumerate((b0, b1, b2, b3)):
        for t in range(5):
            part = total[pl.ds(pl.multiple_of(96 * t + 24 * (j ^ k), 8), 24)]
            ref[0:32, 128 * t : 128 * t + 128] = jnp.concatenate([part, pad], axis=0).astype(BF16)
        for m, part in enumerate(parts):
            ref[32:64, 128 * m : 128 * m + 128] = part
        ref[32:64, 256:640] = jnp.zeros((32, 384), BF16)


def ffn_back_kernel(keep, got, along, dwd, b0, b1, b2, b3, total):
    j = lax.axis_index("blk")
    total[...] = keep[0].astype(F32) + got[0].astype(F32) + along[...].astype(F32)
    for m in range(3):
        dwd[:, 256 * m : 256 * m + 256] = total[384 + 64 * m : 448 + 64 * m]
    for k, ref in enumerate((b0, b1, b2, b3)):
        for m in range(4):
            part = total[pl.ds(pl.multiple_of(96 * m + 24 * (j ^ k), 8), 24)]
            ref[:, 256 * m : 256 * m + 256] = part.astype(BF16)


def attn_bwd_kernel(
    qkv, prob, inv_tot, out_t, g0, g1, g2, g3, w,
    dqkv, one_keep, one_give, table_grad,
    dotm, dom, qm, ktm, delta, dst, dq_acc, dk_acc, dv_acc, near, far,
):
    j_me = lax.axis_index("blk")
    low = low_half(T)
    low_short = low_half(128)
    rows_low = lax.broadcasted_iota(jnp.int32, (128, T), 0) < 64

    for k, ref in enumerate((g0, g1, g2, g3)):
        b = j_me ^ k
        first = ref[0:256].astype(F32)
        rest = ref[256:384].astype(F32)
        second = jnp.concatenate([rest, pltpu.roll(rest, 64, 1)], axis=0)
        t0 = jnp.transpose(first)
        t1 = jnp.transpose(second)
        t0 = t0 * jnp.where(rows_low, inv_tot[0, b], inv_tot[1, b])
        t1 = jnp.where(rows_low, t1 * inv_tot[2, b], 0.0)
        t0, t1 = t0.astype(BF16), t1.astype(BF16)
        f0, f1 = t0.astype(F32), t1.astype(F32)
        dotm[0, b] = jnp.where(rows_low, f0, 0.0).astype(BF16)
        dotm[1, b] = jnp.where(rows_low, 0.0, f0).astype(BF16)
        dotm[2, b] = t1
        back = jnp.transpose(f0)
        dom[0, b] = jnp.where(low, back, 0.0).astype(BF16)
        dom[1, b] = jnp.where(low, 0.0, back).astype(BF16)
        dom[2, b] = jnp.transpose(f1).astype(BF16)

    for i in range(TP):
        at = slice(T * i, T * i + T)
        for h in range(HT):
            g = dotm[h, i].astype(F32)
            g = g[64:128] if h == 1 else g[0:64]
            delta[h, i] = jnp.sum(out_t[h, :, at] * g, axis=0, keepdims=True)
        q0 = qkv[0, i].astype(F32)
        turned = pltpu.roll(qkv[3, i].astype(F32), 64, 1)
        qm[0, i] = jnp.where(low, q0, 0.0).astype(BF16)
        qm[1, i] = jnp.where(low, 0.0, q0).astype(BF16)
        qm[2, i] = jnp.where(low, 0.0, turned).astype(BF16)
        k0 = jnp.transpose(qkv[1, i].astype(F32))
        k1 = jnp.transpose(turned)
        ktm[0, :, at] = jnp.where(rows_low, k0, 0.0).astype(BF16)
        ktm[1, :, at] = jnp.where(rows_low, 0.0, k0).astype(BF16)
        ktm[2, :, at] = jnp.where(rows_low, k1, 0.0).astype(BF16)

    dq_acc[...] = jnp.zeros(dq_acc.shape, F32)
    dk_acc[...] = jnp.zeros(dk_acc.shape, F32)
    dv_acc[...] = jnp.zeros(dv_acc.shape, F32)
    table_grad[...] = jnp.zeros(table_grad.shape, F32)
    key_at = lax.broadcasted_iota(jnp.int32, (128, 128), 0)
    query_at = lax.broadcasted_iota(jnp.int32, (128, 128), 1)
    upper = query_at >= key_at
    turn = (key_at + query_at == 127).astype(F32)

    def diagonals(m):
        m = lax.dot_general(
            turn, m, (((1,), (0,)), ((), ())), precision=HIGHEST, preferred_element_type=F32
        )
        return jnp.sum(pltpu.roll(m, 1, 1, stride=1, stride_axis=0), axis=0, keepdims=True)

    row_id = lax.broadcasted_iota(jnp.int32, (NB, 128), 0)
    lane_id = lax.broadcasted_iota(jnp.int32, (NB, 128), 1)
    hot_neg = bucket_of(-lane_id) == row_id
    hot_pos = bucket_of(128 - lane_id) == row_id

    def head(h, carry):
        second = h // 2
        near[...] = jnp.zeros(near.shape, F32)
        far[...] = jnp.zeros(far.shape, F32)
        for i in range(TP):
            at = slice(T * i, T * i + T)
            row_delta = delta[h, i]
            for j in range(TP):
                dp = dot(qkv[2 + 2 * second, j], dotm[h, i])
                ds = prob[h, i, j].astype(F32) * (dp - row_delta)
                dst[j] = ds.astype(BF16)
                for a in range(2):
                    for c in range(2):
                        gap = 2 * (j - i) + a - c
                        part = ds[128 * a : 128 * a + 128, 128 * c : 128 * c + 128]
                        if abs(gap) <= 1:
                            near[gap + 1] += part
                        else:
                            far[int(gap > 0)] += jnp.sum(part.reshape(16, 8, 128), axis=0)
            d_all = dst[...].reshape(TP * T, T)
            dq_acc[second, :, at] += dot(ktm[h], d_all)
            dk_acc[second] += dot(d_all, qm[h, i])
            dv_acc[second] += dot(prob[h, i].reshape(TP * T, T), dom[h, i])
        before, diagonal, after = near[0], near[1], near[2]
        neg = jnp.where(upper, diagonal, before)
        pos = jnp.where(upper, after, diagonal)
        neg, pos = diagonals(neg), diagonals(pos)
        far_neg = jnp.sum(far[0], axis=0, keepdims=True) + jnp.sum(
            jnp.where(upper, before, 0.0), axis=0, keepdims=True
        )
        far_pos = jnp.sum(far[1], axis=0, keepdims=True) + jnp.sum(
            jnp.where(upper, 0.0, after), axis=0, keepdims=True
        )
        spread = (
            jnp.where(hot_neg, neg, 0.0)
            + jnp.where(hot_pos, pos, 0.0)
            + jnp.where(row_id == 15, far_neg, 0.0)
            + jnp.where(row_id == 31, far_pos, 0.0)
        )
        sums = jnp.sum(spread, axis=1, keepdims=True)
        table_grad[...] += jnp.where(lane_id == HT * j_me + h, sums, 0.0)
        return carry

    lax.fori_loop(0, HT, head, 0)
    for i in range(TP):
        at = slice(T * i, T * i + T)
        dq0 = jnp.transpose(dq_acc[0, :, at])
        dq1 = jnp.transpose(dq_acc[1, :, at])
        dqkv[i, :, 0:128] = dq0.astype(BF16)
        dqkv[i, :, 128:256] = dk_acc[0, at].astype(BF16)
        dqkv[i, :, 256:384] = dv_acc[0, at].astype(BF16)
        dqkv[i, :, 384:512] = (dq1 + dk_acc[1, at]).astype(BF16)
        dqkv[i, :, 512:640] = dv_acc[1, at].astype(BF16)

    def body(k, carry):
        b = j_me ^ k
        put_pair(one_keep, one_give, k, dot_nt(dqkv[b], w[...]).astype(BF16))
        return carry

    lax.fori_loop(0, TP, body, 0)


def finish(parts, w, out, gain):
    total = jnp.zeros((w.shape[0], 128), F32)
    for n, part in enumerate(parts):
        at = slice(128 * n, 128 * n + 128)
        total = total + part * w[:, at].astype(F32)
        out[:, at] = part
    return jnp.sum(total, axis=1, keepdims=True) / gain


def attn_final_kernel(b0, b1, b2, b3, g1, wq, wk, wv, dq, dk, dv, gg1, table, src):
    j_me = lax.axis_index("blk")
    rows = wq.shape[0]
    low = low_half(rows)
    sums = jnp.zeros((NB, 128), F32)
    for k, ref in enumerate((b0, b1, b2, b3)):
        src[j_me ^ k] = ref[0:32].astype(F32)
        sums = sums + ref[32:64, 0:128].astype(F32) + ref[32:64, 128:256].astype(F32)
    table[...] = sums

    def one(j, n):
        return src[j, 0:rows, 128 * n : 128 * n + 128]

    gain_grad = jnp.zeros((rows, 128), F32)
    for n, (w, out) in enumerate(((wq, dq), (wk, dk), (wv, dv))):
        parts = []
        for j in range(0, TP, 2):
            rest = []
            for m in (j, j + 1):
                last = one(m, 4 if n == 2 else 3)
                rest.append(pltpu.roll(last, 64, 1) if n == 1 else last)
            mid = pltpu.roll(one(j + 1, n), 64, 1)
            parts += [
                one(j, n),
                jnp.where(low, rest[0], mid),
                jnp.where(low, mid, pltpu.roll(rest[1], 64, 1)),
            ]
        gain_grad = gain_grad + finish(parts, w, out, g1[...])
    gg1[...] = gain_grad


def ffn_final_kernel(b0, b1, b2, b3, g2, wg, wu, dg, du, gg2, src):
    j_me = lax.axis_index("blk")
    rows = wg.shape[0]
    low = low_half(rows)
    for k, ref in enumerate((b0, b1, b2, b3)):
        src[j_me ^ k] = ref[...].astype(F32)
    gain_grad = jnp.zeros((rows, 128), F32)
    for n, (w, out) in enumerate(((wg, dg), (wu, du))):
        parts = [None] * 16
        for t in range(4):
            at = slice(512 * n + 128 * t, 512 * n + 128 * t + 128)
            for half in range(2):
                a, b = src[2 * half, :, at], src[2 * half + 1, :, at]
                parts[4 * t + half] = jnp.where(low, a, pltpu.roll(b, 64, 1))
                parts[4 * t + 2 + half] = jnp.where(low, pltpu.roll(a, 64, 1), b)
        gain_grad = gain_grad + finish(parts, w, out, g2[...])
    gg2[...] = gain_grad


AXES = ("dp", "blk")


def group_local(
    n_dp, n_blk,
    tokens, segment_ids, w_query, w_key, w_value, w_attn_out, attn_gain, rel_bias,
    w_gate, w_up, w_down, ffn_gain, cotangent,
):
    n_dev = n_dp * n_blk

    def swap(x, mask):
        return lax.ppermute(x, AXES, [(d, d ^ mask) for d in range(n_dev)])

    def share(x):
        along = swap(x, 2)
        return (x, swap(x, 1), along, swap(along, 1))

    def reduce_pair(keep, give):
        got = swap(give, 1)
        return got, swap(keep[1] + got[1], 2)

    tok_own, cot_own = tokens[0], cotangent[0]
    rows = w_query.shape[0]
    table = rel_bias.astype(F32)
    gain1 = jnp.broadcast_to(attn_gain.astype(F32)[:, None], (rows, 128))
    gain2 = jnp.broadcast_to(ffn_gain.astype(F32)[:, None], (rows, 128))

    def spread(x):
        near, far = swap(x, 8), swap(x, 16)
        last = swap(far, 8)
        return (x, near, far, last) + tuple(swap(v, 4) for v in (x, near, far, last))

    slabs = call(
        prep_kernel, (sds((rows, 1664), BF16),) * TP,
        w_query, w_key, w_value, w_gate, w_up, gain1, gain2, name="prep",
        scratch=(pltpu.VMEM((TP, rows, 1664), BF16),),
    )
    slabs = (slabs[0], swap(slabs[1], 1), swap(slabs[2], 2), swap(slabs[3], 3))
    first, second = call(
        pack_kernel, (sds((96, 640), BF16), sds((576, 256), BF16)),
        *slabs, w_down, name="pack", scratch=(pltpu.VMEM((96, 1664), F32),),
    )
    toks = share(tok_own)
    firsts = spread(first)
    segs = share(segment_ids)
    seconds = spread(second)
    wo = lax.all_gather(w_attn_out, AXES, axis=0, tiled=True)
    cots = share(cot_own)

    bias = call(bias_kernel, sds((HT, 3, T, T), F32), table, smem=(0,), name="bias")
    tok, n1, qkv, w_qkv, gains = call(
        qkv_kernel,
        (
            sds((TP, T, D), BF16), sds((TP, T, D), BF16), sds((5, TP, T, 128), BF16),
            sds((D, 640), BF16), sds((8, D), F32),
        ),
        *toks, *firsts, name="qkv",
        flops=2 * 1024 * 768 * 640, nbytes=8 * MIB,
    )
    prob, inv_tot, out_t, att = call(
        attn_fwd_kernel,
        (
            sds((HT, TP, TP, T, T), BF16),
            sds((HT, TP, 1, T), F32),
            sds((HT, DH, TP * T), F32),
            sds((1536, 128), BF16),
        ),
        table, bias, qkv, *segs, smem=(0,), name="attn_fwd",
        scratch=(
            pltpu.VMEM((TP, 8, T), F32),
            pltpu.VMEM((TP, T, T), F32),
            pltpu.VMEM((HT, TP, 128, T), BF16),
            pltpu.VMEM((HT, DH, TP * T), BF16),
            pltpu.VMEM((TP, T, T), F32),
        ),
        flops=8 * 1024 * 1024 * 768, nbytes=8 * MIB,
    )
    atts = share(att)
    (
        attc, wop, cot, n2, hid, ggug, two_keep, two_give, lo_keep, lo_give, mixed_own,
    ) = call(
        ffn_kernel,
        (
            sds((TP, T, D), BF16), sds((D, D), BF16), sds((TP, T, D), BF16), sds((TP, T, D), BF16),
            sds((TP, T, 512), BF16), sds((TP, T, 1024), BF16),
            sds((2, T, D), BF16), sds((2, T, D), BF16), sds((2, T, D), BF16), sds((2, T, D), BF16),
            sds((T, D), F32),
        ),
        *atts, wo, gains, *seconds, tok, *cots, name="ffn",
        scratch=(pltpu.VMEM((D, 1024), BF16), pltpu.VMEM((512, D), BF16)),
        flops=2 * 1024 * 768 * (768 + 512 * 6), nbytes=16 * MIB,
    )
    two_c, two_x = reduce_pair(two_keep, two_give)
    mixed_grad, g0, g1, g2, g3, wo_keep, wo_give = call(
        mid_kernel,
        (sds((T, D), F32),) + (sds((384, 128), BF16),) * 4 + (sds((2, 8, 24, D), BF16),) * 2,
        two_keep, two_c, two_x, mixed_own, cot_own, attc, wop, gains, name="mid",
        scratch=(pltpu.VMEM((D, D), F32),),
        flops=4 * 256 * 768 * 768, nbytes=8 * MIB,
    )
    g1, g2, g3 = swap(g1, 1), swap(g2, 2), swap(g3, 3)
    wo_got, wo_along = reduce_pair(wo_keep, wo_give)
    flat = TP * T
    keep, give = call(
        ffn_dw_kernel, (sds((4, 576, 256), BF16),) * 2,
        n2.reshape(flat, D), ggug.reshape(flat, 1024), hid.reshape(flat, 512), cot.reshape(flat, D),
        name="ffn_dw", scratch=(pltpu.VMEM((D, 1024), F32), pltpu.VMEM((512, D), F32)),
        flops=2 * 1024 * 768 * 512 * 3, nbytes=12 * MIB,
    )
    got = swap(give, 4)
    f_give = keep[2:] + got[2:]
    f_keep = keep[:2] + got[:2]
    got = swap(f_give, 8)
    along = swap(f_keep[1] + got[1], 16)
    dwd, *backs = call(
        ffn_back_kernel, (sds((64, D), F32),) + (sds((rows, 1024), BF16),) * 4,
        f_keep, got, along, name="ffn_back", scratch=(pltpu.VMEM((576, 256), F32),),
    )
    backs = (backs[0], swap(backs[1], 1), swap(backs[2], 2), swap(backs[3], 3))
    ff = w_gate.shape[1]
    dg, du, gg2 = call(
        ffn_final_kernel, (sds((rows, ff), F32),) * 2 + (sds((rows, 128), F32),),
        *backs, gain2, w_gate, w_up, name="ffn_final",
        scratch=(pltpu.VMEM((TP, rows, 1024), F32),),
    )
    dqkv, one_keep, one_give, table_grad = call(
        attn_bwd_kernel,
        (
            sds((TP, T, 640), BF16),
            sds((2, T, D), BF16),
            sds((2, T, D), BF16),
            sds((NB, 128), F32),
        ),
        qkv, prob, inv_tot, out_t, g0, g1, g2, g3, w_qkv, name="attn_bwd",
        scratch=(
            pltpu.VMEM((HT, TP, 128, T), BF16),
            pltpu.VMEM((HT, TP, T, 128), BF16),
            pltpu.VMEM((HT, TP, T, 128), BF16),
            pltpu.VMEM((HT, 128, TP * T), BF16),
            pltpu.VMEM((HT, TP, 1, T), F32),
            pltpu.VMEM((TP, T, T), BF16),
            pltpu.VMEM((2, 128, TP * T), F32),
            pltpu.VMEM((2, TP * T, 128), F32),
            pltpu.VMEM((2, TP * T, 128), F32),
            pltpu.VMEM((3, 128, 128), F32),
            pltpu.VMEM((2, 8, 128), F32),
        ),
        flops=16 * 1024 * 1024 * 768, nbytes=12 * MIB,
    )
    one_c, one_x = reduce_pair(one_keep, one_give)
    lo_c, lo_x = reduce_pair(lo_keep, lo_give)
    layer_out = mixed_own + lo_keep[0].astype(F32) + lo_c[0].astype(F32) + lo_x.astype(F32)

    def chunks(n):
        return sds((n * CHUNK + TAIL, 128), BF16)

    keep, give = call(
        attn_dw_kernel, (chunks(4),) * 2,
        n1.reshape(flat, D), dqkv.reshape(flat, 640), wo_keep, wo_got, wo_along, table_grad,
        name="attn_dw", scratch=(pltpu.VMEM((D, 640), F32), pltpu.VMEM((8, 24, D), F32)),
        flops=2 * 1024 * 768 * 640, nbytes=6 * MIB,
    )
    got = swap(give, 4)
    keep, give = call(
        functools.partial(stage_kernel, 4), (chunks(2),) * 2, keep, got, name="stage_y"
    )
    got = swap(give, 8)
    keep, give = call(
        functools.partial(stage_kernel, 2), (chunks(1),) * 2, keep, got, name="stage_z"
    )
    got = swap(give, 16)
    dwo, *backs = call(
        back_kernel, (sds((rows, D), F32),) + (sds((64, 640), BF16),) * 4,
        keep, got, name="back", scratch=(pltpu.VMEM((CHUNK, 128), F32),),
    )
    backs = (backs[0], swap(backs[1], 1), swap(backs[2], 2), swap(backs[3], 3))
    dq, dk, dv, gg1, table_sum = call(
        attn_final_kernel,
        (sds((rows, D), F32),) * 3 + (sds((rows, 128), F32), sds((NB, 128), F32)),
        *backs, gain1, w_query, w_key, w_value, name="attn_final",
        scratch=(pltpu.VMEM((TP, 32, 640), F32),),
    )

    x = tok_own.astype(F32)
    rstd = lax.rsqrt(jnp.mean(x * x, axis=-1, keepdims=True) + EPSILON)
    n = x * rstd
    u = (one_keep[0].astype(F32) + one_c[0].astype(F32) + one_x.astype(F32)) * gains[0:1]
    tokens_grad = mixed_grad + rstd * (u - n * jnp.mean(u * n, axis=-1, keepdims=True))
    return (
        layer_out.astype(BF16)[None],
        tokens_grad[None],
        dq,
        dk,
        dv,
        dwo,
        gg1[:, 0],
        table_sum[:, :H],
        dg,
        du,
        dwd,
        gg2[:, 0],
    )


KEY_BLOCK = 256
HIGHEST = lax.Precision.HIGHEST


def rms_norm(values, gain):
    return values * lax.rsqrt(jnp.mean(values * values, axis=-1, keepdims=True) + EPSILON) * gain


def split_heads(flat_rows):
    return flat_rows.reshape(flat_rows.shape[0], flat_rows.shape[1], H, DH)


def join_heads(per_head):
    return per_head.reshape(per_head.shape[0], per_head.shape[1], H * DH)


def project(left, matrix):
    return jnp.einsum("rtd,de->rte", left, matrix, preferred_element_type=jnp.float32)


def project_back(left, matrix):
    return jnp.einsum("rte,de->rtd", left, matrix, preferred_element_type=jnp.float32)


def weight_grad(left, right):
    return jnp.einsum("rtd,rte->de", left, right, preferred_element_type=jnp.float32)


def block_scores(queries, key_block, query_pos, key_pos, query_seg, key_seg, bias_table):
    raw_scores = jnp.einsum(
        "rqhd,rkhd->rhqk", queries, key_block, preferred_element_type=jnp.float32
    )
    buckets = bucket_of(key_pos[None, :] - query_pos[:, None])
    one_hot = (buckets[:, :, None] == jnp.arange(NB, dtype=jnp.int32)[None, None, :]).astype(
        jnp.float32
    )
    rel_term = jnp.einsum("qkb,bh->hqk", one_hot, bias_table, precision=HIGHEST)
    allowed = (query_seg[:, :, None] == key_seg[:, None, :])[:, None]
    return (raw_scores + rel_term[None], allowed, one_hot)


def absorb(
    running, queries, key_block, value_block, query_pos, key_pos, query_seg, key_seg, bias_table
):
    row_peak, row_total, weighted = running
    scores, allowed, unused = block_scores(
        queries, key_block, query_pos, key_pos, query_seg, key_seg, bias_table
    )
    block_peak = jnp.max(jnp.where(allowed, scores, MASKED), axis=-1)
    new_peak = jnp.maximum(row_peak, block_peak)
    weights = jnp.where(allowed, jnp.exp(scores - new_peak[..., None]), 0.0)
    factor = jnp.exp(row_peak - new_peak)
    row_total = row_total * factor + jnp.sum(weights, axis=-1)
    weighted = weighted * factor[..., None] + jnp.einsum(
        "rhqk,rkhd->rhqd",
        weights.astype(jnp.bfloat16),
        value_block,
        preferred_element_type=jnp.float32,
    )
    return (new_peak, row_total, weighted)


def pair_grads(
    queries,
    out_grad,
    log_total,
    row_delta,
    key_block,
    value_block,
    query_pos,
    key_pos,
    query_seg,
    key_seg,
    bias_table,
):
    scores, allowed, one_hot = block_scores(
        queries, key_block, query_pos, key_pos, query_seg, key_seg, bias_table
    )
    prob_map = jnp.where(allowed, jnp.exp(scores - log_total[..., None]), 0.0)
    prob_grad = jnp.einsum(
        "rqhd,rkhd->rhqk", out_grad, value_block, preferred_element_type=jnp.float32
    )
    score_grad = prob_map * (prob_grad - row_delta[..., None])
    score_low = score_grad.astype(jnp.bfloat16)
    query_grad = jnp.einsum(
        "rhqk,rkhd->rqhd", score_low, key_block, preferred_element_type=jnp.float32
    )
    key_grad = jnp.einsum("rhqk,rqhd->rkhd", score_low, queries, preferred_element_type=jnp.float32)
    value_grad = jnp.einsum(
        "rhqk,rqhd->rkhd",
        prob_map.astype(jnp.bfloat16),
        out_grad,
        preferred_element_type=jnp.float32,
    )
    table_grad = jnp.einsum("rhqk,qkb->bh", score_grad, one_hot, precision=HIGHEST)
    return (query_grad, key_grad, value_grad, table_grad)


def in_blocks(step_fn, running, pieces):
    length = pieces[0].shape[1]
    block_size = math.gcd(length, KEY_BLOCK)
    block_count = length // block_size
    stacked = tuple(
        (
            jnp.moveaxis(
                member.reshape((member.shape[0], block_count, block_size) + member.shape[2:]), 1, 0
            )
            for member in pieces
        )
    )
    starts = block_size * jnp.arange(block_count, dtype=jnp.int32)

    def scan_step(inner_state, item_pair):
        return (step_fn(inner_state, item_pair[0], item_pair[1]), None)

    running, unused = lax.scan(scan_step, running, (stacked, starts))
    return running


def local(
    tokens,
    segment_ids,
    w_query,
    w_key,
    w_value,
    w_attn_out,
    attn_gain,
    rel_bias,
    w_gate,
    w_up,
    w_down,
    ffn_gain,
    cotangent,
):
    row_count, local_len, unused_dim = tokens.shape
    my_block = lax.axis_index("blk")
    full_query, full_key, full_value, full_out, gain_one = (
        lax.all_gather(w_query, ("dp", "blk"), axis=0, tiled=True),
        lax.all_gather(w_key, ("dp", "blk"), axis=0, tiled=True),
        lax.all_gather(w_value, ("dp", "blk"), axis=0, tiled=True),
        lax.all_gather(w_attn_out, ("dp", "blk"), axis=0, tiled=True),
        lax.all_gather(attn_gain, ("dp", "blk"), axis=0, tiled=True),
    )
    full_gate, full_up, full_down, gain_two = (
        lax.all_gather(w_gate, ("dp", "blk"), axis=0, tiled=True),
        lax.all_gather(w_up, ("dp", "blk"), axis=0, tiled=True),
        lax.all_gather(w_down, ("dp", "blk"), axis=0, tiled=True),
        lax.all_gather(ffn_gain, ("dp", "blk"), axis=0, tiled=True),
    )
    row_segs = lax.all_gather(segment_ids, "blk", axis=1, tiled=True)
    bias_table = rel_bias.astype(jnp.float32)
    gain_one_f = gain_one.astype(jnp.float32)
    gain_two_f = gain_two.astype(jnp.float32)
    inputs = tokens.astype(jnp.float32)
    query_pos = my_block * local_len + jnp.arange(local_len, dtype=jnp.int32)
    normed_one = rms_norm(inputs, gain_one_f).astype(jnp.bfloat16)
    query_flat = project(normed_one, full_query).astype(jnp.bfloat16)
    key_flat = project(normed_one, full_key).astype(jnp.bfloat16)
    value_flat = project(normed_one, full_value).astype(jnp.bfloat16)
    queries = split_heads(query_flat)
    key_heads = split_heads(key_flat)
    value_heads = split_heads(value_flat)

    def forward_piece(running, pieces):

        def step_fn(inner_state, blocks, block_start):
            block_len = blocks[0].shape[1]
            key_pos = block_start + jnp.arange(block_len, dtype=jnp.int32)
            key_seg = lax.dynamic_slice_in_dim(row_segs, block_start, block_len, 1)
            return absorb(
                inner_state,
                queries,
                split_heads(blocks[0]),
                split_heads(blocks[1]),
                query_pos,
                key_pos,
                segment_ids,
                key_seg,
                bias_table,
            )

        return in_blocks(step_fn, running, pieces)

    stat_shape = (row_count, H, local_len)
    start_state = (
        jnp.full(stat_shape, MASKED, jnp.float32),
        jnp.zeros(stat_shape, jnp.float32),
        jnp.zeros(stat_shape + (DH,), jnp.float32),
    )
    row_peak, row_total, weighted = forward_piece(
        start_state,
        (
            lax.all_gather(key_flat, "blk", axis=1, tiled=True),
            lax.all_gather(value_flat, "blk", axis=1, tiled=True),
        ),
    )
    log_total = row_peak + jnp.log(row_total)
    attended_f = jnp.transpose(weighted / row_total[..., None], (0, 2, 1, 3))
    attended = join_heads(attended_f).astype(jnp.bfloat16)
    mixed_in = inputs + project(attended, full_out)
    normed_two = rms_norm(mixed_in, gain_two_f).astype(jnp.bfloat16)
    gate_act = project(normed_two, full_gate)
    up_act = project(normed_two, full_up)

    def gated(gate_in, up_in):
        return jax.nn.gelu(gate_in, approximate=True) * up_in

    hidden_f, gated_back = jax.vjp(gated, gate_act, up_act)
    hidden = hidden_f.astype(jnp.bfloat16)
    layer_out = (mixed_in + project(hidden, full_down)).astype(jnp.bfloat16)
    down_grad = weight_grad(hidden, cotangent)
    hidden_grad = project_back(cotangent, full_down)
    gate_grad, up_grad = gated_back(hidden_grad)
    gate_low = gate_grad.astype(jnp.bfloat16)
    up_low = up_grad.astype(jnp.bfloat16)
    gate_w_grad = weight_grad(normed_two, gate_low)
    up_w_grad = weight_grad(normed_two, up_low)
    two_grad = project_back(gate_low, full_gate) + project_back(up_low, full_up)
    unused_two, norm_two_back = jax.vjp(rms_norm, mixed_in, gain_two_f)
    mixed_part, gain_two_grad = norm_two_back(two_grad)
    mixed_grad = cotangent.astype(jnp.float32) + mixed_part
    mixed_low = mixed_grad.astype(jnp.bfloat16)
    out_w_grad = weight_grad(attended, mixed_low)
    attended_grad = project_back(mixed_low, full_out).astype(jnp.bfloat16)
    grad_heads = split_heads(attended_grad)
    row_delta = jnp.sum(
        jnp.transpose(grad_heads.astype(jnp.float32), (0, 2, 1, 3))
        * (weighted / row_total[..., None]),
        axis=-1,
    )
    zero_heads = jnp.zeros(queries.shape, jnp.float32)
    zero_table = jnp.zeros((NB, H), jnp.float32)

    def query_piece(running, pieces):

        def step_fn(inner_state, blocks, block_start):
            block_len = blocks[0].shape[1]
            key_pos = block_start + jnp.arange(block_len, dtype=jnp.int32)
            key_seg = lax.dynamic_slice_in_dim(row_segs, block_start, block_len, 1)
            pair_parts = pair_grads(
                queries,
                grad_heads,
                log_total,
                row_delta,
                split_heads(blocks[0]),
                split_heads(blocks[1]),
                query_pos,
                key_pos,
                segment_ids,
                key_seg,
                bias_table,
            )
            return inner_state + pair_parts[0]

        return in_blocks(step_fn, running, pieces)

    query_grad = join_heads(
        query_piece(
            zero_heads,
            (
                lax.all_gather(key_flat, "blk", axis=1, tiled=True),
                lax.all_gather(value_flat, "blk", axis=1, tiled=True),
            ),
        )
    )
    log_rows, delta_rows = (
        lax.all_gather(log_total, "blk", axis=2, tiled=True),
        lax.all_gather(row_delta, "blk", axis=2, tiled=True),
    )

    def key_piece(running, pieces):

        def step_fn(inner_state, blocks, block_start):
            block_len = blocks[0].shape[1]
            piece_pos = block_start + jnp.arange(block_len, dtype=jnp.int32)
            piece_seg = lax.dynamic_slice_in_dim(row_segs, block_start, block_len, 1)
            piece_log = lax.dynamic_slice_in_dim(log_rows, block_start, block_len, 2)
            piece_delta = lax.dynamic_slice_in_dim(delta_rows, block_start, block_len, 2)
            pair_parts = pair_grads(
                split_heads(blocks[0]),
                split_heads(blocks[1]),
                piece_log,
                piece_delta,
                key_heads,
                value_heads,
                piece_pos,
                query_pos,
                piece_seg,
                segment_ids,
                bias_table,
            )
            return (
                inner_state[0] + pair_parts[1],
                inner_state[1] + pair_parts[2],
                inner_state[2] + pair_parts[3],
            )

        return in_blocks(step_fn, running, pieces)

    key_grad, value_grad, table_grad = key_piece(
        (zero_heads, zero_heads, zero_table),
        (
            lax.all_gather(query_flat, "blk", axis=1, tiled=True),
            lax.all_gather(attended_grad, "blk", axis=1, tiled=True),
        ),
    )
    query_low = query_grad.astype(jnp.bfloat16)
    key_low = join_heads(key_grad).astype(jnp.bfloat16)
    value_low = join_heads(value_grad).astype(jnp.bfloat16)
    query_w_grad = weight_grad(normed_one, query_low)
    key_w_grad = weight_grad(normed_one, key_low)
    value_w_grad = weight_grad(normed_one, value_low)
    one_grad = (
        project_back(query_low, full_query)
        + project_back(key_low, full_key)
        + project_back(value_low, full_value)
    )
    unused_one, norm_one_back = jax.vjp(rms_norm, inputs, gain_one_f)
    input_part, gain_one_grad = norm_one_back(one_grad)
    tokens_grad = mixed_grad + input_part
    table_sum = lax.psum(table_grad, ("dp", "blk"))
    all_sums = (
        lax.psum_scatter(query_w_grad, ("dp", "blk"), scatter_dimension=0, tiled=True),
        lax.psum_scatter(key_w_grad, ("dp", "blk"), scatter_dimension=0, tiled=True),
        lax.psum_scatter(value_w_grad, ("dp", "blk"), scatter_dimension=0, tiled=True),
        lax.psum_scatter(out_w_grad, ("dp", "blk"), scatter_dimension=0, tiled=True),
        lax.psum_scatter(gain_one_grad, ("dp", "blk"), scatter_dimension=0, tiled=True),
        lax.psum_scatter(gate_w_grad, ("dp", "blk"), scatter_dimension=0, tiled=True),
        lax.psum_scatter(up_w_grad, ("dp", "blk"), scatter_dimension=0, tiled=True),
        lax.psum_scatter(down_grad, ("dp", "blk"), scatter_dimension=0, tiled=True),
        lax.psum_scatter(gain_two_grad, ("dp", "blk"), scatter_dimension=0, tiled=True),
    )
    return (
        layer_out,
        tokens_grad,
        all_sums[0],
        all_sums[1],
        all_sums[2],
        all_sums[3],
        all_sums[4],
        table_sum,
        all_sums[5],
        all_sums[6],
        all_sums[7],
        all_sums[8],
    )


def solution(mesh):
    whole = P(AXES, None)
    rows = P("dp", "blk", None)
    n_dp, n_blk = mesh.shape["dp"], mesh.shape["blk"]
    grouped = functools.partial(group_local, n_dp, n_blk)
    body = grouped if (n_dp, n_blk) == (8, TP) else local
    return jax.shard_map(
        body,
        mesh=mesh,
        in_specs=(
            rows, P("dp", "blk"), whole, whole, whole, whole, P(AXES), P(),
            whole, whole, whole, P(AXES), rows,
        ),
        out_specs=(
            rows, rows, whole, whole, whole, whole, P(AXES), P(), whole, whole, whole, P(AXES),
        ),
        check_vma=False,
    )
```

```python
import functools
import math

import jax
import jax.numpy as jnp
from jax import lax
from jax.experimental import pallas as pl
from jax.experimental.pallas import tpu as pltpu
from jax.sharding import PartitionSpec as P

D = 768
H = 12
DH = 64
NB = 32
THRESHOLDS = (12, 16, 23, 32, 46, 64, 91)
MASKED = -1e30
EPSILON = 1e-06
TP = 4
T = 256
HT = 3
F32 = jnp.float32
BF16 = jnp.bfloat16
MIB = 1 << 20


def dot(a, b):
    return lax.dot_general(a, b, (((1,), (0,)), ((), ())), preferred_element_type=F32)


def dot_nt(a, b):
    return lax.dot_general(a, b, (((1,), (1,)), ((), ())), preferred_element_type=F32)


def dot_tn(a, b):
    return lax.dot_general(a, b, (((0,), (0,)), ((), ())), preferred_element_type=F32)


def bucket_of(relative):
    distance = jnp.abs(relative)
    far = jnp.full(relative.shape, 8, jnp.int32)
    for threshold in THRESHOLDS:
        far = far + (distance >= threshold).astype(jnp.int32)
    return jnp.where(relative > 0, NB // 2, 0) + jnp.where(distance < 8, distance, far)


def call(
    kernel, out_shape, *args, scratch=(), smem=(), held=(), after=(), vmem=8, cost=0, name=None
):
    vspec = pl.BlockSpec(memory_space=pltpu.VMEM)
    sspec = pl.BlockSpec(memory_space=pltpu.SMEM)
    aspec = pl.BlockSpec(memory_space=pl.ANY)
    hspec = pl.BlockSpec(memory_space=pltpu.HBM)
    skip = len(after)

    def body(*refs):
        kernel(*refs[skip:])

    specs = [sspec if n in smem else hspec if n in held else vspec for n in range(len(args))]
    return pl.pallas_call(
        body,
        out_shape=out_shape,
        in_specs=[aspec] * skip + specs,
        out_specs=jax.tree.map(lambda _: vspec, out_shape),
        scratch_shapes=list(scratch),
        compiler_params=pltpu.CompilerParams(vmem_limit_bytes=vmem * MIB),
        cost_estimate=pl.CostEstimate(flops=cost * 1_150_000_000, bytes_accessed=0, transcendentals=0),
        name=name,
    )(*after, *args)


def sds(shape, dtype):
    return jax.ShapeDtypeStruct(shape, dtype)


def low_half(rows):
    return lax.broadcasted_iota(jnp.int32, (rows, 128), 1) < 64


def prep_kernel(
    wq, wk, wv, wg, wu, g1, g2, s0, s1, s2, s3, gains, slabs, vq, vk, vv, vg, vu, sems
):
    j_me = lax.axis_index("blk")
    rows = wq.shape[0]
    pairs = ((wq, vq), (wk, vk), (wv, vv), (wg, vg), (wu, vu))
    copies = [pltpu.make_async_copy(a, b, sems.at[n]) for n, (a, b) in enumerate(pairs)]
    for copy in copies:
        copy.start()
    eye = lax.broadcasted_iota(jnp.int32, (rows, rows), 0) == lax.broadcasted_iota(
        jnp.int32, (rows, rows), 1
    )
    columns = []
    for n, ref in enumerate((g1, g2)):
        row = jnp.broadcast_to(ref[...].astype(F32).reshape(1, rows), (rows, rows))
        column = jnp.sum(jnp.where(eye, row, 0.0), axis=1, keepdims=True)
        columns.append(column)
        gains[n] = jnp.broadcast_to(column, (rows, 128))
    low = low_half(rows)
    lane = lax.broadcasted_iota(jnp.int32, (rows, 128), 1)
    spare = jnp.where(lane == 64, columns[0], jnp.where(lane == 65, columns[1], 0.0))
    for copy in copies:
        copy.wait()

    def tile(ref, index):
        return ref[:, 128 * index : 128 * index + 128].astype(F32)

    for j in range(TP):
        first, second = [], []
        for ref in (vq, vk, vv):
            at = 192 * j // 128
            a, b = tile(ref, at), tile(ref, at + 1)
            if j % 2:
                a, b = pltpu.roll(a, 64, 1), pltpu.roll(b, 64, 1)
                a = jnp.where(low, a, b)
            first.append(a)
            second.append(b)
        tiles = first + [
            jnp.where(low, second[0], pltpu.roll(second[1], 64, 1)),
            jnp.where(low, second[2], spare),
        ]
        for ref in (vg, vu):
            for t in range(4):
                a = tile(ref, 4 * t + j // 2)
                b = tile(ref, 4 * t + 2 + j // 2)
                if j % 2:
                    tiles.append(jnp.where(low, pltpu.roll(a, 64, 1), b))
                else:
                    tiles.append(jnp.where(low, a, pltpu.roll(b, 64, 1)))
        for n, v in enumerate(tiles):
            slabs[j ^ j_me, :, 128 * n : 128 * n + 128] = v.astype(BF16)
    for k, ref in enumerate((s0, s1, s2, s3)):
        ref[...] = slabs[k]


def pack_kernel(s0, s1, s2, s3, wo, first, whole, vo, sem):
    j = lax.axis_index("blk")
    rows = s0.shape[0]
    copy = pltpu.make_async_copy(wo, vo, sem)
    copy.start()
    for k, ref in enumerate((s0, s1, s2, s3)):
        whole[pl.ds(pl.multiple_of(rows * (j ^ k), 8), rows)] = ref[:, 0:640].astype(F32)
    first[0:96] = whole[...].astype(BF16)
    copy.wait()
    out = vo[...].astype(F32)
    rest = [out[8 * n : 8 * n + 8, 640:768] for n in range(3)]
    rest = jnp.concatenate(rest + [jnp.zeros((8, 256), F32)], axis=1)
    first[96:128] = jnp.concatenate([out[:, 0:640], rest], axis=0).astype(BF16)


def pack_more_kernel(s0, s1, s2, s3, wd, cot, seg, second, extra, whole, vd, sems):
    j = lax.axis_index("blk")
    rows = s0.shape[0]
    pairs = ((wd, vd), (cot, extra.at[0:T]))
    copies = [pltpu.make_async_copy(a, b, sems.at[n]) for n, (a, b) in enumerate(pairs)]
    for copy in copies:
        copy.start()
    for k, ref in enumerate((s0, s1, s2, s3)):
        whole[pl.ds(pl.multiple_of(rows * (j ^ k), 8), rows)] = ref[:, 640:1664].astype(F32)
    for n in range(4):
        second[96 * n : 96 * n + 96] = whole[:, 256 * n : 256 * n + 256].astype(BF16)
    ids = jnp.broadcast_to(seg[...], (16, T))
    extra[T : T + 16, 0:T] = (ids // 2).astype(F32).astype(BF16)
    extra[T : T + 16, T : 2 * T] = (ids % 2).astype(F32).astype(BF16)
    extra[T : T + 16, 2 * T : 3 * T] = jnp.zeros((16, T), BF16)
    for copy in copies:
        copy.wait()
    for n in range(3):
        second[384 + 64 * n : 448 + 64 * n] = vd[:, 256 * n : 256 * n + 256]


def stripes_kernel(p0, p1, p2, p3, p4, p5, p6, p7, out, whole):
    dp = lax.axis_index("dp")
    for n, ref in enumerate((p0, p1, p2, p3, p4, p5, p6, p7)):
        at = pl.ds(pl.multiple_of(24 * (dp ^ piece_at(n)), 8), 24)
        part = ref[96:128].astype(F32)
        whole[at, 0:640] = part[0:24]
        rest = [part[24:32, 128 * m : 128 * m + 128] for m in range(3)]
        whole[at, 640:768] = jnp.concatenate(rest, axis=0)
    out[...] = whole[...].astype(BF16)


def out_weight_kernel(p0, p1, p2, p3, out, whole):
    j = lax.axis_index("blk")
    for k, ref in enumerate((p0, p1, p2, p3)):
        rows = ref[...].astype(F32)
        for d in range(8):
            at = pl.multiple_of(24 * (TP * d + (j ^ k)), 8)
            whole[pl.ds(at, 24)] = rows[24 * d : 24 * d + 24]
    for k in range(TP):
        at = pl.multiple_of(192 * (j ^ k), 64)
        out[128 * k : 128 * k + 128] = whole[pl.ds(at, 128)].astype(BF16)
        out[512 + 64 * k : 576 + 64 * k] = whole[pl.ds(at + 128, 64)].astype(BF16)


def bias_kernel(table, out):
    j = lax.axis_index("blk")
    lane = lax.broadcasted_iota(jnp.int32, (8, 512), 1)
    for n in range(3):
        off = (n - 1) * T
        rel = jnp.where(lane < 256, off - lane, off + 512 - lane)
        bucket = bucket_of(rel)
        for h in range(HT):
            row = jnp.zeros((8, 512), F32)
            for b in range(NB):
                row = jnp.where(bucket == b, table[b, HT * j + h], row)
            wide = jnp.broadcast_to(row[0:1], (T, 512))
            out[h, n] = pltpu.roll(wide, 0, 1, stride=1, stride_axis=0)[:, :T]


def piece_at(n):
    return 2 * (n % 4) + n // 4


def qkv_kernel(
    t0, t1, t2, t3, p0, p1, p2, p3, p4, p5, p6, p7, tok, n1, qkv, w, gains
):
    j = lax.axis_index("blk")
    dp = lax.axis_index("dp")
    for k, ref in enumerate((t0, t1, t2, t3)):
        tok[j ^ k] = ref[...]
    for n, ref in enumerate((p0, p1, p2, p3, p4, p5, p6, p7)):
        w[pl.ds(pl.multiple_of(96 * (dp ^ piece_at(n)), 32), 96)] = ref[0:96]
    turned = jnp.transpose(w[:, 512:640].astype(F32))
    gains[...] = turned[64:72]

    def body(b, carry):
        x = tok[b].astype(F32)
        rstd = lax.rsqrt(jnp.mean(x * x, axis=-1, keepdims=True) + EPSILON)
        n = (x * rstd * gains[0:1]).astype(BF16)
        n1[b] = n
        y = dot(n, w[...])
        for t in range(5):
            qkv[t, b] = y[:, 128 * t : 128 * t + 128].astype(BF16)
        return carry

    lax.fori_loop(0, TP, body, 0)


def row_kernel(e0, e1, e2, e3, cot, segq, segk):
    j_me = lax.axis_index("blk")
    for k, ref in enumerate((e0, e1, e2, e3)):
        cot[j_me ^ k] = ref[0:T]
        parts = ref[T : T + 16].astype(F32)
        row = (2.0 * parts[:, 0:T] + parts[:, T : 2 * T])[0:8]
        segq[j_me ^ k] = row
        col = jnp.transpose(jnp.broadcast_to(row[0:1], (128, T)))
        segk[j_me ^ k, :, 0:128] = col
        segk[j_me ^ k, :, 128:256] = col


def attn_fwd_kernel(h, table, bias, qkv, segq, segk, prob, inv_tot, out_t, qt, vt, sc):
    j_me = lax.axis_index("blk")
    rows_low = lax.broadcasted_iota(jnp.int32, (128, T), 0) < 64
    half = slice(64, 128) if h == 1 else slice(0, 64)
    for i in range(TP):
        if h < 2:
            q = jnp.transpose(qkv[0, i].astype(F32))
        else:
            q = jnp.transpose(pltpu.roll(qkv[3, i].astype(F32), 64, 1))
        qt[i] = jnp.where(rows_low == (h == 0), q, 0.0).astype(BF16)
        v = jnp.transpose(qkv[2 + 2 * (h // 2), i].astype(F32)).astype(BF16)
        vt[:, T * i : T * i + T] = v[half]

    tile = 1 + 2 * (h // 2)
    far = (table[15, HT * j_me + h], table[31, HT * j_me + h])
    for i in range(TP):
        peak = jnp.full((1, T), MASKED, F32)
        for j in range(TP):
            s = dot(qkv[tile, j], qt[i])
            if abs(j - i) <= 1:
                s = s + bias[h, j - i + 1]
            else:
                s = s + far[j > i]
            if i in (0, TP - 1) or j in (0, TP - 1):
                s = jnp.where(segk[j] == segq[i, 0:1], s, MASKED)
            sc[j] = s
            peak = jnp.maximum(peak, jnp.max(s, axis=0, keepdims=True))
        total = jnp.zeros((1, T), F32)
        for j in range(TP):
            p = jnp.exp(sc[j] - peak)
            total = total + jnp.sum(p, axis=0, keepdims=True)
            prob[i, j] = p.astype(BF16)
        inv = 1.0 / total
        inv_tot[i] = inv
        out_t[:, T * i : T * i + T] = dot(vt[...], prob[i].reshape(TP * T, T)) * inv


def join_kernel(o0, o1, o2, att):
    for b in range(TP):
        at = slice(T * b, T * b + T)
        both = jnp.concatenate([o0[:, at], o1[:, at]], axis=0)
        att[at, :] = jnp.transpose(both).astype(BF16)
    for b in range(2):
        both = [o2[:, T * c : T * c + T] for c in (b, b + 2)]
        att[1024 + T * b : 1280 + T * b, :] = jnp.transpose(jnp.concatenate(both, axis=0)).astype(BF16)


def put_pair(keep, give, k, value):
    @pl.when(k % 2 == 0)
    def _():
        keep[k // 2] = value

    @pl.when(k % 2 == 1)
    def _():
        give[k // 2] = value


def units_kernel(p0, p1, p2, p3, p4, p5, p6, p7, wgu, wd):
    dp = lax.axis_index("dp")
    for n, ref in enumerate((p0, p1, p2, p3, p4, p5, p6, p7)):
        at = dp ^ piece_at(n)
        rows = pl.ds(pl.multiple_of(96 * at, 32), 96)
        for m in range(4):
            wgu[rows, 256 * m : 256 * m + 256] = ref[96 * m : 96 * m + 96]
        rows = pl.ds(pl.multiple_of(64 * at, 64), 64)
        for m in range(3):
            wd[rows, 256 * m : 256 * m + 256] = ref[384 + 64 * m : 448 + 64 * m]


def ffn_kernel(
    a0, a1, a2, a3, gains, wop, wgu, wd, tok, cot,
    attc, n2, hid, ggug, two_keep, two_give, lo_keep, lo_give, mixed_own,
):
    j = lax.axis_index("blk")
    low = low_half(T)

    def body(k, carry):
        b = j ^ k
        half = b // 2
        refs = (a0, a1, a2, a3)
        for n, ref in enumerate(refs):
            attc[b, :, 128 * n : 128 * n + 128] = ref[pl.ds(pl.multiple_of(b * T, T), T)]
        rest = [
            ref[pl.ds(pl.multiple_of(1024 + (b % 2) * T, T), T)].astype(F32) for ref in refs
        ]
        for n in range(2):
            lo = pltpu.roll(rest[2 * n], 64 * half, 1)
            hi = pltpu.roll(rest[2 * n + 1], 64 * (1 - half), 1)
            attc[b, :, 512 + 128 * n : 640 + 128 * n] = jnp.where(low, lo, hi).astype(BF16)
        mixed = tok[b].astype(F32) + dot(attc[b], wop[...])

        @pl.when(k == 0)
        def _():
            mixed_own[...] = mixed

        rstd = lax.rsqrt(jnp.mean(mixed * mixed, axis=-1, keepdims=True) + EPSILON)
        n = (mixed * rstd * gains[1:2]).astype(BF16)
        n2[b] = n
        gate = dot(n, wgu[:, 0:512])
        up = dot(n, wgu[:, 512:1024])
        c = 0.7978845608028654
        sq = gate * gate
        th = jnp.tanh(c * gate * (1.0 + 0.044715 * sq))
        act = 0.5 * gate * (1.0 + th)
        slope = 0.5 * (1.0 + th) + 0.5 * gate * (1.0 - th * th) * (c * (1.0 + 3 * 0.044715 * sq))
        hidden = (act * up).astype(BF16)
        hid[b] = hidden
        hg = dot_nt(cot[b], wd[...])
        ggug[b, :, 0:512] = (hg * up * slope).astype(BF16)
        ggug[b, :, 512:1024] = (hg * act).astype(BF16)
        two = dot_nt(ggug[b], wgu[...]).astype(BF16)
        put_pair(two_keep, two_give, k, two)
        put_pair(lo_keep, lo_give, k, dot(hidden, wd[...]).astype(BF16))
        return carry

    lax.fori_loop(0, TP, body, 0)


def mid_kernel(keep, rc, rx, mixed_own, cot, attc, wop, gains, mixed_grad, g0, g1, g2, g3, wo_keep, wo_one, wo_three, dw):
    j = lax.axis_index("blk")
    u = (keep[0].astype(F32) + rc[0].astype(F32) + rx[...].astype(F32)) * gains[1:2]
    mixed = mixed_own[...]
    rstd = lax.rsqrt(jnp.mean(mixed * mixed, axis=-1, keepdims=True) + EPSILON)
    n = mixed * rstd
    mg = cot[j].astype(F32) + rstd * (u - n * jnp.mean(u * n, axis=-1, keepdims=True))
    mixed_grad[...] = mg
    ml = mg.astype(BF16)
    ag = dot_nt(ml, wop[...])
    low = low_half(128)
    for k, ref in enumerate((g0, g1, g2, g3)):
        ref[0:256] = ag[:, 128 * k : 128 * k + 128].astype(BF16)
        rest = ag[:, 512 + 128 * (k // 2) : 640 + 128 * (k // 2)]
        top, bottom = rest[0:128], rest[128:256]
        if k % 2 == 0:
            v = jnp.where(low, top, pltpu.roll(bottom, 64, 1))
        else:
            v = jnp.where(low, pltpu.roll(top, 64, 1), bottom)
        ref[256:384] = v.astype(BF16)
    perm = dot_tn(attc[j], ml)
    for k in range(TP):
        at = pl.multiple_of(192 * (j ^ k), 64)
        dw[pl.ds(at, 128)] = perm[128 * k : 128 * k + 128]
        dw[pl.ds(at + 128, 64)] = perm[512 + 64 * k : 512 + 64 * k + 64]
    for k in range(TP):
        ref = (wo_keep.at[0], wo_one, wo_keep.at[1], wo_three)[k]
        for d in range(8):
            at = pl.multiple_of(24 * (TP * d + (j ^ k)), 8)
            ref[d] = dw[pl.ds(at, 24)].astype(BF16)


SLOTS = (0, 2, 1, 3)
CHUNK = 5 * 96 + 6 * 24
TAIL = 16


def slots(body):
    dp = lax.axis_index("dp")
    for give in range(2):
        for slot, z in enumerate(SLOTS):
            body(give, slot, dp ^ (2 * z + give))


def ffn_dw_kernel(n2, ggug, hid, cot, y_keep, y_give, z_keep, z_give, dwgu, dwd):
    for m in range(2):
        at = slice(512 * m, 512 * m + 512)
        dwgu[:, at] = dot_tn(n2[...], ggug[:, at])
    for m in range(3):
        at = slice(256 * m, 256 * m + 256)
        dwd[:, at] = dot_tn(hid[...], cot[:, at])

    def put(g, slot, owner):
        ref = y_give if g else y_keep
        a = pl.ds(pl.multiple_of(96 * owner, 32), 96)
        for m in range(3):
            ref[slot, 96 * m : 96 * m + 96] = dwgu[a, 256 * m : 256 * m + 256].astype(BF16)
        ref = z_give if slot > 1 else z_keep
        slot = 2 * (slot % 2) + g
        ref[slot, 0:96] = dwgu[a, 768:1024].astype(BF16)
        a = pl.ds(pl.multiple_of(64 * owner, 64), 64)
        for m in range(3):
            ref[slot, 96 + 64 * m : 160 + 64 * m] = dwd[a, 256 * m : 256 * m + 256].astype(BF16)

    slots(put)


def ffn_second_kernel(y_keep, y_got, z_keep, z_got, y_next, y_give, z_next, z_give):
    for keep, got, rest, give in ((y_keep, y_got, y_next, y_give), (z_keep, z_got, z_next, z_give)):
        rest[...] = (keep[0:2].astype(F32) + got[0:2].astype(F32)).astype(BF16)
        give[...] = (keep[2:4].astype(F32) + got[2:4].astype(F32)).astype(BF16)


def ffn_third_kernel(y_keep, y_got, z_keep, z_got, y_give, z_give):
    y_give[...] = (y_keep[1].astype(F32) + y_got[1].astype(F32)).astype(BF16)
    z_give[...] = (z_keep[1].astype(F32) + z_got[1].astype(F32)).astype(BF16)


def split(x):
    high = x.astype(BF16).astype(F32)
    return jnp.concatenate([high, x - high], axis=0).astype(BF16)


def attn_dw_kernel(n1, dqkv, wo_keep, wo_got, wo_along, table_grad, keep, give, dw, wo, chunk):
    for t in range(5):
        at = slice(128 * t, 128 * t + 128)
        dw[:, at] = dot_tn(n1[...], dqkv[:, at])
    for d in range(8):
        wo[d] = wo_keep[0, d].astype(F32) + wo_got[d].astype(F32) + wo_along[d].astype(F32)

    def put(g, slot, owner):
        ref = give if g else keep
        a = pl.ds(pl.multiple_of(96 * owner, 32), 96)
        for t in range(5):
            chunk[96 * t : 96 * t + 96] = dw[a, 128 * t : 128 * t + 128]
        for t in range(6):
            chunk[480 + 24 * t : 504 + 24 * t] = wo[owner, :, 128 * t : 128 * t + 128]
        ref[CHUNK * slot : CHUNK * slot + CHUNK] = chunk[...].astype(BF16)

    slots(put)
    for ref in (keep, give):
        ref[4 * CHUNK : 4 * CHUNK + 16] = split(table_grad[...])


def tail_of(ref, base):
    both = ref[base : base + 16].astype(F32)
    return both[0:8] + both[8:16]


def stage_kernel(n, keep, got, next_keep, next_give):
    half = n // 2 * CHUNK
    for at, ref in ((0, next_keep), (half, next_give)):
        here = slice(at, at + half)
        ref[0:half] = (keep[here].astype(F32) + got[here].astype(F32)).astype(BF16)
        ref[half : half + 16] = split(tail_of(keep, n * CHUNK) + tail_of(got, n * CHUNK))


def back_kernel(keep, got, yk, yg, ya, zk, zg, za, dwo, dwd, b0, b1, b2, b3, total, ffn):
    j = lax.axis_index("blk")
    ffn[0:288] = yk[0].astype(F32) + yg[0].astype(F32) + ya[...].astype(F32)
    ffn[288:576] = zk[0].astype(F32) + zg[0].astype(F32) + za[...].astype(F32)
    for m in range(3):
        dwd[:, 256 * m : 256 * m + 256] = ffn[384 + 64 * m : 448 + 64 * m]
    total[...] = keep[0:CHUNK].astype(F32) + got[0:CHUNK].astype(F32)
    parts = split(tail_of(keep, CHUNK) + tail_of(got, CHUNK)).astype(F32)
    parts = jnp.concatenate([parts, jnp.zeros((8, 128), F32)], axis=0).astype(BF16)
    for t in range(6):
        at = 480 + 24 * t
        dwo[:, 128 * t : 128 * t + 128] = total[at : at + 24]
    for k, ref in enumerate((b0, b1, b2, b3)):
        for t in range(5):
            part = total[pl.ds(pl.multiple_of(96 * t + 24 * (j ^ k), 8), 24)]
            ref[:, 128 * t : 128 * t + 128] = part.astype(BF16)
        for m in range(4):
            part = ffn[pl.ds(pl.multiple_of(96 * m + 24 * (j ^ k), 8), 24)]
            ref[:, 640 + 256 * m : 896 + 256 * m] = part.astype(BF16)
        ref[:, 1664:1792] = parts


def attn_bwd_kernel(
    qkv, p0, p1, p2, v0, v1, v2, o0, o1, o2, g0, g1, g2, g3,
    dqkv, table_grad,
    dotm, dom, qm, ktm, delta, dst, dq_acc, dk_acc, dv_acc, near, far,
):
    j_me = lax.axis_index("blk")
    low = low_half(T)
    low_short = low_half(128)
    rows_low = lax.broadcasted_iota(jnp.int32, (128, T), 0) < 64

    for k, ref in enumerate((g0, g1, g2, g3)):
        b = j_me ^ k
        first = ref[0:256].astype(F32)
        rest = ref[256:384].astype(F32)
        second = jnp.concatenate([rest, pltpu.roll(rest, 64, 1)], axis=0)
        t0 = jnp.transpose(first)
        t1 = jnp.transpose(second)
        t0 = t0 * jnp.where(rows_low, v0[b], v1[b])
        t1 = jnp.where(rows_low, t1 * v2[b], 0.0)
        t0, t1 = t0.astype(BF16), t1.astype(BF16)
        f0, f1 = t0.astype(F32), t1.astype(F32)
        dotm[0, b] = jnp.where(rows_low, f0, 0.0).astype(BF16)
        dotm[1, b] = jnp.where(rows_low, 0.0, f0).astype(BF16)
        dotm[2, b] = t1
        back = jnp.transpose(f0)
        dom[0, b] = jnp.where(low, back, 0.0).astype(BF16)
        dom[1, b] = jnp.where(low, 0.0, back).astype(BF16)
        dom[2, b] = jnp.transpose(f1).astype(BF16)

    for i in range(TP):
        at = slice(T * i, T * i + T)
        for h in range(HT):
            g = dotm[h, i].astype(F32)
            g = g[64:128] if h == 1 else g[0:64]
            delta[h, i] = jnp.sum((o0, o1, o2)[h][:, at] * g, axis=0, keepdims=True)
        q0 = qkv[0, i].astype(F32)
        turned = pltpu.roll(qkv[3, i].astype(F32), 64, 1)
        qm[0, i] = jnp.where(low, q0, 0.0).astype(BF16)
        qm[1, i] = jnp.where(low, 0.0, q0).astype(BF16)
        qm[2, i] = jnp.where(low, 0.0, turned).astype(BF16)
        k0 = jnp.transpose(qkv[1, i].astype(F32))
        k1 = jnp.transpose(turned)
        ktm[0, :, at] = jnp.where(rows_low, k0, 0.0).astype(BF16)
        ktm[1, :, at] = jnp.where(rows_low, 0.0, k0).astype(BF16)
        ktm[2, :, at] = jnp.where(rows_low, k1, 0.0).astype(BF16)

    dq_acc[...] = jnp.zeros(dq_acc.shape, F32)
    dk_acc[...] = jnp.zeros(dk_acc.shape, F32)
    dv_acc[...] = jnp.zeros(dv_acc.shape, F32)
    table_grad[...] = jnp.zeros(table_grad.shape, F32)
    key_at = lax.broadcasted_iota(jnp.int32, (128, 128), 0)
    query_at = lax.broadcasted_iota(jnp.int32, (128, 128), 1)
    upper = query_at >= key_at
    turn = (key_at + query_at == 127).astype(F32)

    def diagonals(m):
        m = lax.dot_general(
            turn, m, (((1,), (0,)), ((), ())), precision=HIGHEST, preferred_element_type=F32
        )
        return jnp.sum(pltpu.roll(m, 1, 1, stride=1, stride_axis=0), axis=0, keepdims=True)

    row_id = lax.broadcasted_iota(jnp.int32, (NB, 128), 0)
    lane_id = lax.broadcasted_iota(jnp.int32, (NB, 128), 1)
    hot_neg = bucket_of(-lane_id) == row_id
    hot_pos = bucket_of(128 - lane_id) == row_id

    for h, prob in enumerate((p0, p1, p2)):
        second = h // 2
        near[...] = jnp.zeros(near.shape, F32)
        far[...] = jnp.zeros(far.shape, F32)
        for i in range(TP):
            at = slice(T * i, T * i + T)
            row_delta = delta[h, i]
            for j in range(TP):
                dp = dot(qkv[2 + 2 * second, j], dotm[h, i])
                ds = prob[i, j].astype(F32) * (dp - row_delta)
                dst[j] = ds.astype(BF16)
                for a in range(2):
                    for c in range(2):
                        gap = 2 * (j - i) + a - c
                        part = ds[128 * a : 128 * a + 128, 128 * c : 128 * c + 128]
                        if abs(gap) <= 1:
                            near[gap + 1] += part
                        else:
                            far[int(gap > 0)] += jnp.sum(part.reshape(16, 8, 128), axis=0)
            d_all = dst[...].reshape(TP * T, T)
            dq_acc[second, :, at] += dot(ktm[h], d_all)
            dk_acc[second] += dot(d_all, qm[h, i])
            dv_acc[second] += dot(prob[i].reshape(TP * T, T), dom[h, i])
        before, diagonal, after = near[0], near[1], near[2]
        neg = jnp.where(upper, diagonal, before)
        pos = jnp.where(upper, after, diagonal)
        neg, pos = diagonals(neg), diagonals(pos)
        far_neg = jnp.sum(far[0], axis=0, keepdims=True) + jnp.sum(
            jnp.where(upper, before, 0.0), axis=0, keepdims=True
        )
        far_pos = jnp.sum(far[1], axis=0, keepdims=True) + jnp.sum(
            jnp.where(upper, 0.0, after), axis=0, keepdims=True
        )
        spread = (
            jnp.where(hot_neg, neg, 0.0)
            + jnp.where(hot_pos, pos, 0.0)
            + jnp.where(row_id == 15, far_neg, 0.0)
            + jnp.where(row_id == 31, far_pos, 0.0)
        )
        sums = jnp.sum(spread, axis=1, keepdims=True)
        sums = jnp.sum(jnp.where(lane_id == row_id, sums, 0.0), axis=0, keepdims=True)
        table_grad[h : h + 1] = sums
    for i in range(TP):
        at = slice(T * i, T * i + T)
        dq0 = jnp.transpose(dq_acc[0, :, at])
        dq1 = jnp.transpose(dq_acc[1, :, at])
        dqkv[i, :, 0:128] = dq0.astype(BF16)
        dqkv[i, :, 128:256] = dk_acc[0, at].astype(BF16)
        dqkv[i, :, 256:384] = dv_acc[0, at].astype(BF16)
        dqkv[i, :, 384:512] = (dq1 + dk_acc[1, at]).astype(BF16)
        dqkv[i, :, 512:640] = dv_acc[1, at].astype(BF16)


def one_grad_kernel(dqkv, w, keep, give):
    j = lax.axis_index("blk")

    def body(k, carry):
        put_pair(keep, give, k, dot_nt(dqkv[j ^ k], w[...]).astype(BF16))
        return carry

    lax.fori_loop(0, TP, body, 0)


def finish(parts, w, out, gain):
    total = jnp.zeros((w.shape[0], 128), F32)
    for n, part in enumerate(parts):
        at = slice(128 * n, 128 * n + 128)
        total = total + part * w[:, at].astype(F32)
        out[:, at] = part
    return jnp.sum(total, axis=1, keepdims=True) / gain


def put_row(ref, wide):
    rows = wide.shape[0]
    row_id = lax.broadcasted_iota(jnp.int32, (rows, 128), 0)
    eye = row_id == lax.broadcasted_iota(jnp.int32, (rows, 128), 1)
    ref[...] = jnp.sum(jnp.where(eye, wide, 0.0), axis=0, keepdims=True)[:, 0:rows]


def final_kernel(
    b0, b1, b2, b3, gains, wq, wk, wv, wg, wu, dq, dk, dv, dg, du, gg1, gg2, table, src
):
    j_me = lax.axis_index("blk")
    rows = wq.shape[0]
    low = low_half(rows)
    heads = jnp.zeros((128, 128), F32)
    head_id = lax.broadcasted_iota(jnp.int32, (128, 128), 0)
    for k, ref in enumerate((b0, b1, b2, b3)):
        src[j_me ^ k] = ref[:, 0:1664].astype(F32)
        parts = ref[:, 1664:1792].astype(F32)
        for h in range(HT):
            row = parts[h : h + 1] + parts[8 + h : 9 + h]
            heads = jnp.where(head_id == HT * (j_me ^ k) + h, row, heads)
    table[...] = jnp.transpose(heads)[0:NB, 0:H]

    def one(j, n):
        return src[j, 0:rows, 128 * n : 128 * n + 128]

    gain_grad = jnp.zeros((rows, 128), F32)
    for n, (w, out) in enumerate(((wq, dq), (wk, dk), (wv, dv))):
        parts = []
        for j in range(0, TP, 2):
            rest = []
            for m in (j, j + 1):
                last = one(m, 4 if n == 2 else 3)
                rest.append(pltpu.roll(last, 64, 1) if n == 1 else last)
            mid = pltpu.roll(one(j + 1, n), 64, 1)
            parts += [
                one(j, n),
                jnp.where(low, rest[0], mid),
                jnp.where(low, mid, pltpu.roll(rest[1], 64, 1)),
            ]
        gain_grad = gain_grad + finish(parts, w, out, gains[0])
    put_row(gg1, gain_grad)
    gain_grad = jnp.zeros((rows, 128), F32)
    for n, (w, out) in enumerate(((wg, dg), (wu, du))):
        parts = [None] * 16
        for t in range(4):
            at = 5 + 4 * n + t
            for half in range(2):
                a, b = one(2 * half, at), one(2 * half + 1, at)
                parts[4 * t + half] = jnp.where(low, a, pltpu.roll(b, 64, 1))
                parts[4 * t + 2 + half] = jnp.where(low, pltpu.roll(a, 64, 1), b)
        gain_grad = gain_grad + finish(parts, w, out, gains[1])
    put_row(gg2, gain_grad)


def close_kernel(keep, got, along, mixed_grad, tok, gains, tokens_grad):
    x = tok[lax.axis_index("blk")].astype(F32)
    rstd = lax.rsqrt(jnp.mean(x * x, axis=-1, keepdims=True) + EPSILON)
    n = x * rstd
    u = (keep[0].astype(F32) + got[0].astype(F32) + along[...].astype(F32)) * gains[0:1]
    grad = rstd * (u - n * jnp.mean(u * n, axis=-1, keepdims=True))
    tokens_grad[...] = mixed_grad[...] + grad


AXES = ("dp", "blk")
GATE = 0
COST = {"qkv": 0, "attn_fwd": (0, 20, 20), "units": 30, "ffn": 0, "ffn_dw": 0, "mid": 20, "attn_bwd": 40, "one_grad": 40, "stage_y": 10, "stage_z": 10}


def group_local(
    n_dp, n_blk,
    tokens, segment_ids, w_query, w_key, w_value, w_attn_out, attn_gain, rel_bias,
    w_gate, w_up, w_down, ffn_gain, cotangent,
):
    n_dev = n_dp * n_blk

    def later(x, *others):
        return lax.optimization_barrier((x,) + others)[0]

    def swap(x, mask):
        return lax.ppermute(x, AXES, [(d, d ^ mask) for d in range(n_dev)])

    def share(x, *others):
        along = swap(x, 2)
        return (x, swap(x, 1), along, swap(later(along, *others), 1))

    def reduce_pair(keep, give):
        got = swap(give, 1)
        return got, swap(keep[1] + got[1], 2)

    def round_one(x, late=None):
        late = x if late is None else late
        return lax.optimization_barrier((swap(x, 16), swap(late, 8), swap(late, 4)))

    def round_two(state):
        far, near, _ = state
        return lax.optimization_barrier((swap(far, 8), swap(near, 4), swap(far, 4)))

    def gathered(x, one, two):
        far, near, other = one
        last, near_y, far_y = two
        return (x, near, far, last, other, near_y, far_y, swap(last, 4))

    tok_own, cot_own = tokens[0], cotangent[0]
    rows, ff = w_query.shape[0], w_gate.shape[1]
    flat = TP * T
    table = rel_bias.astype(F32)

    toks_x, toks_c = swap(tok_own, 2), swap(tok_own, 1)
    *slabs, gain_cols = call(
        prep_kernel,
        (sds((rows, 1664), BF16),) * TP + (sds((2, rows, 128), F32),),
        w_query, w_key, w_value, w_gate, w_up, attn_gain, ffn_gain,
        name="prep", vmem=60, held=(0, 1, 2, 3, 4),
        scratch=(
            pltpu.VMEM((TP, rows, 1664), BF16),
            *(pltpu.VMEM((rows, D), BF16),) * 3,
            *(pltpu.VMEM((rows, ff), BF16),) * 2,
            pltpu.SemaphoreType.DMA((5,)),
        ),
    )
    slabs = (slabs[0], swap(slabs[1], 1), swap(slabs[2], 2), swap(slabs[3], 3))
    bias = call(bias_kernel, sds((HT, 3, T, T), F32), table, smem=(0,), name="bias")
    first = call(
        pack_kernel, sds((128, 640), BF16), *slabs, w_attn_out,
        name="pack", vmem=60, held=(4,), after=(bias,),
        scratch=(pltpu.VMEM((96, 640), F32), pltpu.VMEM((rows, D), BF16), pltpu.SemaphoreType.DMA),
    )
    second, extra = call(
        pack_more_kernel, (sds((576, 256), BF16), sds((T + 16, D), BF16)),
        *slabs, w_down, cot_own, segment_ids, name="pack_more", vmem=60, held=(4, 5), after=(first,),
        scratch=(
            pltpu.VMEM((96, 1024), F32), pltpu.VMEM((64, D), BF16), pltpu.SemaphoreType.DMA((2,)),
        ),
    )
    first_one = round_one(first)
    first_two = round_two(lax.optimization_barrier(first_one + (extra,))[:3])
    firsts = gathered(first, first_one, first_two)
    toks = (tok_own, toks_c, toks_x, swap(later(toks_x, *first_two), 1))
    second_one = round_one(later(second, *first_one), later(second, *first_two))

    tok, n1, qkv, w_qkv, gains = call(
        qkv_kernel,
        (
            sds((TP, T, D), BF16), sds((TP, T, D), BF16), sds((5, TP, T, 128), BF16),
            sds((D, 640), BF16), sds((8, D), F32),
        ),
        *toks, *firsts, name="qkv", vmem=16, cost=COST["qkv"],
    )
    extras = share(extra, gains)
    cot, segq, segk = call(
        row_kernel, (sds((TP, T, D), BF16), sds((TP, 8, T), F32), sds((TP, T, T), F32)),
        *extras, name="row",
    )
    stripes = call(
        stripes_kernel, sds((192, D), BF16), *firsts, name="stripes", after=(segq,),
        scratch=(pltpu.VMEM((192, D), F32),),
    )
    stripes = share(stripes)
    wop = call(
        out_weight_kernel, sds((D, D), BF16), *stripes, name="out_weight",
        scratch=(pltpu.VMEM((D, D), F32),),
    )
    heads = []
    for h in range(HT):
        heads.append(
            call(
                functools.partial(attn_fwd_kernel, h),
                (sds((TP, TP, T, T), BF16), sds((TP, 1, T), F32), sds((DH, flat), F32)),
                table, bias, qkv, segq, segk, smem=(0,), name="attn_fwd", vmem=14,
                cost=COST["attn_fwd"][h], after=(heads[-1][1],) if heads else (),
                scratch=(
                    pltpu.VMEM((TP, 128, T), BF16),
                    pltpu.VMEM((DH, flat), BF16),
                    pltpu.VMEM((TP, T, T), F32),
                ),
            )
        )
    probs, inv_tots, out_ts = zip(*heads)
    second_two = round_two(lax.optimization_barrier(second_one + (inv_tots[GATE],))[:3])
    seconds = gathered(second, second_one, second_two)
    att = call(join_kernel, sds((1536, 128), BF16), *out_ts, name="join")
    atts = share(att, wop)
    wgu, wd = call(
        units_kernel, (sds((D, 1024), BF16), sds((512, D), BF16)), *seconds, name="units",
        cost=COST["units"],
    )
    attc, n2, hid, ggug, two_keep, two_give, lo_keep, lo_give, mixed_own = call(
        ffn_kernel,
        (
            sds((TP, T, D), BF16), sds((TP, T, D), BF16),
            sds((TP, T, 512), BF16), sds((TP, T, 1024), BF16),
            sds((2, T, D), BF16), sds((2, T, D), BF16), sds((2, T, D), BF16), sds((2, T, D), BF16),
            sds((T, D), F32),
        ),
        *atts, gains, wop, wgu, wd, tok, cot, name="ffn", vmem=30, cost=COST["ffn"],
    )
    two_c, two_x = reduce_pair(two_keep, two_give)
    y_keep, y_give, z_keep, z_give = call(
        ffn_dw_kernel, (sds((4, 288, 256), BF16),) * 4,
        n2.reshape(flat, D), ggug.reshape(flat, 1024), hid.reshape(flat, 512), cot.reshape(flat, D),
        name="ffn_dw", vmem=20, cost=COST["ffn_dw"],
        scratch=(pltpu.VMEM((D, 1024), F32), pltpu.VMEM((512, D), F32)),
    )
    y_got, z_got = swap(y_give, 4), swap(z_give, 8)
    mixed_grad, g0, g1, g2, g3, wo_keep, *wo_gives = call(
        mid_kernel,
        (sds((T, D), F32),) + (sds((384, 128), BF16),) * 4
        + (sds((2, 8, 24, D), BF16),) + (sds((8, 24, D), BF16),) * 2,
        two_keep, two_c, two_x, mixed_own, cot, attc, wop, gains, name="mid", vmem=16,
        after=(y_give,), scratch=(pltpu.VMEM((D, D), F32),), cost=COST["mid"],
    )
    g1, g2, g3 = swap(g1, 1), swap(g2, 2), swap(g3, 3)
    lo_c = swap(later(lo_give, mixed_grad), 1)
    lo_x = swap(later(lo_keep[1] + lo_c[1], g1, g2, g3), 2)
    layer_out = mixed_own + lo_keep[0].astype(F32) + lo_c[0].astype(F32) + lo_x.astype(F32)
    wo_got = (swap(wo_gives[0], 1), swap(wo_gives[1], 1))
    wo_along = swap(later(wo_keep[1] + wo_got[1], g1, g2, g3), 2)
    dqkv, table_grad = call(
        attn_bwd_kernel,
        (sds((TP, T, 640), BF16), sds((8, 128), F32)),
        qkv, *probs, *inv_tots, *out_ts, g0, g1, g2, g3, name="attn_bwd", vmem=26,
        cost=COST["attn_bwd"], after=(y_got, z_got),
        scratch=(
            pltpu.VMEM((HT, TP, 128, T), BF16),
            pltpu.VMEM((HT, TP, T, 128), BF16),
            pltpu.VMEM((HT, TP, T, 128), BF16),
            pltpu.VMEM((HT, 128, TP * T), BF16),
            pltpu.VMEM((HT, TP, 1, T), F32),
            pltpu.VMEM((TP, T, T), BF16),
            pltpu.VMEM((2, 128, TP * T), F32),
            pltpu.VMEM((2, TP * T, 128), F32),
            pltpu.VMEM((2, TP * T, 128), F32),
            pltpu.VMEM((3, 128, 128), F32),
            pltpu.VMEM((2, 8, 128), F32),
        ),
    )

    def chunks(n):
        return sds((n * CHUNK + TAIL, 128), BF16)

    keep, give = call(
        attn_dw_kernel, (chunks(4),) * 2,
        n1.reshape(flat, D), dqkv.reshape(flat, 640), wo_keep, wo_got[0], wo_along, table_grad,
        name="attn_dw", vmem=16,
        scratch=(
            pltpu.VMEM((D, 640), F32), pltpu.VMEM((8, 24, D), F32), pltpu.VMEM((CHUNK, 128), F32),
        ),
    )
    got = swap(give, 4)
    y_keep, y_give, z_keep, z_give = call(
        ffn_second_kernel, (sds((2, 288, 256), BF16),) * 4, y_keep, y_got, z_keep, z_got,
        name="ffn_second", after=(give,),
    )
    y_got, z_got = swap(y_give, 8), swap(z_give, 16)
    one_keep, one_give = call(
        one_grad_kernel, (sds((2, T, D), BF16),) * 2, dqkv, w_qkv, name="one_grad", vmem=16,
        after=(y_give,), cost=COST["one_grad"],
    )
    one_c, one_x = reduce_pair(one_keep, one_give)
    tokens_grad = call(
        close_kernel, sds((T, D), F32), one_keep, one_c, one_x, mixed_grad, tok, gains,
        name="close", vmem=10,
    )
    y_give, z_give = call(
        ffn_third_kernel, (sds((288, 256), BF16),) * 2, y_keep, y_got, z_keep, z_got,
        name="ffn_third", after=(give,),
    )
    y_along, z_along = swap(y_give, 16), swap(z_give, 4)
    keep, give = call(
        functools.partial(stage_kernel, 4), (chunks(2),) * 2, keep, got, name="stage_y",
        after=(y_give,), cost=COST["stage_y"],
    )
    got = swap(give, 8)
    keep, give = call(
        functools.partial(stage_kernel, 2), (chunks(1),) * 2, keep, got, name="stage_z",
        after=(y_along, z_along), cost=COST["stage_z"],
    )
    got = swap(give, 16)
    dwo, dwd, *backs = call(
        back_kernel,
        (sds((rows, D), F32), sds((64, D), F32)) + (sds((rows, 1792), BF16),) * 4,
        keep, got, y_keep, y_got, y_along, z_keep, z_got, z_along, name="back", after=(tokens_grad,),
        scratch=(pltpu.VMEM((CHUNK, 128), F32), pltpu.VMEM((576, 256), F32)),
    )
    backs = (backs[0], swap(backs[1], 1), swap(backs[2], 2), swap(backs[3], 3))
    dq, dk, dv, dg, du, gg1, gg2, table_sum = call(
        final_kernel,
        (sds((rows, D), F32),) * 3
        + (sds((rows, ff), F32),) * 2
        + (sds((1, rows), F32), sds((1, rows), F32), sds((NB, H), F32)),
        *backs, gain_cols, w_query, w_key, w_value, w_gate, w_up, name="final",
        scratch=(pltpu.VMEM((TP, rows, 1664), F32),),
    )

    return (
        layer_out.astype(BF16)[None],
        tokens_grad[None],
        dq,
        dk,
        dv,
        dwo,
        gg1[0],
        table_sum,
        dg,
        du,
        dwd,
        gg2[0],
    )


KEY_BLOCK = 256
HIGHEST = lax.Precision.HIGHEST


def rms_norm(values, gain):
    return values * lax.rsqrt(jnp.mean(values * values, axis=-1, keepdims=True) + EPSILON) * gain


def split_heads(flat_rows):
    return flat_rows.reshape(flat_rows.shape[0], flat_rows.shape[1], H, DH)


def join_heads(per_head):
    return per_head.reshape(per_head.shape[0], per_head.shape[1], H * DH)


def project(left, matrix):
    return jnp.einsum("rtd,de->rte", left, matrix, preferred_element_type=jnp.float32)


def project_back(left, matrix):
    return jnp.einsum("rte,de->rtd", left, matrix, preferred_element_type=jnp.float32)


def weight_grad(left, right):
    return jnp.einsum("rtd,rte->de", left, right, preferred_element_type=jnp.float32)


def block_scores(queries, key_block, query_pos, key_pos, query_seg, key_seg, bias_table):
    raw_scores = jnp.einsum(
        "rqhd,rkhd->rhqk", queries, key_block, preferred_element_type=jnp.float32
    )
    buckets = bucket_of(key_pos[None, :] - query_pos[:, None])
    one_hot = (buckets[:, :, None] == jnp.arange(NB, dtype=jnp.int32)[None, None, :]).astype(
        jnp.float32
    )
    rel_term = jnp.einsum("qkb,bh->hqk", one_hot, bias_table, precision=HIGHEST)
    allowed = (query_seg[:, :, None] == key_seg[:, None, :])[:, None]
    return (raw_scores + rel_term[None], allowed, one_hot)


def absorb(
    running, queries, key_block, value_block, query_pos, key_pos, query_seg, key_seg, bias_table
):
    row_peak, row_total, weighted = running
    scores, allowed, unused = block_scores(
        queries, key_block, query_pos, key_pos, query_seg, key_seg, bias_table
    )
    block_peak = jnp.max(jnp.where(allowed, scores, MASKED), axis=-1)
    new_peak = jnp.maximum(row_peak, block_peak)
    weights = jnp.where(allowed, jnp.exp(scores - new_peak[..., None]), 0.0)
    factor = jnp.exp(row_peak - new_peak)
    row_total = row_total * factor + jnp.sum(weights, axis=-1)
    weighted = weighted * factor[..., None] + jnp.einsum(
        "rhqk,rkhd->rhqd",
        weights.astype(jnp.bfloat16),
        value_block,
        preferred_element_type=jnp.float32,
    )
    return (new_peak, row_total, weighted)


def pair_grads(
    queries,
    out_grad,
    log_total,
    row_delta,
    key_block,
    value_block,
    query_pos,
    key_pos,
    query_seg,
    key_seg,
    bias_table,
):
    scores, allowed, one_hot = block_scores(
        queries, key_block, query_pos, key_pos, query_seg, key_seg, bias_table
    )
    prob_map = jnp.where(allowed, jnp.exp(scores - log_total[..., None]), 0.0)
    prob_grad = jnp.einsum(
        "rqhd,rkhd->rhqk", out_grad, value_block, preferred_element_type=jnp.float32
    )
    score_grad = prob_map * (prob_grad - row_delta[..., None])
    score_low = score_grad.astype(jnp.bfloat16)
    query_grad = jnp.einsum(
        "rhqk,rkhd->rqhd", score_low, key_block, preferred_element_type=jnp.float32
    )
    key_grad = jnp.einsum("rhqk,rqhd->rkhd", score_low, queries, preferred_element_type=jnp.float32)
    value_grad = jnp.einsum(
        "rhqk,rqhd->rkhd",
        prob_map.astype(jnp.bfloat16),
        out_grad,
        preferred_element_type=jnp.float32,
    )
    table_grad = jnp.einsum("rhqk,qkb->bh", score_grad, one_hot, precision=HIGHEST)
    return (query_grad, key_grad, value_grad, table_grad)


def in_blocks(step_fn, running, pieces):
    length = pieces[0].shape[1]
    block_size = math.gcd(length, KEY_BLOCK)
    block_count = length // block_size
    stacked = tuple(
        (
            jnp.moveaxis(
                member.reshape((member.shape[0], block_count, block_size) + member.shape[2:]), 1, 0
            )
            for member in pieces
        )
    )
    starts = block_size * jnp.arange(block_count, dtype=jnp.int32)

    def scan_step(inner_state, item_pair):
        return (step_fn(inner_state, item_pair[0], item_pair[1]), None)

    running, unused = lax.scan(scan_step, running, (stacked, starts))
    return running


def local(
    tokens,
    segment_ids,
    w_query,
    w_key,
    w_value,
    w_attn_out,
    attn_gain,
    rel_bias,
    w_gate,
    w_up,
    w_down,
    ffn_gain,
    cotangent,
):
    row_count, local_len, unused_dim = tokens.shape
    my_block = lax.axis_index("blk")
    full_query, full_key, full_value, full_out, gain_one = (
        lax.all_gather(w_query, ("dp", "blk"), axis=0, tiled=True),
        lax.all_gather(w_key, ("dp", "blk"), axis=0, tiled=True),
        lax.all_gather(w_value, ("dp", "blk"), axis=0, tiled=True),
        lax.all_gather(w_attn_out, ("dp", "blk"), axis=0, tiled=True),
        lax.all_gather(attn_gain, ("dp", "blk"), axis=0, tiled=True),
    )
    full_gate, full_up, full_down, gain_two = (
        lax.all_gather(w_gate, ("dp", "blk"), axis=0, tiled=True),
        lax.all_gather(w_up, ("dp", "blk"), axis=0, tiled=True),
        lax.all_gather(w_down, ("dp", "blk"), axis=0, tiled=True),
        lax.all_gather(ffn_gain, ("dp", "blk"), axis=0, tiled=True),
    )
    row_segs = lax.all_gather(segment_ids, "blk", axis=1, tiled=True)
    bias_table = rel_bias.astype(jnp.float32)
    gain_one_f = gain_one.astype(jnp.float32)
    gain_two_f = gain_two.astype(jnp.float32)
    inputs = tokens.astype(jnp.float32)
    query_pos = my_block * local_len + jnp.arange(local_len, dtype=jnp.int32)
    normed_one = rms_norm(inputs, gain_one_f).astype(jnp.bfloat16)
    query_flat = project(normed_one, full_query).astype(jnp.bfloat16)
    key_flat = project(normed_one, full_key).astype(jnp.bfloat16)
    value_flat = project(normed_one, full_value).astype(jnp.bfloat16)
    queries = split_heads(query_flat)
    key_heads = split_heads(key_flat)
    value_heads = split_heads(value_flat)

    def forward_piece(running, pieces):

        def step_fn(inner_state, blocks, block_start):
            block_len = blocks[0].shape[1]
            key_pos = block_start + jnp.arange(block_len, dtype=jnp.int32)
            key_seg = lax.dynamic_slice_in_dim(row_segs, block_start, block_len, 1)
            return absorb(
                inner_state,
                queries,
                split_heads(blocks[0]),
                split_heads(blocks[1]),
                query_pos,
                key_pos,
                segment_ids,
                key_seg,
                bias_table,
            )

        return in_blocks(step_fn, running, pieces)

    stat_shape = (row_count, H, local_len)
    start_state = (
        jnp.full(stat_shape, MASKED, jnp.float32),
        jnp.zeros(stat_shape, jnp.float32),
        jnp.zeros(stat_shape + (DH,), jnp.float32),
    )
    row_peak, row_total, weighted = forward_piece(
        start_state,
        (
            lax.all_gather(key_flat, "blk", axis=1, tiled=True),
            lax.all_gather(value_flat, "blk", axis=1, tiled=True),
        ),
    )
    log_total = row_peak + jnp.log(row_total)
    attended_f = jnp.transpose(weighted / row_total[..., None], (0, 2, 1, 3))
    attended = join_heads(attended_f).astype(jnp.bfloat16)
    mixed_in = inputs + project(attended, full_out)
    normed_two = rms_norm(mixed_in, gain_two_f).astype(jnp.bfloat16)
    gate_act = project(normed_two, full_gate)
    up_act = project(normed_two, full_up)

    def gated(gate_in, up_in):
        return jax.nn.gelu(gate_in, approximate=True) * up_in

    hidden_f, gated_back = jax.vjp(gated, gate_act, up_act)
    hidden = hidden_f.astype(jnp.bfloat16)
    layer_out = (mixed_in + project(hidden, full_down)).astype(jnp.bfloat16)
    down_grad = weight_grad(hidden, cotangent)
    hidden_grad = project_back(cotangent, full_down)
    gate_grad, up_grad = gated_back(hidden_grad)
    gate_low = gate_grad.astype(jnp.bfloat16)
    up_low = up_grad.astype(jnp.bfloat16)
    gate_w_grad = weight_grad(normed_two, gate_low)
    up_w_grad = weight_grad(normed_two, up_low)
    two_grad = project_back(gate_low, full_gate) + project_back(up_low, full_up)
    unused_two, norm_two_back = jax.vjp(rms_norm, mixed_in, gain_two_f)
    mixed_part, gain_two_grad = norm_two_back(two_grad)
    mixed_grad = cotangent.astype(jnp.float32) + mixed_part
    mixed_low = mixed_grad.astype(jnp.bfloat16)
    out_w_grad = weight_grad(attended, mixed_low)
    attended_grad = project_back(mixed_low, full_out).astype(jnp.bfloat16)
    grad_heads = split_heads(attended_grad)
    row_delta = jnp.sum(
        jnp.transpose(grad_heads.astype(jnp.float32), (0, 2, 1, 3))
        * (weighted / row_total[..., None]),
        axis=-1,
    )
    zero_heads = jnp.zeros(queries.shape, jnp.float32)
    zero_table = jnp.zeros((NB, H), jnp.float32)

    def query_piece(running, pieces):

        def step_fn(inner_state, blocks, block_start):
            block_len = blocks[0].shape[1]
            key_pos = block_start + jnp.arange(block_len, dtype=jnp.int32)
            key_seg = lax.dynamic_slice_in_dim(row_segs, block_start, block_len, 1)
            pair_parts = pair_grads(
                queries,
                grad_heads,
                log_total,
                row_delta,
                split_heads(blocks[0]),
                split_heads(blocks[1]),
                query_pos,
                key_pos,
                segment_ids,
                key_seg,
                bias_table,
            )
            return inner_state + pair_parts[0]

        return in_blocks(step_fn, running, pieces)

    query_grad = join_heads(
        query_piece(
            zero_heads,
            (
                lax.all_gather(key_flat, "blk", axis=1, tiled=True),
                lax.all_gather(value_flat, "blk", axis=1, tiled=True),
            ),
        )
    )
    log_rows, delta_rows = (
        lax.all_gather(log_total, "blk", axis=2, tiled=True),
        lax.all_gather(row_delta, "blk", axis=2, tiled=True),
    )

    def key_piece(running, pieces):

        def step_fn(inner_state, blocks, block_start):
            block_len = blocks[0].shape[1]
            piece_pos = block_start + jnp.arange(block_len, dtype=jnp.int32)
            piece_seg = lax.dynamic_slice_in_dim(row_segs, block_start, block_len, 1)
            piece_log = lax.dynamic_slice_in_dim(log_rows, block_start, block_len, 2)
            piece_delta = lax.dynamic_slice_in_dim(delta_rows, block_start, block_len, 2)
            pair_parts = pair_grads(
                split_heads(blocks[0]),
                split_heads(blocks[1]),
                piece_log,
                piece_delta,
                key_heads,
                value_heads,
                piece_pos,
                query_pos,
                piece_seg,
                segment_ids,
                bias_table,
            )
            return (
                inner_state[0] + pair_parts[1],
                inner_state[1] + pair_parts[2],
                inner_state[2] + pair_parts[3],
            )

        return in_blocks(step_fn, running, pieces)

    key_grad, value_grad, table_grad = key_piece(
        (zero_heads, zero_heads, zero_table),
        (
            lax.all_gather(query_flat, "blk", axis=1, tiled=True),
            lax.all_gather(attended_grad, "blk", axis=1, tiled=True),
        ),
    )
    query_low = query_grad.astype(jnp.bfloat16)
    key_low = join_heads(key_grad).astype(jnp.bfloat16)
    value_low = join_heads(value_grad).astype(jnp.bfloat16)
    query_w_grad = weight_grad(normed_one, query_low)
    key_w_grad = weight_grad(normed_one, key_low)
    value_w_grad = weight_grad(normed_one, value_low)
    one_grad = (
        project_back(query_low, full_query)
        + project_back(key_low, full_key)
        + project_back(value_low, full_value)
    )
    unused_one, norm_one_back = jax.vjp(rms_norm, inputs, gain_one_f)
    input_part, gain_one_grad = norm_one_back(one_grad)
    tokens_grad = mixed_grad + input_part
    table_sum = lax.psum(table_grad, ("dp", "blk"))
    all_sums = (
        lax.psum_scatter(query_w_grad, ("dp", "blk"), scatter_dimension=0, tiled=True),
        lax.psum_scatter(key_w_grad, ("dp", "blk"), scatter_dimension=0, tiled=True),
        lax.psum_scatter(value_w_grad, ("dp", "blk"), scatter_dimension=0, tiled=True),
        lax.psum_scatter(out_w_grad, ("dp", "blk"), scatter_dimension=0, tiled=True),
        lax.psum_scatter(gain_one_grad, ("dp", "blk"), scatter_dimension=0, tiled=True),
        lax.psum_scatter(gate_w_grad, ("dp", "blk"), scatter_dimension=0, tiled=True),
        lax.psum_scatter(up_w_grad, ("dp", "blk"), scatter_dimension=0, tiled=True),
        lax.psum_scatter(down_grad, ("dp", "blk"), scatter_dimension=0, tiled=True),
        lax.psum_scatter(gain_two_grad, ("dp", "blk"), scatter_dimension=0, tiled=True),
    )
    return (
        layer_out,
        tokens_grad,
        all_sums[0],
        all_sums[1],
        all_sums[2],
        all_sums[3],
        all_sums[4],
        table_sum,
        all_sums[5],
        all_sums[6],
        all_sums[7],
        all_sums[8],
    )


def solution(mesh):
    whole = P(AXES, None)
    rows = P("dp", "blk", None)
    n_dp, n_blk = mesh.shape["dp"], mesh.shape["blk"]
    grouped = functools.partial(group_local, n_dp, n_blk)
    body = grouped if (n_dp, n_blk) == (8, TP) else local
    return jax.shard_map(
        body,
        mesh=mesh,
        in_specs=(
            rows, P("dp", "blk"), whole, whole, whole, whole, P(AXES), P(),
            whole, whole, whole, P(AXES), rows,
        ),
        out_specs=(
            rows, rows, whole, whole, whole, whole, P(AXES), P(), whole, whole, whole, P(AXES),
        ),
        check_vma=False,
    )
```

```python
import functools
import math

import jax
import jax.numpy as jnp
from jax import lax
from jax.experimental import pallas as pl
from jax.experimental.pallas import tpu as pltpu
from jax.sharding import PartitionSpec as P

D = 768
H = 12
DH = 64
NB = 32
THRESHOLDS = (12, 16, 23, 32, 46, 64, 91)
MASKED = -1e30
EPSILON = 1e-06
TP = 4
T = 256
HT = 3
F32 = jnp.float32
BF16 = jnp.bfloat16
MIB = 1 << 20


def dot(a, b):
    return lax.dot_general(a, b, (((1,), (0,)), ((), ())), preferred_element_type=F32)


def dot_nt(a, b):
    return lax.dot_general(a, b, (((1,), (1,)), ((), ())), preferred_element_type=F32)


def dot_tn(a, b):
    return lax.dot_general(a, b, (((0,), (0,)), ((), ())), preferred_element_type=F32)


def bucket_of(relative):
    distance = jnp.abs(relative)
    far = jnp.full(relative.shape, 8, jnp.int32)
    for threshold in THRESHOLDS:
        far = far + (distance >= threshold).astype(jnp.int32)
    return jnp.where(relative > 0, NB // 2, 0) + jnp.where(distance < 8, distance, far)


def call(
    kernel, out_shape, *args, scratch=(), smem=(), held=(), after=(), vmem=8, cost=0, name=None
):
    vspec = pl.BlockSpec(memory_space=pltpu.VMEM)
    sspec = pl.BlockSpec(memory_space=pltpu.SMEM)
    aspec = pl.BlockSpec(memory_space=pl.ANY)
    hspec = pl.BlockSpec(memory_space=pltpu.HBM)
    skip = len(after)

    def body(*refs):
        kernel(*refs[skip:])

    specs = [sspec if n in smem else hspec if n in held else vspec for n in range(len(args))]
    return pl.pallas_call(
        body,
        out_shape=out_shape,
        in_specs=[aspec] * skip + specs,
        out_specs=jax.tree.map(lambda _: vspec, out_shape),
        scratch_shapes=list(scratch),
        compiler_params=pltpu.CompilerParams(vmem_limit_bytes=vmem * MIB),
        cost_estimate=pl.CostEstimate(flops=cost * 1_150_000_000, bytes_accessed=0, transcendentals=0),
        name=name,
    )(*after, *args)


def sds(shape, dtype):
    return jax.ShapeDtypeStruct(shape, dtype)


def low_half(rows):
    return lax.broadcasted_iota(jnp.int32, (rows, 128), 1) < 64


def prep_kernel(
    wq, wk, wv, wg, wu, tok, seg, g1, g2, s0, s1, s2, s3, ts, gains, slabs, vq, vk, vv, vg, vu, sems
):
    j_me = lax.axis_index("blk")
    rows = wq.shape[0]
    pairs = ((wq, vq), (wk, vk), (wv, vv), (wg, vg), (wu, vu), (tok, ts.at[0:T]))
    copies = [pltpu.make_async_copy(a, b, sems.at[n]) for n, (a, b) in enumerate(pairs)]
    for copy in copies:
        copy.start()
    eye = lax.broadcasted_iota(jnp.int32, (rows, rows), 0) == lax.broadcasted_iota(
        jnp.int32, (rows, rows), 1
    )
    columns = []
    for n, ref in enumerate((g1, g2)):
        row = jnp.broadcast_to(ref[...].astype(F32).reshape(1, rows), (rows, rows))
        column = jnp.sum(jnp.where(eye, row, 0.0), axis=1, keepdims=True)
        columns.append(column)
        gains[n] = jnp.broadcast_to(column, (rows, 128))
    ids = jnp.broadcast_to(seg[...], (16, T))
    ts[T : T + 16, 0:T] = (ids // 2).astype(F32).astype(BF16)
    ts[T : T + 16, T : 2 * T] = (ids % 2).astype(F32).astype(BF16)
    ts[T : T + 16, 2 * T : 3 * T] = jnp.zeros((16, T), BF16)
    low = low_half(rows)
    lane = lax.broadcasted_iota(jnp.int32, (rows, 128), 1)
    spare = jnp.where(lane == 64, columns[0], jnp.where(lane == 65, columns[1], 0.0))
    for copy in copies:
        copy.wait()

    def tile(ref, index):
        return ref[:, 128 * index : 128 * index + 128].astype(F32)

    for j in range(TP):
        first, second = [], []
        for ref in (vq, vk, vv):
            at = 192 * j // 128
            a, b = tile(ref, at), tile(ref, at + 1)
            if j % 2:
                a, b = pltpu.roll(a, 64, 1), pltpu.roll(b, 64, 1)
                a = jnp.where(low, a, b)
            first.append(a)
            second.append(b)
        tiles = first + [
            jnp.where(low, second[0], pltpu.roll(second[1], 64, 1)),
            jnp.where(low, second[2], spare),
        ]
        for ref in (vg, vu):
            for t in range(4):
                a = tile(ref, 4 * t + j // 2)
                b = tile(ref, 4 * t + 2 + j // 2)
                if j % 2:
                    tiles.append(jnp.where(low, pltpu.roll(a, 64, 1), b))
                else:
                    tiles.append(jnp.where(low, a, pltpu.roll(b, 64, 1)))
        for n, v in enumerate(tiles):
            slabs[j ^ j_me, :, 128 * n : 128 * n + 128] = v.astype(BF16)
    for k, ref in enumerate((s0, s1, s2, s3)):
        ref[...] = slabs[k]


def pack_kernel(s0, s1, s2, s3, wo, first, whole, vo, sem):
    j = lax.axis_index("blk")
    rows = s0.shape[0]
    copy = pltpu.make_async_copy(wo, vo, sem)
    copy.start()
    for k, ref in enumerate((s0, s1, s2, s3)):
        whole[pl.ds(pl.multiple_of(rows * (j ^ k), 8), rows)] = ref[:, 0:640].astype(F32)
    first[0:96] = whole[...].astype(BF16)
    copy.wait()
    out = vo[...].astype(F32)
    rest = [out[8 * n : 8 * n + 8, 640:768] for n in range(3)]
    rest = jnp.concatenate(rest + [jnp.zeros((8, 256), F32)], axis=1)
    first[96:128] = jnp.concatenate([out[:, 0:640], rest], axis=0).astype(BF16)


def pack_more_kernel(s0, s1, s2, s3, wd, second, whole, vd, sem):
    j = lax.axis_index("blk")
    rows = s0.shape[0]
    copy = pltpu.make_async_copy(wd, vd, sem)
    copy.start()
    for k, ref in enumerate((s0, s1, s2, s3)):
        whole[pl.ds(pl.multiple_of(rows * (j ^ k), 8), rows)] = ref[:, 640:1664].astype(F32)
    for n in range(4):
        second[96 * n : 96 * n + 96] = whole[:, 256 * n : 256 * n + 256].astype(BF16)
    copy.wait()
    for n in range(3):
        second[384 + 64 * n : 448 + 64 * n] = vd[:, 256 * n : 256 * n + 256]


def stripes_kernel(p0, p1, p2, p3, p4, p5, p6, p7, out, whole):
    dp = lax.axis_index("dp")
    for n, ref in enumerate((p0, p1, p2, p3, p4, p5, p6, p7)):
        at = pl.ds(pl.multiple_of(24 * (dp ^ piece_at(n)), 8), 24)
        part = ref[96:128].astype(F32)
        whole[at, 0:640] = part[0:24]
        rest = [part[24:32, 128 * m : 128 * m + 128] for m in range(3)]
        whole[at, 640:768] = jnp.concatenate(rest, axis=0)
    out[...] = whole[...].astype(BF16)


def out_weight_kernel(p0, p1, p2, p3, out, whole):
    j = lax.axis_index("blk")
    for k, ref in enumerate((p0, p1, p2, p3)):
        rows = ref[...].astype(F32)
        for d in range(8):
            at = pl.multiple_of(24 * (TP * d + (j ^ k)), 8)
            whole[pl.ds(at, 24)] = rows[24 * d : 24 * d + 24]
    for k in range(TP):
        at = pl.multiple_of(192 * (j ^ k), 64)
        out[128 * k : 128 * k + 128] = whole[pl.ds(at, 128)].astype(BF16)
        out[512 + 64 * k : 576 + 64 * k] = whole[pl.ds(at + 128, 64)].astype(BF16)


def bias_kernel(table, out):
    j = lax.axis_index("blk")
    lane = lax.broadcasted_iota(jnp.int32, (8, 512), 1)
    for n in range(3):
        off = (n - 1) * T
        rel = jnp.where(lane < 256, off - lane, off + 512 - lane)
        bucket = bucket_of(rel)
        for h in range(HT):
            row = jnp.zeros((8, 512), F32)
            for b in range(NB):
                row = jnp.where(bucket == b, table[HT * j + h, b], row)
            wide = jnp.broadcast_to(row[0:1], (T, 512))
            out[h, n] = pltpu.roll(wide, 0, 1, stride=1, stride_axis=0)[:, :T]


def piece_at(n):
    return 2 * (n % 4) + n // 4


def qkv_kernel(
    t0, t1, t2, t3, p0, p1, p2, p3, p4, p5, p6, p7, tok, n1, qkv, w, gains, segq, segk
):
    j = lax.axis_index("blk")
    dp = lax.axis_index("dp")
    for k, ref in enumerate((t0, t1, t2, t3)):
        tok[j ^ k] = ref[0:T]
        parts = ref[T : T + 16].astype(F32)
        row = (2.0 * parts[:, 0:T] + parts[:, T : 2 * T])[0:8]
        segq[j ^ k] = row
        col = jnp.transpose(jnp.broadcast_to(row[0:1], (128, T)))
        segk[j ^ k, :, 0:128] = col
        segk[j ^ k, :, 128:256] = col
    for n, ref in enumerate((p0, p1, p2, p3, p4, p5, p6, p7)):
        w[pl.ds(pl.multiple_of(96 * (dp ^ piece_at(n)), 32), 96)] = ref[0:96]
    turned = jnp.transpose(w[:, 512:640].astype(F32))
    gains[...] = turned[64:72]

    def body(b, carry):
        x = tok[b].astype(F32)
        rstd = lax.rsqrt(jnp.mean(x * x, axis=-1, keepdims=True) + EPSILON)
        n = (x * rstd * gains[0:1]).astype(BF16)
        n1[b] = n
        y = dot(n, w[...])
        for t in range(5):
            qkv[t, b] = y[:, 128 * t : 128 * t + 128].astype(BF16)
        return carry

    lax.fori_loop(0, TP, body, 0)


def attn_fwd_kernel(h, table, bias, qkv, segq, segk, prob, inv_tot, out_t, qt, vt, sc):
    j_me = lax.axis_index("blk")
    rows_low = lax.broadcasted_iota(jnp.int32, (128, T), 0) < 64
    half = slice(64, 128) if h == 1 else slice(0, 64)
    for i in range(TP):
        if h < 2:
            q = jnp.transpose(qkv[0, i].astype(F32))
        else:
            q = jnp.transpose(pltpu.roll(qkv[3, i].astype(F32), 64, 1))
        qt[i] = jnp.where(rows_low == (h == 0), q, 0.0).astype(BF16)
        v = jnp.transpose(qkv[2 + 2 * (h // 2), i].astype(F32)).astype(BF16)
        vt[:, T * i : T * i + T] = v[half]

    tile = 1 + 2 * (h // 2)
    far = (table[HT * j_me + h, 15], table[HT * j_me + h, 31])
    for i in range(TP):
        peak = jnp.full((1, T), MASKED, F32)
        for j in range(TP):
            s = dot(qkv[tile, j], qt[i])
            if abs(j - i) <= 1:
                s = s + bias[h, j - i + 1]
            else:
                s = s + far[j > i]
            if i in (0, TP - 1) or j in (0, TP - 1):
                s = jnp.where(segk[j] == segq[i, 0:1], s, MASKED)
            sc[j] = s
            peak = jnp.maximum(peak, jnp.max(s, axis=0, keepdims=True))
        total = jnp.zeros((1, T), F32)
        for j in range(TP):
            p = jnp.exp(sc[j] - peak)
            total = total + jnp.sum(p, axis=0, keepdims=True)
            prob[i, j] = p.astype(BF16)
        inv = 1.0 / total
        inv_tot[i] = inv
        out_t[:, T * i : T * i + T] = dot(vt[...], prob[i].reshape(TP * T, T)) * inv


def join_kernel(o0, o1, o2, att):
    for b in range(TP):
        at = slice(T * b, T * b + T)
        both = jnp.concatenate([o0[:, at], o1[:, at]], axis=0)
        att[at, :] = jnp.transpose(both).astype(BF16)
    for b in range(2):
        both = [o2[:, T * c : T * c + T] for c in (b, b + 2)]
        att[1024 + T * b : 1280 + T * b, :] = jnp.transpose(jnp.concatenate(both, axis=0)).astype(BF16)


def put_pair(keep, give, k, value):
    @pl.when(k % 2 == 0)
    def _():
        keep[k // 2] = value

    @pl.when(k % 2 == 1)
    def _():
        give[k // 2] = value


def units_kernel(p0, p1, p2, p3, p4, p5, p6, p7, wgu, wd):
    dp = lax.axis_index("dp")
    for n, ref in enumerate((p0, p1, p2, p3, p4, p5, p6, p7)):
        at = dp ^ piece_at(n)
        rows = pl.ds(pl.multiple_of(96 * at, 32), 96)
        for m in range(4):
            wgu[rows, 256 * m : 256 * m + 256] = ref[96 * m : 96 * m + 96]
        rows = pl.ds(pl.multiple_of(64 * at, 64), 64)
        for m in range(3):
            wd[rows, 256 * m : 256 * m + 256] = ref[384 + 64 * m : 448 + 64 * m]


def ffn_kernel(
    ks, a0, a1, a2, a3, gains, wop, wgu, wd, tok, c0, c1,
    n2, hid, ggug, keep, give, attc, mixed_own,
):
    j = lax.axis_index("blk")
    low = low_half(T)
    refs = (a0, a1, a2, a3)
    for m, k in enumerate(ks):
        b = j ^ k
        half = b // 2
        for n, ref in enumerate(refs):
            attc[m, :, 128 * n : 128 * n + 128] = ref[pl.ds(pl.multiple_of(b * T, T), T)]
        rest = [
            ref[pl.ds(pl.multiple_of(1024 + (b % 2) * T, T), T)].astype(F32) for ref in refs
        ]
        for n in range(2):
            lo = pltpu.roll(rest[2 * n], 64 * half, 1)
            hi = pltpu.roll(rest[2 * n + 1], 64 * (1 - half), 1)
            attc[m, :, 512 + 128 * n : 640 + 128 * n] = jnp.where(low, lo, hi).astype(BF16)
        mixed = tok[b].astype(F32) + dot(attc[m], wop[...])
        if k == 0:
            mixed_own[...] = mixed
        rstd = lax.rsqrt(jnp.mean(mixed * mixed, axis=-1, keepdims=True) + EPSILON)
        n = (mixed * rstd * gains[1:2]).astype(BF16)
        n2[m] = n
        gate = dot(n, wgu[:, 0:512])
        up = dot(n, wgu[:, 512:1024])
        c = 0.7978845608028654
        sq = gate * gate
        th = jnp.tanh(c * gate * (1.0 + 0.044715 * sq))
        act = 0.5 * gate * (1.0 + th)
        slope = 0.5 * (1.0 + th) + 0.5 * gate * (1.0 - th * th) * (c * (1.0 + 3 * 0.044715 * sq))
        hid[m] = (act * up).astype(BF16)
        hg = dot_nt((c0, c1)[m][...], wd[...])
        ggug[m, :, 0:512] = (hg * up * slope).astype(BF16)
        ggug[m, :, 512:1024] = (hg * act).astype(BF16)
        (keep, give)[m][...] = dot_nt(ggug[m], wgu[...]).astype(BF16)


def mid_kernel(keep, rc, rx, mixed_own, cot, attc, wop, gains, mixed_grad, g0, g1, g2, g3, wo_keep, wo_one, wo_three, dw):
    j = lax.axis_index("blk")
    u = (keep[...].astype(F32) + rc[...].astype(F32) + rx[...].astype(F32)) * gains[1:2]
    mixed = mixed_own[...]
    rstd = lax.rsqrt(jnp.mean(mixed * mixed, axis=-1, keepdims=True) + EPSILON)
    n = mixed * rstd
    mg = cot[...].astype(F32) + rstd * (u - n * jnp.mean(u * n, axis=-1, keepdims=True))
    mixed_grad[...] = mg
    ml = mg.astype(BF16)
    ag = dot_nt(ml, wop[...])
    low = low_half(128)
    for k, ref in enumerate((g0, g1, g2, g3)):
        ref[0:256] = ag[:, 128 * k : 128 * k + 128].astype(BF16)
        rest = ag[:, 512 + 128 * (k // 2) : 640 + 128 * (k // 2)]
        top, bottom = rest[0:128], rest[128:256]
        if k % 2 == 0:
            v = jnp.where(low, top, pltpu.roll(bottom, 64, 1))
        else:
            v = jnp.where(low, pltpu.roll(top, 64, 1), bottom)
        ref[256:384] = v.astype(BF16)
    perm = dot_tn(attc[0], ml)
    for k in range(TP):
        at = pl.multiple_of(192 * (j ^ k), 64)
        dw[pl.ds(at, 128)] = perm[128 * k : 128 * k + 128]
        dw[pl.ds(at + 128, 64)] = perm[512 + 64 * k : 512 + 64 * k + 64]
    for k in range(TP):
        ref = (wo_keep.at[0], wo_one, wo_keep.at[1], wo_three)[k]
        for d in range(8):
            at = pl.multiple_of(24 * (TP * d + (j ^ k)), 8)
            ref[d] = dw[pl.ds(at, 24)].astype(BF16)


SLOTS = (0, 2, 1, 3)
FIRST = 3 * 96
SECOND = 2 * 96 + 6 * 24
TAIL = 16


def slots(body):
    dp = lax.axis_index("dp")
    for give in range(2):
        for slot, z in enumerate(SLOTS):
            body(give, slot, dp ^ (2 * z + give))


def ffn_dw_kernel(
    na, ga, ha, nb, gb, hb, c0, c1, c2, c3, wd, y_keep, y_give, z_keep, z_give, lo_keep, lo_give, dwgu, dwd
):
    for m in range(2):
        at = slice(512 * m, 512 * m + 512)
        dwgu[:, at] = dot_tn(na[...], ga[:, at]) + dot_tn(nb[...], gb[:, at])
    for m in range(3):
        at = slice(256 * m, 256 * m + 256)
        dwd[:, at] = (
            dot_tn(ha[0:T], c2[:, at])
            + dot_tn(ha[T : 2 * T], c3[:, at])
            + dot_tn(hb[0:T], c0[:, at])
            + dot_tn(hb[T : 2 * T], c1[:, at])
        )
    for n, ref in enumerate((hb, ha)):
        lo_keep[n] = dot(ref[0:T], wd[...]).astype(BF16)
        lo_give[n] = dot(ref[T : 2 * T], wd[...]).astype(BF16)

    def put(g, slot, owner):
        ref = y_give if g else y_keep
        a = pl.ds(pl.multiple_of(96 * owner, 32), 96)
        for m in range(3):
            ref[slot, 96 * m : 96 * m + 96] = dwgu[a, 256 * m : 256 * m + 256].astype(BF16)
        ref = z_give if slot > 1 else z_keep
        slot = 2 * (slot % 2) + g
        ref[slot, 0:96] = dwgu[a, 768:1024].astype(BF16)
        a = pl.ds(pl.multiple_of(64 * owner, 64), 64)
        for m in range(3):
            ref[slot, 96 + 64 * m : 160 + 64 * m] = dwd[a, 256 * m : 256 * m + 256].astype(BF16)

    slots(put)


def ffn_second_kernel(y_keep, y_got, z_keep, z_got, y_next, y_give, z_next, z_give):
    for keep, got, rest, give in ((y_keep, y_got, y_next, y_give), (z_keep, z_got, z_next, z_give)):
        rest[...] = (keep[0:2].astype(F32) + got[0:2].astype(F32)).astype(BF16)
        give[...] = (keep[2:4].astype(F32) + got[2:4].astype(F32)).astype(BF16)


def ffn_third_kernel(y_keep, y_got, z_keep, z_got, y_give, z_give):
    y_give[...] = (y_keep[1].astype(F32) + y_got[1].astype(F32)).astype(BF16)
    z_give[...] = (z_keep[1].astype(F32) + z_got[1].astype(F32)).astype(BF16)


def split(x):
    high = x.astype(BF16).astype(F32)
    return jnp.concatenate([high, x - high], axis=0).astype(BF16)


def first_dw_kernel(n1, dqkv, keep, give, dw):
    for t in range(3):
        at = slice(128 * t, 128 * t + 128)
        dw[:, at] = dot_tn(n1[...], dqkv[:, at])

    def put(g, slot, owner):
        ref = give if g else keep
        a = pl.ds(pl.multiple_of(96 * owner, 32), 96)
        for t in range(3):
            at = FIRST * slot + 96 * t
            ref[at : at + 96] = dw[a, 128 * t : 128 * t + 128].astype(BF16)

    slots(put)


def second_dw_kernel(n1, dqkv, wo_keep, wo_got, wo_along, ta, tb, keep, give, dw, wo, chunk):
    for t in range(2):
        at = slice(128 * t, 128 * t + 128)
        dw[:, at] = dot_tn(n1[...], dqkv[:, at])
    for d in range(8):
        wo[d] = wo_keep[0, d].astype(F32) + wo_got[d].astype(F32) + wo_along[d].astype(F32)

    def put(g, slot, owner):
        ref = give if g else keep
        a = pl.ds(pl.multiple_of(96 * owner, 32), 96)
        for t in range(2):
            chunk[96 * t : 96 * t + 96] = dw[a, 128 * t : 128 * t + 128]
        for t in range(6):
            chunk[192 + 24 * t : 216 + 24 * t] = wo[owner, :, 128 * t : 128 * t + 128]
        ref[SECOND * slot : SECOND * slot + SECOND] = chunk[...].astype(BF16)

    slots(put)
    for ref in (keep, give):
        ref[4 * SECOND : 4 * SECOND + 16] = split(ta[...] + tb[...])


def tail_of(ref, base):
    both = ref[base : base + 16].astype(F32)
    return both[0:8] + both[8:16]


def stage_kernel(n, chunk, keep, got, next_keep, next_give):
    half = n // 2 * chunk
    for at, ref in ((0, next_keep), (half, next_give)):
        here = slice(at, at + half)
        ref[0:half] = (keep[here].astype(F32) + got[here].astype(F32)).astype(BF16)
        if chunk == SECOND:
            ref[half : half + 16] = split(tail_of(keep, n * chunk) + tail_of(got, n * chunk))


def back_kernel(ka, ga, kb, gb, yk, yg, ya, zk, zg, za, dwo, dwd, b0, b1, b2, b3, total, ffn):
    j = lax.axis_index("blk")
    ffn[0:288] = yk[0].astype(F32) + yg[0].astype(F32) + ya[...].astype(F32)
    ffn[288:576] = zk[0].astype(F32) + zg[0].astype(F32) + za[...].astype(F32)
    for m in range(3):
        dwd[:, 256 * m : 256 * m + 256] = ffn[384 + 64 * m : 448 + 64 * m]
    total[0:FIRST] = ka[...].astype(F32) + ga[...].astype(F32)
    total[FIRST : FIRST + SECOND] = kb[0:SECOND].astype(F32) + gb[0:SECOND].astype(F32)
    parts = split(tail_of(kb, SECOND) + tail_of(gb, SECOND)).astype(F32)
    parts = jnp.concatenate([parts, jnp.zeros((8, 128), F32)], axis=0).astype(BF16)
    for t in range(6):
        at = 480 + 24 * t
        dwo[:, 128 * t : 128 * t + 128] = total[at : at + 24]
    for k, ref in enumerate((b0, b1, b2, b3)):
        for t in range(5):
            part = total[pl.ds(pl.multiple_of(96 * t + 24 * (j ^ k), 8), 24)]
            ref[:, 128 * t : 128 * t + 128] = part.astype(BF16)
        for m in range(4):
            part = ffn[pl.ds(pl.multiple_of(96 * m + 24 * (j ^ k), 8), 24)]
            ref[:, 640 + 256 * m : 896 + 256 * m] = part.astype(BF16)
        ref[:, 1664:1792] = parts


def attn_bwd_kernel(second, *refs):
    count = 1 if second else 2
    heads = range(HT - 1, HT) if second else range(2)
    qkv, refs = refs[0], refs[1:]
    probs, refs = refs[:count], refs[count:]
    invs, refs = refs[:count], refs[count:]
    outs, refs = refs[:count], refs[count:]
    (g0, g1, g2, g3, dqkv, table_grad,
     dotm, dom, qm, ktm, delta, dst, dq_acc, dk_acc, dv_acc, near, far) = refs
    j_me = lax.axis_index("blk")
    low = low_half(T)
    rows_low = lax.broadcasted_iota(jnp.int32, (128, T), 0) < 64

    for k, ref in enumerate((g0, g1, g2, g3)):
        b = j_me ^ k
        if second:
            rest = ref[256:384].astype(F32)
            rows = jnp.concatenate([rest, pltpu.roll(rest, 64, 1)], axis=0)
            turned = jnp.where(rows_low, jnp.transpose(rows) * invs[0][b], 0.0)
        else:
            turned = jnp.transpose(ref[0:256].astype(F32))
            turned = turned * jnp.where(rows_low, invs[0][b], invs[1][b])
        turned = turned.astype(BF16).astype(F32)
        back = jnp.transpose(turned)
        for n in range(count):
            dotm[n, b] = jnp.where(rows_low == (n == 0), turned, 0.0).astype(BF16)
            dom[n, b] = jnp.where(low == (n == 0), back, 0.0).astype(BF16)

    for i in range(TP):
        at = slice(T * i, T * i + T)
        if second:
            q = pltpu.roll(qkv[3, i].astype(F32), 64, 1)
            keys = jnp.transpose(q)
        else:
            q = qkv[0, i].astype(F32)
            keys = jnp.transpose(qkv[1, i].astype(F32))
        for n in range(count):
            g = dotm[n, i].astype(F32)[64 * n : 64 * n + 64]
            delta[n, i] = jnp.sum(outs[n][:, at] * g, axis=0, keepdims=True)
            qm[n, i] = jnp.where(low == (n == 0 and not second), q, 0.0).astype(BF16)
            ktm[n, :, at] = jnp.where(rows_low == (n == 0), keys, 0.0).astype(BF16)

    dq_acc[...] = jnp.zeros(dq_acc.shape, F32)
    dk_acc[...] = jnp.zeros(dk_acc.shape, F32)
    dv_acc[...] = jnp.zeros(dv_acc.shape, F32)
    table_grad[...] = jnp.zeros(table_grad.shape, F32)
    key_at = lax.broadcasted_iota(jnp.int32, (128, 128), 0)
    query_at = lax.broadcasted_iota(jnp.int32, (128, 128), 1)
    upper = query_at >= key_at
    turn = (key_at + query_at == 127).astype(F32)

    def diagonals(m):
        m = lax.dot_general(
            turn, m, (((1,), (0,)), ((), ())), precision=HIGHEST, preferred_element_type=F32
        )
        return jnp.sum(pltpu.roll(m, 1, 1, stride=1, stride_axis=0), axis=0, keepdims=True)

    row_id = lax.broadcasted_iota(jnp.int32, (NB, 128), 0)
    lane_id = lax.broadcasted_iota(jnp.int32, (NB, 128), 1)
    hot_neg = bucket_of(-lane_id) == row_id
    hot_pos = bucket_of(128 - lane_id) == row_id

    for n, prob in enumerate(probs):
        near[...] = jnp.zeros(near.shape, F32)
        far[...] = jnp.zeros(far.shape, F32)
        for i in range(TP):
            at = slice(T * i, T * i + T)
            row_delta = delta[n, i]
            for j in range(TP):
                dp = dot(qkv[2 + 2 * second, j], dotm[n, i])
                ds = prob[i, j].astype(F32) * (dp - row_delta)
                dst[j] = ds.astype(BF16)
                for a in range(2):
                    for c in range(2):
                        gap = 2 * (j - i) + a - c
                        part = ds[128 * a : 128 * a + 128, 128 * c : 128 * c + 128]
                        if abs(gap) <= 1:
                            near[gap + 1] += part
                        else:
                            far[int(gap > 0)] += jnp.sum(part.reshape(16, 8, 128), axis=0)
            d_all = dst[...].reshape(TP * T, T)
            dq_acc[:, at] += dot(ktm[n], d_all)
            dk_acc[...] += dot(d_all, qm[n, i])
            dv_acc[...] += dot(prob[i].reshape(TP * T, T), dom[n, i])
        before, diagonal, after = near[0], near[1], near[2]
        neg = jnp.where(upper, diagonal, before)
        pos = jnp.where(upper, after, diagonal)
        neg, pos = diagonals(neg), diagonals(pos)
        far_neg = jnp.sum(far[0], axis=0, keepdims=True) + jnp.sum(
            jnp.where(upper, before, 0.0), axis=0, keepdims=True
        )
        far_pos = jnp.sum(far[1], axis=0, keepdims=True) + jnp.sum(
            jnp.where(upper, 0.0, after), axis=0, keepdims=True
        )
        spread = (
            jnp.where(hot_neg, neg, 0.0)
            + jnp.where(hot_pos, pos, 0.0)
            + jnp.where(row_id == 15, far_neg, 0.0)
            + jnp.where(row_id == 31, far_pos, 0.0)
        )
        sums = jnp.sum(spread, axis=1, keepdims=True)
        sums = jnp.sum(jnp.where(lane_id == row_id, sums, 0.0), axis=0, keepdims=True)
        h = heads[n]
        table_grad[h : h + 1] = sums
    for i in range(TP):
        at = slice(T * i, T * i + T)
        dq = jnp.transpose(dq_acc[:, at])
        if second:
            parts = (dq + dk_acc[at], dv_acc[at])
        else:
            parts = (dq, dk_acc[at], dv_acc[at])
        for n, part in enumerate(parts):
            dqkv[i, :, 128 * n : 128 * n + 128] = part.astype(BF16)


def one_grad_kernel(da, db, w, keep, give):
    j = lax.axis_index("blk")

    def body(k, carry):
        total = dot_nt(da[j ^ k], w[:, 0:384]) + dot_nt(db[j ^ k], w[:, 384:640])
        put_pair(keep, give, k, total.astype(BF16))
        return carry

    lax.fori_loop(0, TP, body, 0)


def finish(parts, w, out, gain):
    total = jnp.zeros((w.shape[0], 128), F32)
    for n, part in enumerate(parts):
        at = slice(128 * n, 128 * n + 128)
        total = total + part * w[:, at].astype(F32)
        out[:, at] = part
    return jnp.sum(total, axis=1, keepdims=True) / gain


def put_row(ref, wide):
    rows = wide.shape[0]
    row_id = lax.broadcasted_iota(jnp.int32, (rows, 128), 0)
    eye = row_id == lax.broadcasted_iota(jnp.int32, (rows, 128), 1)
    ref[...] = jnp.sum(jnp.where(eye, wide, 0.0), axis=0, keepdims=True)[:, 0:rows]


def final_kernel(
    b0, b1, b2, b3, gains, wq, wk, wv, wg, wu, dq, dk, dv, dg, du, gg1, gg2, table, src
):
    j_me = lax.axis_index("blk")
    rows = wq.shape[0]
    low = low_half(rows)
    heads = jnp.zeros((128, 128), F32)
    head_id = lax.broadcasted_iota(jnp.int32, (128, 128), 0)
    for k, ref in enumerate((b0, b1, b2, b3)):
        src[j_me ^ k] = ref[:, 0:1664].astype(F32)
        parts = ref[:, 1664:1792].astype(F32)
        for h in range(HT):
            row = parts[h : h + 1] + parts[8 + h : 9 + h]
            heads = jnp.where(head_id == HT * (j_me ^ k) + h, row, heads)
    table[...] = heads[0:H, 0:NB]

    def one(j, n):
        return src[j, 0:rows, 128 * n : 128 * n + 128]

    gain_grad = jnp.zeros((rows, 128), F32)
    for n, (w, out) in enumerate(((wq, dq), (wk, dk), (wv, dv))):
        parts = []
        for j in range(0, TP, 2):
            rest = []
            for m in (j, j + 1):
                last = one(m, 4 if n == 2 else 3)
                rest.append(pltpu.roll(last, 64, 1) if n == 1 else last)
            mid = pltpu.roll(one(j + 1, n), 64, 1)
            parts += [
                one(j, n),
                jnp.where(low, rest[0], mid),
                jnp.where(low, mid, pltpu.roll(rest[1], 64, 1)),
            ]
        gain_grad = gain_grad + finish(parts, w, out, gains[0])
    put_row(gg1, gain_grad)
    gain_grad = jnp.zeros((rows, 128), F32)
    for n, (w, out) in enumerate(((wg, dg), (wu, du))):
        parts = [None] * 16
        for t in range(4):
            at = 5 + 4 * n + t
            for half in range(2):
                a, b = one(2 * half, at), one(2 * half + 1, at)
                parts[4 * t + half] = jnp.where(low, a, pltpu.roll(b, 64, 1))
                parts[4 * t + 2 + half] = jnp.where(low, pltpu.roll(a, 64, 1), b)
        gain_grad = gain_grad + finish(parts, w, out, gains[1])
    put_row(gg2, gain_grad)


def close_kernel(keep, got, along, mixed_grad, tok, gains, tokens_grad):
    x = tok[lax.axis_index("blk")].astype(F32)
    rstd = lax.rsqrt(jnp.mean(x * x, axis=-1, keepdims=True) + EPSILON)
    n = x * rstd
    u = (keep[0].astype(F32) + got[0].astype(F32) + along[...].astype(F32)) * gains[0:1]
    grad = rstd * (u - n * jnp.mean(u * n, axis=-1, keepdims=True))
    tokens_grad[...] = mixed_grad[...] + grad


AXES = ("dp", "blk")
COST = {"qkv": 0, "attn_fwd": (0, 0, 0), "units": 15, "ffn": 0, "ffn_dw": 0, "mid": 20, "attn_bwd": (0, 10), "one_grad": 40, "stage_y": 10, "stage_z": 10}


def group_local(
    n_dp, n_blk,
    tokens, segment_ids, w_query, w_key, w_value, w_attn_out, attn_gain, rel_bias,
    w_gate, w_up, w_down, ffn_gain, cotangent,
):
    n_dev = n_dp * n_blk

    def later(x, *others):
        return lax.optimization_barrier((x,) + others)[0]

    def swap(x, mask):
        return lax.ppermute(x, AXES, [(d, d ^ mask) for d in range(n_dev)])

    def share(x, *others):
        along = swap(x, 2)
        return (x, swap(x, 1), along, swap(later(along, *others), 1))

    def reduce_pair(keep, give):
        got = swap(give, 1)
        return got, swap(keep[1] + got[1], 2)

    def round_one(x):
        return lax.optimization_barrier((swap(x, 16), swap(x, 8), swap(x, 4)))

    def round_two(far, near):
        return lax.optimization_barrier((swap(far, 8), swap(near, 4), swap(far, 4)))

    def gathered(x, one, two, *others):
        far, near, other = one
        last, near_y, far_y = two
        return (x, near, far, last, other, near_y, far_y, swap(later(last, *others), 4))

    tok_own, cot_own = tokens[0], cotangent[0]
    rows, ff = w_query.shape[0], w_gate.shape[1]
    flat = TP * T
    table = rel_bias.astype(F32).T

    *slabs, tok_seg, gain_cols = call(
        prep_kernel,
        (sds((rows, 1664), BF16),) * TP + (sds((T + 16, D), BF16), sds((2, rows, 128), F32)),
        w_query, w_key, w_value, w_gate, w_up, tok_own, segment_ids, attn_gain, ffn_gain,
        name="prep", vmem=60, held=(0, 1, 2, 3, 4, 5),
        scratch=(
            pltpu.VMEM((TP, rows, 1664), BF16),
            *(pltpu.VMEM((rows, D), BF16),) * 3,
            *(pltpu.VMEM((rows, ff), BF16),) * 2,
            pltpu.SemaphoreType.DMA((6,)),
        ),
    )
    toks_x, toks_c = swap(tok_seg, 2), swap(tok_seg, 1)
    slabs = (slabs[0], swap(slabs[1], 1), swap(slabs[2], 2), swap(slabs[3], 3))
    first = call(
        pack_kernel, sds((128, 640), BF16), *slabs, w_attn_out,
        name="pack", vmem=60, held=(4,),
        scratch=(pltpu.VMEM((96, 640), F32), pltpu.VMEM((rows, D), BF16), pltpu.SemaphoreType.DMA),
    )
    second = call(
        pack_more_kernel, sds((576, 256), BF16), *slabs, w_down,
        name="pack_more", vmem=60, held=(4,), after=(first,),
        scratch=(pltpu.VMEM((96, 1024), F32), pltpu.VMEM((64, D), BF16), pltpu.SemaphoreType.DMA),
    )
    first_one = round_one(first)
    bias = call(
        bias_kernel, sds((HT, 3, T, T), F32), table, smem=(0,), name="bias", after=(second,)
    )
    far, near = lax.optimization_barrier(first_one + (second, bias))[:2]
    first_two = round_two(far, near)
    toks_r = swap(later(toks_x, *first_two), 1)
    firsts = gathered(first, first_one, first_two, *())
    toks = (tok_seg, toks_c, toks_x, toks_r)
    cots_x = swap(later(cot_own, *first_one), 2)
    second_one = (
        swap(later(second, *first_one), 16),
        swap(later(second, *first_two), 8),
        swap(later(second, *first_two), 4),
    )

    tok, n1, qkv, w_qkv, gains, segq, segk = call(
        qkv_kernel,
        (
            sds((TP, T, D), BF16), sds((TP, T, D), BF16), sds((5, TP, T, 128), BF16),
            sds((D, 640), BF16), sds((8, D), F32), sds((TP, 8, T), F32), sds((TP, T, T), F32),
        ),
        *toks, *firsts, name="qkv", vmem=16, cost=COST["qkv"],
    )
    stripes = call(
        stripes_kernel, sds((192, D), BF16), *firsts, name="stripes", after=(segq,),
        scratch=(pltpu.VMEM((192, D), F32),),
    )
    stripes = share(stripes)
    wop = call(
        out_weight_kernel, sds((D, D), BF16), *stripes, name="out_weight",
        scratch=(pltpu.VMEM((D, D), F32),),
    )
    heads = []
    for h in range(HT):
        heads.append(
            call(
                functools.partial(attn_fwd_kernel, h),
                (sds((TP, TP, T, T), BF16), sds((TP, 1, T), F32), sds((DH, flat), F32)),
                table, bias, qkv, segq, segk, smem=(0,), name="attn_fwd", vmem=14,
                cost=COST["attn_fwd"][h], after=(heads[-1][1],) if heads else (cots_x,),
                scratch=(
                    pltpu.VMEM((TP, 128, T), BF16),
                    pltpu.VMEM((DH, flat), BF16),
                    pltpu.VMEM((TP, T, T), F32),
                ),
            )
        )
    probs, inv_tots, out_ts = zip(*heads)
    cots = (cot_own, swap(later(cot_own, inv_tots[0]), 1), cots_x, swap(later(cots_x, inv_tots[0]), 1))
    far, near = lax.optimization_barrier(second_one + (inv_tots[0],))[:2]
    second_two = round_two(far, near)
    seconds = gathered(second, second_one, second_two)
    att = call(join_kernel, sds((1536, 128), BF16), *out_ts, name="join")
    atts = share(att, wop)
    wgu, wd = call(
        units_kernel, (sds((D, 1024), BF16), sds((512, D), BF16)), *seconds, name="units",
        cost=COST["units"],
    )

    def ffn(ks, *after):
        return call(
            functools.partial(ffn_kernel, ks),
            (
                sds((2, T, D), BF16), sds((2, T, 512), BF16), sds((2, T, 1024), BF16),
                sds((T, D), BF16), sds((T, D), BF16), sds((2, T, D), BF16), sds((T, D), F32),
            ),
            *atts, gains, wop, wgu, wd, tok, cots[ks[0]], cots[ks[1]], name="ffn", vmem=24,
            cost=COST["ffn"], after=after,
        )

    n2_a, hid_a, ggug_a, keep, give, _, _ = ffn((2, 3))
    two_x = keep + swap(give, 1)
    n2_b, hid_b, ggug_b, two_keep, give, attc, mixed_own = ffn((0, 1), two_x)
    two_x = swap(two_x, 2)
    two_c = swap(give, 1)
    y_keep, y_give, z_keep, z_give, lo_keep, lo_give = call(
        ffn_dw_kernel, (sds((4, 288, 256), BF16),) * 4 + (sds((2, T, D), BF16),) * 2,
        n2_a.reshape(2 * T, D), ggug_a.reshape(2 * T, 1024), hid_a.reshape(2 * T, 512),
        n2_b.reshape(2 * T, D), ggug_b.reshape(2 * T, 1024), hid_b.reshape(2 * T, 512),
        *cots, wd, name="ffn_dw", vmem=20, cost=COST["ffn_dw"],
        scratch=(pltpu.VMEM((D, 1024), F32), pltpu.VMEM((512, D), F32)),
    )
    y_got, z_got = swap(y_give, 4), swap(z_give, 8)
    mixed_grad, g0, g1, g2, g3, wo_keep, *wo_gives = call(
        mid_kernel,
        (sds((T, D), F32),) + (sds((384, 128), BF16),) * 4
        + (sds((2, 8, 24, D), BF16),) + (sds((8, 24, D), BF16),) * 2,
        two_keep, two_c, two_x, mixed_own, cot_own, attc, wop, gains, name="mid", vmem=16,
        after=(y_give,), scratch=(pltpu.VMEM((D, D), F32),), cost=COST["mid"],
    )
    g1, g2, g3 = swap(g1, 1), swap(g2, 2), swap(g3, 3)
    lo_c = swap(later(lo_give, mixed_grad), 1)
    lo_sum = lo_keep[1] + lo_c[1]
    wo_got = (swap(wo_gives[0], 1), swap(wo_gives[1], 1))
    wo_along = swap(later(wo_keep[1] + wo_got[1], g1, g2, g3), 2)

    def attn_bwd(second, *after):
        mine = slice(2, 3) if second else slice(0, 2)
        count = 1 if second else 2
        return call(
            functools.partial(attn_bwd_kernel, second),
            (sds((TP, T, 256 if second else 384), BF16), sds((8, 128), F32)),
            qkv, *probs[mine], *inv_tots[mine], *out_ts[mine], g0, g1, g2, g3,
            name="attn_bwd", vmem=22, cost=COST["attn_bwd"][second], after=after,
            scratch=(
                pltpu.VMEM((count, TP, 128, T), BF16),
                pltpu.VMEM((count, TP, T, 128), BF16),
                pltpu.VMEM((count, TP, T, 128), BF16),
                pltpu.VMEM((count, 128, TP * T), BF16),
                pltpu.VMEM((count, TP, 1, T), F32),
                pltpu.VMEM((TP, T, T), BF16),
                pltpu.VMEM((128, TP * T), F32),
                pltpu.VMEM((TP * T, 128), F32),
                pltpu.VMEM((TP * T, 128), F32),
                pltpu.VMEM((3, 128, 128), F32),
                pltpu.VMEM((2, 8, 128), F32),
            ),
        )

    def chunks(n, chunk):
        return sds((n * chunk + (TAIL if chunk == SECOND else 0), 128), BF16)

    def stage(n, chunk, keep, got, name, *after):
        return call(
            functools.partial(stage_kernel, n, chunk), (chunks(n // 2, chunk),) * 2, keep, got,
            name=name, after=after, cost=COST[name],
        )

    da, ta = attn_bwd(0)
    a_keep, a_give = call(
        first_dw_kernel, (chunks(4, FIRST),) * 2, n1.reshape(flat, D), da.reshape(flat, 384),
        name="first_dw", vmem=12, scratch=(pltpu.VMEM((D, 384), F32),),
    )
    a_got = swap(a_give, 4)
    y_keep, y_give, z_keep, z_give = call(
        ffn_second_kernel, (sds((2, 288, 256), BF16),) * 4, y_keep, y_got, z_keep, z_got,
        name="ffn_second", after=(a_give,),
    )
    y_got, z_got = swap(y_give, 8), swap(z_give, 16)
    db, tb = attn_bwd(1, y_give, *())
    b_keep, b_give = call(
        second_dw_kernel, (chunks(4, SECOND),) * 2,
        n1.reshape(flat, D), db.reshape(flat, 256), wo_keep, wo_got[0], wo_along, ta, tb,
        name="second_dw", vmem=12,
        scratch=(
            pltpu.VMEM((D, 256), F32), pltpu.VMEM((8, 24, D), F32), pltpu.VMEM((SECOND, 128), F32),
        ),
    )
    b_got = swap(b_give, 4)
    one_keep, one_give = call(
        one_grad_kernel, (sds((2, T, D), BF16),) * 2, da, db, w_qkv, name="one_grad", vmem=16,
        after=(b_give,), cost=COST["one_grad"],
    )
    one_c, one_x = reduce_pair(one_keep, one_give)
    a_keep, a_give = stage(4, FIRST, a_keep, a_got, "stage_y", b_give)
    a_got = swap(a_give, 8)
    y_give, z_give = call(
        ffn_third_kernel, (sds((288, 256), BF16),) * 2, y_keep, y_got, z_keep, z_got,
        name="ffn_third", after=(a_give,),
    )
    y_along, z_along = swap(y_give, 16), swap(z_give, 4)
    b_keep, b_give = stage(4, SECOND, b_keep, b_got, "stage_y", *(y_give,))
    b_got = swap(b_give, 8)
    a_keep, a_give = stage(2, FIRST, a_keep, a_got, "stage_z", b_give)
    a_got = swap(a_give, 16)
    b_keep, b_give = stage(2, SECOND, b_keep, b_got, "stage_z", *(a_give,))
    b_got = swap(b_give, 16)
    lo_x = swap(later(lo_sum, one_c), 2)
    layer_out = mixed_own + lo_keep[0].astype(F32) + lo_c[0].astype(F32) + lo_x.astype(F32)
    tokens_grad = call(
        close_kernel, sds((T, D), F32), one_keep, one_c, one_x, mixed_grad, tok, gains,
        name="close", vmem=10, after=(a_got,),
    )
    dwo, dwd, *backs = call(
        back_kernel,
        (sds((rows, D), F32), sds((64, D), F32)) + (sds((rows, 1792), BF16),) * 4,
        a_keep, a_got, b_keep, b_got, y_keep, y_got, y_along, z_keep, z_got, z_along,
        name="back", after=(tokens_grad,),
        scratch=(pltpu.VMEM((FIRST + SECOND, 128), F32), pltpu.VMEM((576, 256), F32)),
    )
    backs = (backs[0], swap(backs[1], 1), swap(backs[2], 2), swap(backs[3], 3))
    dq, dk, dv, dg, du, gg1, gg2, table_sum = call(
        final_kernel,
        (sds((rows, D), F32),) * 3
        + (sds((rows, ff), F32),) * 2
        + (sds((1, rows), F32), sds((1, rows), F32), sds((H, NB), F32)),
        *backs, gain_cols, w_query, w_key, w_value, w_gate, w_up, name="final",
        scratch=(pltpu.VMEM((TP, rows, 1664), F32),),
    )

    return (
        layer_out.astype(BF16)[None],
        tokens_grad[None],
        dq,
        dk,
        dv,
        dwo,
        gg1[0],
        table_sum.T,
        dg,
        du,
        dwd,
        gg2[0],
    )


KEY_BLOCK = 256
HIGHEST = lax.Precision.HIGHEST


def rms_norm(values, gain):
    return values * lax.rsqrt(jnp.mean(values * values, axis=-1, keepdims=True) + EPSILON) * gain


def split_heads(flat_rows):
    return flat_rows.reshape(flat_rows.shape[0], flat_rows.shape[1], H, DH)


def join_heads(per_head):
    return per_head.reshape(per_head.shape[0], per_head.shape[1], H * DH)


def project(left, matrix):
    return jnp.einsum("rtd,de->rte", left, matrix, preferred_element_type=jnp.float32)


def project_back(left, matrix):
    return jnp.einsum("rte,de->rtd", left, matrix, preferred_element_type=jnp.float32)


def weight_grad(left, right):
    return jnp.einsum("rtd,rte->de", left, right, preferred_element_type=jnp.float32)


def block_scores(queries, key_block, query_pos, key_pos, query_seg, key_seg, bias_table):
    raw_scores = jnp.einsum(
        "rqhd,rkhd->rhqk", queries, key_block, preferred_element_type=jnp.float32
    )
    buckets = bucket_of(key_pos[None, :] - query_pos[:, None])
    one_hot = (buckets[:, :, None] == jnp.arange(NB, dtype=jnp.int32)[None, None, :]).astype(
        jnp.float32
    )
    rel_term = jnp.einsum("qkb,bh->hqk", one_hot, bias_table, precision=HIGHEST)
    allowed = (query_seg[:, :, None] == key_seg[:, None, :])[:, None]
    return (raw_scores + rel_term[None], allowed, one_hot)


def absorb(
    running, queries, key_block, value_block, query_pos, key_pos, query_seg, key_seg, bias_table
):
    row_peak, row_total, weighted = running
    scores, allowed, unused = block_scores(
        queries, key_block, query_pos, key_pos, query_seg, key_seg, bias_table
    )
    block_peak = jnp.max(jnp.where(allowed, scores, MASKED), axis=-1)
    new_peak = jnp.maximum(row_peak, block_peak)
    weights = jnp.where(allowed, jnp.exp(scores - new_peak[..., None]), 0.0)
    factor = jnp.exp(row_peak - new_peak)
    row_total = row_total * factor + jnp.sum(weights, axis=-1)
    weighted = weighted * factor[..., None] + jnp.einsum(
        "rhqk,rkhd->rhqd",
        weights.astype(jnp.bfloat16),
        value_block,
        preferred_element_type=jnp.float32,
    )
    return (new_peak, row_total, weighted)


def pair_grads(
    queries,
    out_grad,
    log_total,
    row_delta,
    key_block,
    value_block,
    query_pos,
    key_pos,
    query_seg,
    key_seg,
    bias_table,
):
    scores, allowed, one_hot = block_scores(
        queries, key_block, query_pos, key_pos, query_seg, key_seg, bias_table
    )
    prob_map = jnp.where(allowed, jnp.exp(scores - log_total[..., None]), 0.0)
    prob_grad = jnp.einsum(
        "rqhd,rkhd->rhqk", out_grad, value_block, preferred_element_type=jnp.float32
    )
    score_grad = prob_map * (prob_grad - row_delta[..., None])
    score_low = score_grad.astype(jnp.bfloat16)
    query_grad = jnp.einsum(
        "rhqk,rkhd->rqhd", score_low, key_block, preferred_element_type=jnp.float32
    )
    key_grad = jnp.einsum("rhqk,rqhd->rkhd", score_low, queries, preferred_element_type=jnp.float32)
    value_grad = jnp.einsum(
        "rhqk,rqhd->rkhd",
        prob_map.astype(jnp.bfloat16),
        out_grad,
        preferred_element_type=jnp.float32,
    )
    table_grad = jnp.einsum("rhqk,qkb->bh", score_grad, one_hot, precision=HIGHEST)
    return (query_grad, key_grad, value_grad, table_grad)


def in_blocks(step_fn, running, pieces):
    length = pieces[0].shape[1]
    block_size = math.gcd(length, KEY_BLOCK)
    block_count = length // block_size
    stacked = tuple(
        (
            jnp.moveaxis(
                member.reshape((member.shape[0], block_count, block_size) + member.shape[2:]), 1, 0
            )
            for member in pieces
        )
    )
    starts = block_size * jnp.arange(block_count, dtype=jnp.int32)

    def scan_step(inner_state, item_pair):
        return (step_fn(inner_state, item_pair[0], item_pair[1]), None)

    running, unused = lax.scan(scan_step, running, (stacked, starts))
    return running


def local(
    tokens,
    segment_ids,
    w_query,
    w_key,
    w_value,
    w_attn_out,
    attn_gain,
    rel_bias,
    w_gate,
    w_up,
    w_down,
    ffn_gain,
    cotangent,
):
    row_count, local_len, unused_dim = tokens.shape
    my_block = lax.axis_index("blk")
    full_query, full_key, full_value, full_out, gain_one = (
        lax.all_gather(w_query, ("dp", "blk"), axis=0, tiled=True),
        lax.all_gather(w_key, ("dp", "blk"), axis=0, tiled=True),
        lax.all_gather(w_value, ("dp", "blk"), axis=0, tiled=True),
        lax.all_gather(w_attn_out, ("dp", "blk"), axis=0, tiled=True),
        lax.all_gather(attn_gain, ("dp", "blk"), axis=0, tiled=True),
    )
    full_gate, full_up, full_down, gain_two = (
        lax.all_gather(w_gate, ("dp", "blk"), axis=0, tiled=True),
        lax.all_gather(w_up, ("dp", "blk"), axis=0, tiled=True),
        lax.all_gather(w_down, ("dp", "blk"), axis=0, tiled=True),
        lax.all_gather(ffn_gain, ("dp", "blk"), axis=0, tiled=True),
    )
    row_segs = lax.all_gather(segment_ids, "blk", axis=1, tiled=True)
    bias_table = rel_bias.astype(jnp.float32)
    gain_one_f = gain_one.astype(jnp.float32)
    gain_two_f = gain_two.astype(jnp.float32)
    inputs = tokens.astype(jnp.float32)
    query_pos = my_block * local_len + jnp.arange(local_len, dtype=jnp.int32)
    normed_one = rms_norm(inputs, gain_one_f).astype(jnp.bfloat16)
    query_flat = project(normed_one, full_query).astype(jnp.bfloat16)
    key_flat = project(normed_one, full_key).astype(jnp.bfloat16)
    value_flat = project(normed_one, full_value).astype(jnp.bfloat16)
    queries = split_heads(query_flat)
    key_heads = split_heads(key_flat)
    value_heads = split_heads(value_flat)

    def forward_piece(running, pieces):

        def step_fn(inner_state, blocks, block_start):
            block_len = blocks[0].shape[1]
            key_pos = block_start + jnp.arange(block_len, dtype=jnp.int32)
            key_seg = lax.dynamic_slice_in_dim(row_segs, block_start, block_len, 1)
            return absorb(
                inner_state,
                queries,
                split_heads(blocks[0]),
                split_heads(blocks[1]),
                query_pos,
                key_pos,
                segment_ids,
                key_seg,
                bias_table,
            )

        return in_blocks(step_fn, running, pieces)

    stat_shape = (row_count, H, local_len)
    start_state = (
        jnp.full(stat_shape, MASKED, jnp.float32),
        jnp.zeros(stat_shape, jnp.float32),
        jnp.zeros(stat_shape + (DH,), jnp.float32),
    )
    row_peak, row_total, weighted = forward_piece(
        start_state,
        (
            lax.all_gather(key_flat, "blk", axis=1, tiled=True),
            lax.all_gather(value_flat, "blk", axis=1, tiled=True),
        ),
    )
    log_total = row_peak + jnp.log(row_total)
    attended_f = jnp.transpose(weighted / row_total[..., None], (0, 2, 1, 3))
    attended = join_heads(attended_f).astype(jnp.bfloat16)
    mixed_in = inputs + project(attended, full_out)
    normed_two = rms_norm(mixed_in, gain_two_f).astype(jnp.bfloat16)
    gate_act = project(normed_two, full_gate)
    up_act = project(normed_two, full_up)

    def gated(gate_in, up_in):
        return jax.nn.gelu(gate_in, approximate=True) * up_in

    hidden_f, gated_back = jax.vjp(gated, gate_act, up_act)
    hidden = hidden_f.astype(jnp.bfloat16)
    layer_out = (mixed_in + project(hidden, full_down)).astype(jnp.bfloat16)
    down_grad = weight_grad(hidden, cotangent)
    hidden_grad = project_back(cotangent, full_down)
    gate_grad, up_grad = gated_back(hidden_grad)
    gate_low = gate_grad.astype(jnp.bfloat16)
    up_low = up_grad.astype(jnp.bfloat16)
    gate_w_grad = weight_grad(normed_two, gate_low)
    up_w_grad = weight_grad(normed_two, up_low)
    two_grad = project_back(gate_low, full_gate) + project_back(up_low, full_up)
    unused_two, norm_two_back = jax.vjp(rms_norm, mixed_in, gain_two_f)
    mixed_part, gain_two_grad = norm_two_back(two_grad)
    mixed_grad = cotangent.astype(jnp.float32) + mixed_part
    mixed_low = mixed_grad.astype(jnp.bfloat16)
    out_w_grad = weight_grad(attended, mixed_low)
    attended_grad = project_back(mixed_low, full_out).astype(jnp.bfloat16)
    grad_heads = split_heads(attended_grad)
    row_delta = jnp.sum(
        jnp.transpose(grad_heads.astype(jnp.float32), (0, 2, 1, 3))
        * (weighted / row_total[..., None]),
        axis=-1,
    )
    zero_heads = jnp.zeros(queries.shape, jnp.float32)
    zero_table = jnp.zeros((NB, H), jnp.float32)

    def query_piece(running, pieces):

        def step_fn(inner_state, blocks, block_start):
            block_len = blocks[0].shape[1]
            key_pos = block_start + jnp.arange(block_len, dtype=jnp.int32)
            key_seg = lax.dynamic_slice_in_dim(row_segs, block_start, block_len, 1)
            pair_parts = pair_grads(
                queries,
                grad_heads,
                log_total,
                row_delta,
                split_heads(blocks[0]),
                split_heads(blocks[1]),
                query_pos,
                key_pos,
                segment_ids,
                key_seg,
                bias_table,
            )
            return inner_state + pair_parts[0]

        return in_blocks(step_fn, running, pieces)

    query_grad = join_heads(
        query_piece(
            zero_heads,
            (
                lax.all_gather(key_flat, "blk", axis=1, tiled=True),
                lax.all_gather(value_flat, "blk", axis=1, tiled=True),
            ),
        )
    )
    log_rows, delta_rows = (
        lax.all_gather(log_total, "blk", axis=2, tiled=True),
        lax.all_gather(row_delta, "blk", axis=2, tiled=True),
    )

    def key_piece(running, pieces):

        def step_fn(inner_state, blocks, block_start):
            block_len = blocks[0].shape[1]
            piece_pos = block_start + jnp.arange(block_len, dtype=jnp.int32)
            piece_seg = lax.dynamic_slice_in_dim(row_segs, block_start, block_len, 1)
            piece_log = lax.dynamic_slice_in_dim(log_rows, block_start, block_len, 2)
            piece_delta = lax.dynamic_slice_in_dim(delta_rows, block_start, block_len, 2)
            pair_parts = pair_grads(
                split_heads(blocks[0]),
                split_heads(blocks[1]),
                piece_log,
                piece_delta,
                key_heads,
                value_heads,
                piece_pos,
                query_pos,
                piece_seg,
                segment_ids,
                bias_table,
            )
            return (
                inner_state[0] + pair_parts[1],
                inner_state[1] + pair_parts[2],
                inner_state[2] + pair_parts[3],
            )

        return in_blocks(step_fn, running, pieces)

    key_grad, value_grad, table_grad = key_piece(
        (zero_heads, zero_heads, zero_table),
        (
            lax.all_gather(query_flat, "blk", axis=1, tiled=True),
            lax.all_gather(attended_grad, "blk", axis=1, tiled=True),
        ),
    )
    query_low = query_grad.astype(jnp.bfloat16)
    key_low = join_heads(key_grad).astype(jnp.bfloat16)
    value_low = join_heads(value_grad).astype(jnp.bfloat16)
    query_w_grad = weight_grad(normed_one, query_low)
    key_w_grad = weight_grad(normed_one, key_low)
    value_w_grad = weight_grad(normed_one, value_low)
    one_grad = (
        project_back(query_low, full_query)
        + project_back(key_low, full_key)
        + project_back(value_low, full_value)
    )
    unused_one, norm_one_back = jax.vjp(rms_norm, inputs, gain_one_f)
    input_part, gain_one_grad = norm_one_back(one_grad)
    tokens_grad = mixed_grad + input_part
    table_sum = lax.psum(table_grad, ("dp", "blk"))
    all_sums = (
        lax.psum_scatter(query_w_grad, ("dp", "blk"), scatter_dimension=0, tiled=True),
        lax.psum_scatter(key_w_grad, ("dp", "blk"), scatter_dimension=0, tiled=True),
        lax.psum_scatter(value_w_grad, ("dp", "blk"), scatter_dimension=0, tiled=True),
        lax.psum_scatter(out_w_grad, ("dp", "blk"), scatter_dimension=0, tiled=True),
        lax.psum_scatter(gain_one_grad, ("dp", "blk"), scatter_dimension=0, tiled=True),
        lax.psum_scatter(gate_w_grad, ("dp", "blk"), scatter_dimension=0, tiled=True),
        lax.psum_scatter(up_w_grad, ("dp", "blk"), scatter_dimension=0, tiled=True),
        lax.psum_scatter(down_grad, ("dp", "blk"), scatter_dimension=0, tiled=True),
        lax.psum_scatter(gain_two_grad, ("dp", "blk"), scatter_dimension=0, tiled=True),
    )
    return (
        layer_out,
        tokens_grad,
        all_sums[0],
        all_sums[1],
        all_sums[2],
        all_sums[3],
        all_sums[4],
        table_sum,
        all_sums[5],
        all_sums[6],
        all_sums[7],
        all_sums[8],
    )


def solution(mesh):
    whole = P(AXES, None)
    rows = P("dp", "blk", None)
    n_dp, n_blk = mesh.shape["dp"], mesh.shape["blk"]
    grouped = functools.partial(group_local, n_dp, n_blk)
    body = grouped if (n_dp, n_blk) == (8, TP) else local
    return jax.shard_map(
        body,
        mesh=mesh,
        in_specs=(
            rows, P("dp", "blk"), whole, whole, whole, whole, P(AXES), P(),
            whole, whole, whole, P(AXES), rows,
        ),
        out_specs=(
            rows, rows, whole, whole, whole, whole, P(AXES), P(), whole, whole, whole, P(AXES),
        ),
        check_vma=False,
    )
```

```python
import functools
import math

import jax
import jax.numpy as jnp
from jax import lax
from jax.experimental import pallas as pl
from jax.experimental.pallas import tpu as pltpu
from jax.sharding import PartitionSpec as P

D = 768
H = 12
DH = 64
NB = 32
THRESHOLDS = (12, 16, 23, 32, 46, 64, 91)
MASKED = -1e30
EPSILON = 1e-06
TP = 4
T = 256
HT = 3
F32 = jnp.float32
BF16 = jnp.bfloat16
MIB = 1 << 20


def dot(a, b):
    return lax.dot_general(a, b, (((1,), (0,)), ((), ())), preferred_element_type=F32)


def dot_nt(a, b):
    return lax.dot_general(a, b, (((1,), (1,)), ((), ())), preferred_element_type=F32)


def dot_tn(a, b):
    return lax.dot_general(a, b, (((0,), (0,)), ((), ())), preferred_element_type=F32)


def bucket_of(relative):
    distance = jnp.abs(relative)
    far = jnp.full(relative.shape, 8, jnp.int32)
    for threshold in THRESHOLDS:
        far = far + (distance >= threshold).astype(jnp.int32)
    return jnp.where(relative > 0, NB // 2, 0) + jnp.where(distance < 8, distance, far)


def call(
    kernel, out_shape, *args, scratch=(), smem=(), held=(), after=(), vmem=8, cost=0, name=None
):
    vspec = pl.BlockSpec(memory_space=pltpu.VMEM)
    sspec = pl.BlockSpec(memory_space=pltpu.SMEM)
    aspec = pl.BlockSpec(memory_space=pl.ANY)
    hspec = pl.BlockSpec(memory_space=pltpu.HBM)
    skip = len(after)

    def body(*refs):
        kernel(*refs[skip:])

    specs = [sspec if n in smem else hspec if n in held else vspec for n in range(len(args))]
    return pl.pallas_call(
        body,
        out_shape=out_shape,
        in_specs=[aspec] * skip + specs,
        out_specs=jax.tree.map(lambda _: vspec, out_shape),
        scratch_shapes=list(scratch),
        compiler_params=pltpu.CompilerParams(vmem_limit_bytes=vmem * MIB),
        cost_estimate=pl.CostEstimate(flops=cost * 1_150_000_000, bytes_accessed=0, transcendentals=0),
        name=name,
    )(*after, *args)


def sds(shape, dtype):
    return jax.ShapeDtypeStruct(shape, dtype)


def low_half(rows):
    return lax.broadcasted_iota(jnp.int32, (rows, 128), 1) < 64


def prep_kernel(
    wq, wk, wv, wg, wu, tok, seg, g1, g2, s0, s1, s2, s3, ts, gains, slabs, vq, vk, vv, vg, vu, sems
):
    j_me = lax.axis_index("blk")
    rows = wq.shape[0]
    pairs = ((wq, vq), (wk, vk), (wv, vv), (wg, vg), (wu, vu), (tok, ts.at[0:T]))
    copies = [pltpu.make_async_copy(a, b, sems.at[n]) for n, (a, b) in enumerate(pairs)]
    for copy in copies:
        copy.start()
    eye = lax.broadcasted_iota(jnp.int32, (rows, rows), 0) == lax.broadcasted_iota(
        jnp.int32, (rows, rows), 1
    )
    columns = []
    for n, ref in enumerate((g1, g2)):
        row = jnp.broadcast_to(ref[...].astype(F32).reshape(1, rows), (rows, rows))
        column = jnp.sum(jnp.where(eye, row, 0.0), axis=1, keepdims=True)
        columns.append(column)
        gains[n] = jnp.broadcast_to(column, (rows, 128))
    ids = jnp.broadcast_to(seg[...], (16, T))
    ts[T : T + 16, 0:T] = (ids // 2).astype(F32).astype(BF16)
    ts[T : T + 16, T : 2 * T] = (ids % 2).astype(F32).astype(BF16)
    ts[T : T + 16, 2 * T : 3 * T] = jnp.zeros((16, T), BF16)
    low = low_half(rows)
    lane = lax.broadcasted_iota(jnp.int32, (rows, 128), 1)
    spare = jnp.where(lane == 64, columns[0], jnp.where(lane == 65, columns[1], 0.0))
    for copy in copies:
        copy.wait()

    def tile(ref, index):
        return ref[:, 128 * index : 128 * index + 128].astype(F32)

    for j in range(TP):
        first, second = [], []
        for ref in (vq, vk, vv):
            at = 192 * j // 128
            a, b = tile(ref, at), tile(ref, at + 1)
            if j % 2:
                a, b = pltpu.roll(a, 64, 1), pltpu.roll(b, 64, 1)
                a = jnp.where(low, a, b)
            first.append(a)
            second.append(b)
        tiles = first + [
            jnp.where(low, second[0], pltpu.roll(second[1], 64, 1)),
            jnp.where(low, second[2], spare),
        ]
        for ref in (vg, vu):
            for t in range(4):
                a = tile(ref, 4 * t + j // 2)
                b = tile(ref, 4 * t + 2 + j // 2)
                if j % 2:
                    tiles.append(jnp.where(low, pltpu.roll(a, 64, 1), b))
                else:
                    tiles.append(jnp.where(low, a, pltpu.roll(b, 64, 1)))
        for n, v in enumerate(tiles):
            slabs[j ^ j_me, :, 128 * n : 128 * n + 128] = v.astype(BF16)
    for k, ref in enumerate((s0, s1, s2, s3)):
        ref[...] = slabs[k]


def pack_kernel(s0, s1, s2, s3, wo, first, whole, vo, sem):
    j = lax.axis_index("blk")
    rows = s0.shape[0]
    copy = pltpu.make_async_copy(wo, vo, sem)
    copy.start()
    for k, ref in enumerate((s0, s1, s2, s3)):
        whole[pl.ds(pl.multiple_of(rows * (j ^ k), 8), rows)] = ref[:, 0:640].astype(F32)
    first[0:96] = whole[...].astype(BF16)
    copy.wait()
    out = vo[...].astype(F32)
    rest = [out[8 * n : 8 * n + 8, 640:768] for n in range(3)]
    rest = jnp.concatenate(rest + [jnp.zeros((8, 256), F32)], axis=1)
    first[96:128] = jnp.concatenate([out[:, 0:640], rest], axis=0).astype(BF16)


def pack_more_kernel(s0, s1, s2, s3, wd, second, whole, vd, sem):
    j = lax.axis_index("blk")
    rows = s0.shape[0]
    copy = pltpu.make_async_copy(wd, vd, sem)
    copy.start()
    for k, ref in enumerate((s0, s1, s2, s3)):
        whole[pl.ds(pl.multiple_of(rows * (j ^ k), 8), rows)] = ref[:, 640:1664].astype(F32)
    for n in range(4):
        second[96 * n : 96 * n + 96] = whole[:, 256 * n : 256 * n + 256].astype(BF16)
    copy.wait()
    for n in range(3):
        second[384 + 64 * n : 448 + 64 * n] = vd[:, 256 * n : 256 * n + 256]


def stripes_kernel(p0, p1, p2, p3, p4, p5, p6, p7, out, whole):
    dp = lax.axis_index("dp")
    for n, ref in enumerate((p0, p1, p2, p3, p4, p5, p6, p7)):
        at = pl.ds(pl.multiple_of(24 * (dp ^ piece_at(n)), 8), 24)
        part = ref[96:128].astype(F32)
        whole[at, 0:640] = part[0:24]
        rest = [part[24:32, 128 * m : 128 * m + 128] for m in range(3)]
        whole[at, 640:768] = jnp.concatenate(rest, axis=0)
    out[...] = whole[...].astype(BF16)


def out_weight_kernel(p0, p1, p2, p3, out, whole):
    j = lax.axis_index("blk")
    for k, ref in enumerate((p0, p1, p2, p3)):
        rows = ref[...].astype(F32)
        for d in range(8):
            at = pl.multiple_of(24 * (TP * d + (j ^ k)), 8)
            whole[pl.ds(at, 24)] = rows[24 * d : 24 * d + 24]
    for k in range(TP):
        at = pl.multiple_of(192 * (j ^ k), 64)
        out[128 * k : 128 * k + 128] = whole[pl.ds(at, 128)].astype(BF16)
        out[512 + 64 * k : 576 + 64 * k] = whole[pl.ds(at + 128, 64)].astype(BF16)


def bias_kernel(table, out):
    j = lax.axis_index("blk")
    lane = lax.broadcasted_iota(jnp.int32, (8, 512), 1)
    for n in range(3):
        off = (n - 1) * T
        rel = jnp.where(lane < 256, off - lane, off + 512 - lane)
        bucket = bucket_of(rel)
        for h in range(HT):
            row = jnp.zeros((8, 512), F32)
            for b in range(NB):
                row = jnp.where(bucket == b, table[HT * j + h, b], row)
            wide = jnp.broadcast_to(row[0:1], (T, 512))
            out[h, n] = pltpu.roll(wide, 0, 1, stride=1, stride_axis=0)[:, :T]


def piece_at(n):
    return 2 * (n % 4) + n // 4


def qkv_kernel(
    t0, t1, t2, t3, p0, p1, p2, p3, p4, p5, p6, p7, tok, n1, qkv, w, gains, segq, segk
):
    j = lax.axis_index("blk")
    dp = lax.axis_index("dp")
    for k, ref in enumerate((t0, t1, t2, t3)):
        tok[j ^ k] = ref[0:T]
        parts = ref[T : T + 16].astype(F32)
        row = (2.0 * parts[:, 0:T] + parts[:, T : 2 * T])[0:8]
        segq[j ^ k] = row
        col = jnp.transpose(jnp.broadcast_to(row[0:1], (128, T)))
        segk[j ^ k, :, 0:128] = col
        segk[j ^ k, :, 128:256] = col
    for n, ref in enumerate((p0, p1, p2, p3, p4, p5, p6, p7)):
        w[pl.ds(pl.multiple_of(96 * (dp ^ piece_at(n)), 32), 96)] = ref[0:96]
    turned = jnp.transpose(w[:, 512:640].astype(F32))
    gains[...] = turned[64:72]

    def body(b, carry):
        x = tok[b].astype(F32)
        rstd = lax.rsqrt(jnp.mean(x * x, axis=-1, keepdims=True) + EPSILON)
        n = (x * rstd * gains[0:1]).astype(BF16)
        n1[b] = n
        y = dot(n, w[...])
        for t in range(5):
            qkv[t, b] = y[:, 128 * t : 128 * t + 128].astype(BF16)
        return carry

    lax.fori_loop(0, TP, body, 0)


def attn_fwd_kernel(h, table, bias, qkv, segq, segk, prob, inv_tot, out_t, qt, vt, sc):
    j_me = lax.axis_index("blk")
    rows_low = lax.broadcasted_iota(jnp.int32, (128, T), 0) < 64
    half = slice(64, 128) if h == 1 else slice(0, 64)
    for i in range(TP):
        if h < 2:
            q = jnp.transpose(qkv[0, i].astype(F32))
        else:
            q = jnp.transpose(pltpu.roll(qkv[3, i].astype(F32), 64, 1))
        qt[i] = jnp.where(rows_low == (h == 0), q, 0.0).astype(BF16)
        v = jnp.transpose(qkv[2 + 2 * (h // 2), i].astype(F32)).astype(BF16)
        vt[:, T * i : T * i + T] = v[half]

    tile = 1 + 2 * (h // 2)
    far = (table[HT * j_me + h, 15], table[HT * j_me + h, 31])
    for i in range(TP):
        peak = jnp.full((1, T), MASKED, F32)
        for j in range(TP):
            s = dot(qkv[tile, j], qt[i])
            if abs(j - i) <= 1:
                s = s + bias[h, j - i + 1]
            else:
                s = s + far[j > i]
            if i in (0, TP - 1) or j in (0, TP - 1):
                s = jnp.where(segk[j] == segq[i, 0:1], s, MASKED)
            sc[j] = s
            peak = jnp.maximum(peak, jnp.max(s, axis=0, keepdims=True))
        total = jnp.zeros((1, T), F32)
        for j in range(TP):
            p = jnp.exp(sc[j] - peak)
            total = total + jnp.sum(p, axis=0, keepdims=True)
            prob[i, j] = p.astype(BF16)
        inv = 1.0 / total
        inv_tot[i] = inv
        out_t[:, T * i : T * i + T] = dot(vt[...], prob[i].reshape(TP * T, T)) * inv


def join_kernel(o0, o1, o2, att):
    for b in range(TP):
        at = slice(T * b, T * b + T)
        both = jnp.concatenate([o0[:, at], o1[:, at]], axis=0)
        att[at, :] = jnp.transpose(both).astype(BF16)
    for b in range(2):
        both = [o2[:, T * c : T * c + T] for c in (b, b + 2)]
        att[1024 + T * b : 1280 + T * b, :] = jnp.transpose(jnp.concatenate(both, axis=0)).astype(BF16)


def put_pair(keep, give, k, value):
    @pl.when(k % 2 == 0)
    def _():
        keep[k // 2] = value

    @pl.when(k % 2 == 1)
    def _():
        give[k // 2] = value


def units_kernel(p0, p1, p2, p3, p4, p5, p6, p7, wgu, wd):
    dp = lax.axis_index("dp")
    for n, ref in enumerate((p0, p1, p2, p3, p4, p5, p6, p7)):
        at = dp ^ piece_at(n)
        rows = pl.ds(pl.multiple_of(96 * at, 32), 96)
        for m in range(4):
            wgu[rows, 256 * m : 256 * m + 256] = ref[96 * m : 96 * m + 96]
        rows = pl.ds(pl.multiple_of(64 * at, 64), 64)
        for m in range(3):
            wd[rows, 256 * m : 256 * m + 256] = ref[384 + 64 * m : 448 + 64 * m]


def ffn_kernel(
    ks, a0, a1, a2, a3, gains, wop, wgu, wd, tok, c0, c1,
    n2, hid, ggug, keep, give, attc, mixed_own,
):
    j = lax.axis_index("blk")
    low = low_half(T)
    refs = (a0, a1, a2, a3)
    for m, k in enumerate(ks):
        b = j ^ k
        half = b // 2
        for n, ref in enumerate(refs):
            attc[m, :, 128 * n : 128 * n + 128] = ref[pl.ds(pl.multiple_of(b * T, T), T)]
        rest = [
            ref[pl.ds(pl.multiple_of(1024 + (b % 2) * T, T), T)].astype(F32) for ref in refs
        ]
        for n in range(2):
            lo = pltpu.roll(rest[2 * n], 64 * half, 1)
            hi = pltpu.roll(rest[2 * n + 1], 64 * (1 - half), 1)
            attc[m, :, 512 + 128 * n : 640 + 128 * n] = jnp.where(low, lo, hi).astype(BF16)
        mixed = tok[b].astype(F32) + dot(attc[m], wop[...])
        if k == 0:
            mixed_own[...] = mixed
        rstd = lax.rsqrt(jnp.mean(mixed * mixed, axis=-1, keepdims=True) + EPSILON)
        n = (mixed * rstd * gains[1:2]).astype(BF16)
        n2[m] = n
        gate = dot(n, wgu[:, 0:512])
        up = dot(n, wgu[:, 512:1024])
        c = 0.7978845608028654
        sq = gate * gate
        th = jnp.tanh(c * gate * (1.0 + 0.044715 * sq))
        act = 0.5 * gate * (1.0 + th)
        slope = 0.5 * (1.0 + th) + 0.5 * gate * (1.0 - th * th) * (c * (1.0 + 3 * 0.044715 * sq))
        hid[m] = (act * up).astype(BF16)
        hg = dot_nt((c0, c1)[m][...], wd[...])
        ggug[m, :, 0:512] = (hg * up * slope).astype(BF16)
        ggug[m, :, 512:1024] = (hg * act).astype(BF16)
        (keep, give)[m][...] = dot_nt(ggug[m], wgu[...]).astype(BF16)


def mid_kernel(keep, rc, rx, mixed_own, cot, attc, wop, gains, mixed_grad, g0, g1, g2, g3, wo_keep, wo_one, wo_three, dw):
    j = lax.axis_index("blk")
    u = (keep[...].astype(F32) + rc[...].astype(F32) + rx[...].astype(F32)) * gains[1:2]
    mixed = mixed_own[...]
    rstd = lax.rsqrt(jnp.mean(mixed * mixed, axis=-1, keepdims=True) + EPSILON)
    n = mixed * rstd
    mg = cot[...].astype(F32) + rstd * (u - n * jnp.mean(u * n, axis=-1, keepdims=True))
    mixed_grad[...] = mg
    ml = mg.astype(BF16)
    ag = dot_nt(ml, wop[...])
    low = low_half(128)
    for k, ref in enumerate((g0, g1, g2, g3)):
        ref[0:256] = ag[:, 128 * k : 128 * k + 128].astype(BF16)
        rest = ag[:, 512 + 128 * (k // 2) : 640 + 128 * (k // 2)]
        top, bottom = rest[0:128], rest[128:256]
        if k % 2 == 0:
            v = jnp.where(low, top, pltpu.roll(bottom, 64, 1))
        else:
            v = jnp.where(low, pltpu.roll(top, 64, 1), bottom)
        ref[256:384] = v.astype(BF16)
    perm = dot_tn(attc[0], ml)
    for k in range(TP):
        at = pl.multiple_of(192 * (j ^ k), 64)
        dw[pl.ds(at, 128)] = perm[128 * k : 128 * k + 128]
        dw[pl.ds(at + 128, 64)] = perm[512 + 64 * k : 512 + 64 * k + 64]
    for k in range(TP):
        ref = (wo_keep.at[0], wo_one, wo_keep.at[1], wo_three)[k]
        for d in range(8):
            at = pl.multiple_of(24 * (TP * d + (j ^ k)), 8)
            ref[d] = dw[pl.ds(at, 24)].astype(BF16)


SLOTS = (0, 2, 1, 3)
FIRST = 3 * 96
SECOND = 2 * 96 + 6 * 24
TAIL = 16


def slots(body):
    dp = lax.axis_index("dp")
    for give in range(2):
        for slot, z in enumerate(SLOTS):
            body(give, slot, dp ^ (2 * z + give))


def ffn_dw_kernel(
    na, ga, ha, nb, gb, hb, c0, c1, c2, c3, wd, y_keep, y_give, z_keep, z_give, lo_keep, lo_give, dwgu, dwd
):
    for m in range(2):
        at = slice(512 * m, 512 * m + 512)
        dwgu[:, at] = dot_tn(na[...], ga[:, at]) + dot_tn(nb[...], gb[:, at])
    for m in range(3):
        at = slice(256 * m, 256 * m + 256)
        dwd[:, at] = (
            dot_tn(ha[0:T], c2[:, at])
            + dot_tn(ha[T : 2 * T], c3[:, at])
            + dot_tn(hb[0:T], c0[:, at])
            + dot_tn(hb[T : 2 * T], c1[:, at])
        )
    for n, ref in enumerate((hb, ha)):
        lo_keep[n] = dot(ref[0:T], wd[...]).astype(BF16)
        lo_give[n] = dot(ref[T : 2 * T], wd[...]).astype(BF16)

    def put(g, slot, owner):
        ref = y_give if g else y_keep
        a = pl.ds(pl.multiple_of(96 * owner, 32), 96)
        for m in range(3):
            ref[slot, 96 * m : 96 * m + 96] = dwgu[a, 256 * m : 256 * m + 256].astype(BF16)
        ref = z_give if slot > 1 else z_keep
        slot = 2 * (slot % 2) + g
        ref[slot, 0:96] = dwgu[a, 768:1024].astype(BF16)
        a = pl.ds(pl.multiple_of(64 * owner, 64), 64)
        for m in range(3):
            ref[slot, 96 + 64 * m : 160 + 64 * m] = dwd[a, 256 * m : 256 * m + 256].astype(BF16)

    slots(put)


def ffn_second_kernel(y_keep, y_got, z_keep, z_got, y_next, y_give, z_next, z_give):
    for keep, got, rest, give in ((y_keep, y_got, y_next, y_give), (z_keep, z_got, z_next, z_give)):
        rest[...] = (keep[0:2].astype(F32) + got[0:2].astype(F32)).astype(BF16)
        give[...] = (keep[2:4].astype(F32) + got[2:4].astype(F32)).astype(BF16)


def ffn_third_kernel(y_keep, y_got, z_keep, z_got, y_give, z_give):
    y_give[...] = (y_keep[1].astype(F32) + y_got[1].astype(F32)).astype(BF16)
    z_give[...] = (z_keep[1].astype(F32) + z_got[1].astype(F32)).astype(BF16)


def split(x):
    high = x.astype(BF16).astype(F32)
    return jnp.concatenate([high, x - high], axis=0).astype(BF16)


def first_dw_kernel(n1, dqkv, keep, give, dw):
    for t in range(3):
        at = slice(128 * t, 128 * t + 128)
        dw[:, at] = dot_tn(n1[...], dqkv[:, at])

    def put(g, slot, owner):
        ref = give if g else keep
        a = pl.ds(pl.multiple_of(96 * owner, 32), 96)
        for t in range(3):
            at = FIRST * slot + 96 * t
            ref[at : at + 96] = dw[a, 128 * t : 128 * t + 128].astype(BF16)

    slots(put)


def second_dw_kernel(n1, dqkv, wo_keep, wo_got, wo_along, ta, tb, keep, give, dw, wo, chunk):
    for t in range(2):
        at = slice(128 * t, 128 * t + 128)
        dw[:, at] = dot_tn(n1[...], dqkv[:, at])
    for d in range(8):
        wo[d] = wo_keep[0, d].astype(F32) + wo_got[d].astype(F32) + wo_along[d].astype(F32)

    def put(g, slot, owner):
        ref = give if g else keep
        a = pl.ds(pl.multiple_of(96 * owner, 32), 96)
        for t in range(2):
            chunk[96 * t : 96 * t + 96] = dw[a, 128 * t : 128 * t + 128]
        for t in range(6):
            chunk[192 + 24 * t : 216 + 24 * t] = wo[owner, :, 128 * t : 128 * t + 128]
        ref[SECOND * slot : SECOND * slot + SECOND] = chunk[...].astype(BF16)

    slots(put)
    for ref in (keep, give):
        ref[4 * SECOND : 4 * SECOND + 16] = split(ta[...] + tb[...])


def tail_of(ref, base):
    both = ref[base : base + 16].astype(F32)
    return both[0:8] + both[8:16]


def stage_kernel(n, chunk, keep, got, next_keep, next_give):
    half = n // 2 * chunk
    for at, ref in ((0, next_keep), (half, next_give)):
        here = slice(at, at + half)
        ref[0:half] = (keep[here].astype(F32) + got[here].astype(F32)).astype(BF16)
        if chunk == SECOND:
            ref[half : half + 16] = split(tail_of(keep, n * chunk) + tail_of(got, n * chunk))


def first_back_kernel(ka, ga, yk, yg, ya, zk, zg, za, dwd, b0, b1, b2, b3, total, ffn):
    j = lax.axis_index("blk")
    ffn[0:288] = yk[0].astype(F32) + yg[0].astype(F32) + ya[...].astype(F32)
    ffn[288:576] = zk[0].astype(F32) + zg[0].astype(F32) + za[...].astype(F32)
    for m in range(3):
        dwd[:, 256 * m : 256 * m + 256] = ffn[384 + 64 * m : 448 + 64 * m]
    total[...] = ka[...].astype(F32) + ga[...].astype(F32)
    for k, ref in enumerate((b0, b1, b2, b3)):
        for t in range(3):
            part = total[pl.ds(pl.multiple_of(96 * t + 24 * (j ^ k), 8), 24)]
            ref[:, 128 * t : 128 * t + 128] = part.astype(BF16)
        for m in range(4):
            part = ffn[pl.ds(pl.multiple_of(96 * m + 24 * (j ^ k), 8), 24)]
            ref[:, 384 + 256 * m : 640 + 256 * m] = part.astype(BF16)


def second_back_kernel(kb, gb, dwo, b0, b1, b2, b3, total):
    j = lax.axis_index("blk")
    total[...] = kb[0:SECOND].astype(F32) + gb[0:SECOND].astype(F32)
    parts = split(tail_of(kb, SECOND) + tail_of(gb, SECOND)).astype(F32)
    parts = jnp.concatenate([parts, jnp.zeros((8, 128), F32)], axis=0).astype(BF16)
    for t in range(6):
        at = 192 + 24 * t
        dwo[:, 128 * t : 128 * t + 128] = total[at : at + 24]
    for k, ref in enumerate((b0, b1, b2, b3)):
        for t in range(2):
            part = total[pl.ds(pl.multiple_of(96 * t + 24 * (j ^ k), 8), 24)]
            ref[:, 128 * t : 128 * t + 128] = part.astype(BF16)
        ref[:, 256:384] = parts


def attn_bwd_kernel(second, *refs):
    count = 1 if second else 2
    heads = range(HT - 1, HT) if second else range(2)
    qkv, refs = refs[0], refs[1:]
    probs, refs = refs[:count], refs[count:]
    invs, refs = refs[:count], refs[count:]
    outs, refs = refs[:count], refs[count:]
    (g0, g1, g2, g3, dqkv, table_grad,
     dotm, dom, qm, ktm, delta, dst, dq_acc, dk_acc, dv_acc, near, far) = refs
    j_me = lax.axis_index("blk")
    low = low_half(T)
    rows_low = lax.broadcasted_iota(jnp.int32, (128, T), 0) < 64

    for k, ref in enumerate((g0, g1, g2, g3)):
        b = j_me ^ k
        if second:
            rest = ref[256:384].astype(F32)
            rows = jnp.concatenate([rest, pltpu.roll(rest, 64, 1)], axis=0)
            turned = jnp.where(rows_low, jnp.transpose(rows) * invs[0][b], 0.0)
        else:
            turned = jnp.transpose(ref[0:256].astype(F32))
            turned = turned * jnp.where(rows_low, invs[0][b], invs[1][b])
        turned = turned.astype(BF16).astype(F32)
        back = jnp.transpose(turned)
        for n in range(count):
            dotm[n, b] = jnp.where(rows_low == (n == 0), turned, 0.0).astype(BF16)
            dom[n, b] = jnp.where(low == (n == 0), back, 0.0).astype(BF16)

    for i in range(TP):
        at = slice(T * i, T * i + T)
        if second:
            q = pltpu.roll(qkv[3, i].astype(F32), 64, 1)
            keys = jnp.transpose(q)
        else:
            q = qkv[0, i].astype(F32)
            keys = jnp.transpose(qkv[1, i].astype(F32))
        for n in range(count):
            g = dotm[n, i].astype(F32)[64 * n : 64 * n + 64]
            delta[n, i] = jnp.sum(outs[n][:, at] * g, axis=0, keepdims=True)
            qm[n, i] = jnp.where(low == (n == 0 and not second), q, 0.0).astype(BF16)
            ktm[n, :, at] = jnp.where(rows_low == (n == 0), keys, 0.0).astype(BF16)

    dq_acc[...] = jnp.zeros(dq_acc.shape, F32)
    dk_acc[...] = jnp.zeros(dk_acc.shape, F32)
    dv_acc[...] = jnp.zeros(dv_acc.shape, F32)
    table_grad[...] = jnp.zeros(table_grad.shape, F32)
    key_at = lax.broadcasted_iota(jnp.int32, (128, 128), 0)
    query_at = lax.broadcasted_iota(jnp.int32, (128, 128), 1)
    upper = query_at >= key_at
    turn = (key_at + query_at == 127).astype(F32)

    def diagonals(m):
        m = lax.dot_general(
            turn, m, (((1,), (0,)), ((), ())), precision=HIGHEST, preferred_element_type=F32
        )
        return jnp.sum(pltpu.roll(m, 1, 1, stride=1, stride_axis=0), axis=0, keepdims=True)

    row_id = lax.broadcasted_iota(jnp.int32, (NB, 128), 0)
    lane_id = lax.broadcasted_iota(jnp.int32, (NB, 128), 1)
    hot_neg = bucket_of(-lane_id) == row_id
    hot_pos = bucket_of(128 - lane_id) == row_id

    for n, prob in enumerate(probs):
        near[...] = jnp.zeros(near.shape, F32)
        far[...] = jnp.zeros(far.shape, F32)
        for i in range(TP):
            at = slice(T * i, T * i + T)
            row_delta = delta[n, i]
            for j in range(TP):
                dp = dot(qkv[2 + 2 * second, j], dotm[n, i])
                ds = prob[i, j].astype(F32) * (dp - row_delta)
                dst[j] = ds.astype(BF16)
                for a in range(2):
                    for c in range(2):
                        gap = 2 * (j - i) + a - c
                        part = ds[128 * a : 128 * a + 128, 128 * c : 128 * c + 128]
                        if abs(gap) <= 1:
                            near[gap + 1] += part
                        else:
                            far[int(gap > 0)] += jnp.sum(part.reshape(16, 8, 128), axis=0)
            d_all = dst[...].reshape(TP * T, T)
            dq_acc[:, at] += dot(ktm[n], d_all)
            dk_acc[...] += dot(d_all, qm[n, i])
            dv_acc[...] += dot(prob[i].reshape(TP * T, T), dom[n, i])
        before, diagonal, after = near[0], near[1], near[2]
        neg = jnp.where(upper, diagonal, before)
        pos = jnp.where(upper, after, diagonal)
        neg, pos = diagonals(neg), diagonals(pos)
        far_neg = jnp.sum(far[0], axis=0, keepdims=True) + jnp.sum(
            jnp.where(upper, before, 0.0), axis=0, keepdims=True
        )
        far_pos = jnp.sum(far[1], axis=0, keepdims=True) + jnp.sum(
            jnp.where(upper, 0.0, after), axis=0, keepdims=True
        )
        spread = (
            jnp.where(hot_neg, neg, 0.0)
            + jnp.where(hot_pos, pos, 0.0)
            + jnp.where(row_id == 15, far_neg, 0.0)
            + jnp.where(row_id == 31, far_pos, 0.0)
        )
        sums = jnp.sum(spread, axis=1, keepdims=True)
        sums = jnp.sum(jnp.where(lane_id == row_id, sums, 0.0), axis=0, keepdims=True)
        h = heads[n]
        table_grad[h : h + 1] = sums
    for i in range(TP):
        at = slice(T * i, T * i + T)
        dq = jnp.transpose(dq_acc[:, at])
        if second:
            parts = (dq + dk_acc[at], dv_acc[at])
        else:
            parts = (dq, dk_acc[at], dv_acc[at])
        for n, part in enumerate(parts):
            dqkv[i, :, 128 * n : 128 * n + 128] = part.astype(BF16)


def one_grad_kernel(da, db, w, keep, give):
    j = lax.axis_index("blk")

    def body(k, carry):
        total = dot_nt(da[j ^ k], w[:, 0:384]) + dot_nt(db[j ^ k], w[:, 384:640])
        put_pair(keep, give, k, total.astype(BF16))
        return carry

    lax.fori_loop(0, TP, body, 0)


def finish(parts, w, out, gain):
    total = jnp.zeros((w.shape[0], 128), F32)
    for n, part in enumerate(parts):
        at = slice(128 * n, 128 * n + 128)
        total = total + part * w[:, at].astype(F32)
        out[:, at] = part
    return jnp.sum(total, axis=1, keepdims=True) / gain


def put_row(ref, wide):
    rows = wide.shape[0]
    row_id = lax.broadcasted_iota(jnp.int32, (rows, 128), 0)
    eye = row_id == lax.broadcasted_iota(jnp.int32, (rows, 128), 1)
    ref[...] = jnp.sum(jnp.where(eye, wide, 0.0), axis=0, keepdims=True)[:, 0:rows]


def first_final_kernel(b0, b1, b2, b3, gains, wg, wu, dg, du, gg2, src):
    j_me = lax.axis_index("blk")
    low = low_half(wg.shape[0])
    for k, ref in enumerate((b0, b1, b2, b3)):
        src[j_me ^ k] = ref[:, 384:1408].astype(F32)
    gain_grad = 0.0
    for n, (w, out) in enumerate(((wg, dg), (wu, du))):
        parts = [None] * 16
        for t in range(4):
            at = slice(512 * n + 128 * t, 512 * n + 128 * t + 128)
            for half in range(2):
                a, b = src[2 * half, :, at], src[2 * half + 1, :, at]
                parts[4 * t + half] = jnp.where(low, a, pltpu.roll(b, 64, 1))
                parts[4 * t + 2 + half] = jnp.where(low, pltpu.roll(a, 64, 1), b)
        gain_grad = gain_grad + finish(parts, w, out, gains[1])
    put_row(gg2, gain_grad)


def second_final_kernel(
    a0, a1, a2, a3, b0, b1, b2, b3, gains, wq, wk, wv, dq, dk, dv, gg1, table, src
):
    j_me = lax.axis_index("blk")
    low = low_half(wq.shape[0])
    heads = jnp.zeros((128, 128), F32)
    head_id = lax.broadcasted_iota(jnp.int32, (128, 128), 0)
    for k, (first, second) in enumerate(zip((a0, a1, a2, a3), (b0, b1, b2, b3))):
        src[j_me ^ k, :, 0:384] = first[:, 0:384].astype(F32)
        src[j_me ^ k, :, 384:640] = second[:, 0:256].astype(F32)
        parts = second[:, 256:384].astype(F32)
        for h in range(HT):
            row = parts[h : h + 1] + parts[8 + h : 9 + h]
            heads = jnp.where(head_id == HT * (j_me ^ k) + h, row, heads)
    table[...] = heads[0:H, 0:NB]

    def one(j, n):
        return src[j, :, 128 * n : 128 * n + 128]

    gain_grad = 0.0
    for n, (w, out) in enumerate(((wq, dq), (wk, dk), (wv, dv))):
        parts = []
        for j in range(0, TP, 2):
            rest = []
            for m in (j, j + 1):
                last = one(m, 4 if n == 2 else 3)
                rest.append(pltpu.roll(last, 64, 1) if n == 1 else last)
            mid = pltpu.roll(one(j + 1, n), 64, 1)
            parts += [
                one(j, n),
                jnp.where(low, rest[0], mid),
                jnp.where(low, mid, pltpu.roll(rest[1], 64, 1)),
            ]
        gain_grad = gain_grad + finish(parts, w, out, gains[0])
    put_row(gg1, gain_grad)


def close_kernel(keep, got, along, mixed_grad, tok, gains, tokens_grad, mark):
    mark[...] = jnp.zeros((8, 128), F32)
    x = tok[lax.axis_index("blk")].astype(F32)
    rstd = lax.rsqrt(jnp.mean(x * x, axis=-1, keepdims=True) + EPSILON)
    n = x * rstd
    u = (keep[0].astype(F32) + got[0].astype(F32) + along[...].astype(F32)) * gains[0:1]
    grad = rstd * (u - n * jnp.mean(u * n, axis=-1, keepdims=True))
    tokens_grad[...] = mixed_grad[...] + grad


AXES = ("dp", "blk")
COST = {"qkv": 0, "attn_fwd": (0, 0, 0), "units": 15, "ffn": 0, "ffn_dw": 0, "mid": 0, "attn_bwd": (0, 10), "one_grad": 40, "stage_y": 0, "stage_z": 10, "first_back": 0}


def group_local(
    n_dp, n_blk,
    tokens, segment_ids, w_query, w_key, w_value, w_attn_out, attn_gain, rel_bias,
    w_gate, w_up, w_down, ffn_gain, cotangent,
):
    n_dev = n_dp * n_blk

    def later(x, *others):
        return lax.optimization_barrier((x,) + others)[0]

    def swap(x, mask):
        return lax.ppermute(x, AXES, [(d, d ^ mask) for d in range(n_dev)])

    def share(x, *others):
        along = swap(x, 2)
        return (x, swap(x, 1), along, swap(later(along, *others), 1))

    def reduce_pair(keep, give):
        got = swap(give, 1)
        return got, swap(keep[1] + got[1], 2)

    def round_one(x):
        return lax.optimization_barrier((swap(x, 16), swap(x, 8), swap(x, 4)))

    def round_two(far, near):
        return lax.optimization_barrier((swap(far, 8), swap(near, 4), swap(far, 4)))

    def gathered(x, one, two, *others):
        far, near, other = one
        last, near_y, far_y = two
        return (x, near, far, last, other, near_y, far_y, swap(later(last, *others), 4))

    tok_own, cot_own = tokens[0], cotangent[0]
    rows, ff = w_query.shape[0], w_gate.shape[1]
    flat = TP * T
    table = rel_bias.astype(F32).T

    *slabs, tok_seg, gain_cols = call(
        prep_kernel,
        (sds((rows, 1664), BF16),) * TP + (sds((T + 16, D), BF16), sds((2, rows, 128), F32)),
        w_query, w_key, w_value, w_gate, w_up, tok_own, segment_ids, attn_gain, ffn_gain,
        name="prep", vmem=60, held=(0, 1, 2, 3, 4, 5),
        scratch=(
            pltpu.VMEM((TP, rows, 1664), BF16),
            *(pltpu.VMEM((rows, D), BF16),) * 3,
            *(pltpu.VMEM((rows, ff), BF16),) * 2,
            pltpu.SemaphoreType.DMA((6,)),
        ),
    )
    toks_x, toks_c = swap(tok_seg, 2), swap(tok_seg, 1)
    slabs = (slabs[0], swap(slabs[1], 1), swap(slabs[2], 2), swap(slabs[3], 3))
    first = call(
        pack_kernel, sds((128, 640), BF16), *slabs, w_attn_out,
        name="pack", vmem=60, held=(4,),
        scratch=(pltpu.VMEM((96, 640), F32), pltpu.VMEM((rows, D), BF16), pltpu.SemaphoreType.DMA),
    )
    second = call(
        pack_more_kernel, sds((576, 256), BF16), *slabs, w_down,
        name="pack_more", vmem=60, held=(4,), after=(first,),
        scratch=(pltpu.VMEM((96, 1024), F32), pltpu.VMEM((64, D), BF16), pltpu.SemaphoreType.DMA),
    )
    first_one = round_one(first)
    bias = call(
        bias_kernel, sds((HT, 3, T, T), F32), table, smem=(0,), name="bias", after=(second,)
    )
    far, near = lax.optimization_barrier(first_one + (second, bias))[:2]
    first_two = round_two(far, near)
    toks_r = swap(later(toks_x, *first_two), 1)
    firsts = gathered(first, first_one, first_two, *())
    toks = (tok_seg, toks_c, toks_x, toks_r)
    second_one = (
        swap(later(second, *first_one), 16),
        swap(later(second, *first_two), 8),
        swap(later(second, *first_two), 4),
    )

    tok, n1, qkv, w_qkv, gains, segq, segk = call(
        qkv_kernel,
        (
            sds((TP, T, D), BF16), sds((TP, T, D), BF16), sds((5, TP, T, 128), BF16),
            sds((D, 640), BF16), sds((8, D), F32), sds((TP, 8, T), F32), sds((TP, T, T), F32),
        ),
        *toks, *firsts, name="qkv", vmem=16, cost=COST["qkv"],
    )
    stripes = call(
        stripes_kernel, sds((192, D), BF16), *firsts, name="stripes", after=(segq,),
        scratch=(pltpu.VMEM((192, D), F32),),
    )
    stripes = share(stripes)
    wop = call(
        out_weight_kernel, sds((D, D), BF16), *stripes, name="out_weight",
        scratch=(pltpu.VMEM((D, D), F32),),
    )
    cots_x = swap(later(cot_own, *(gains,)), 2)
    heads = []
    for h in range(HT):
        heads.append(
            call(
                functools.partial(attn_fwd_kernel, h),
                (sds((TP, TP, T, T), BF16), sds((TP, 1, T), F32), sds((DH, flat), F32)),
                table, bias, qkv, segq, segk, smem=(0,), name="attn_fwd", vmem=14,
                cost=COST["attn_fwd"][h], after=((heads[-1][1],) if heads else ()) + ((cots_x,) if h == 2 else ()),
                scratch=(
                    pltpu.VMEM((TP, 128, T), BF16),
                    pltpu.VMEM((DH, flat), BF16),
                    pltpu.VMEM((TP, T, T), F32),
                ),
            )
        )
    probs, inv_tots, out_ts = zip(*heads)
    cots = (cot_own, swap(later(cot_own, inv_tots[0]), 1), cots_x, swap(later(cots_x, inv_tots[0]), 1))
    far, near = lax.optimization_barrier(second_one + (inv_tots[0],))[:2]
    second_two = round_two(far, near)
    seconds = gathered(second, second_one, second_two)
    att = call(join_kernel, sds((1536, 128), BF16), *out_ts, name="join")
    atts = share(att, wop)
    wgu, wd = call(
        units_kernel, (sds((D, 1024), BF16), sds((512, D), BF16)), *seconds, name="units",
        cost=COST["units"],
    )

    def ffn(ks, *after):
        return call(
            functools.partial(ffn_kernel, ks),
            (
                sds((2, T, D), BF16), sds((2, T, 512), BF16), sds((2, T, 1024), BF16),
                sds((T, D), BF16), sds((T, D), BF16), sds((2, T, D), BF16), sds((T, D), F32),
            ),
            *atts, gains, wop, wgu, wd, tok, cots[ks[0]], cots[ks[1]], name="ffn", vmem=24,
            cost=COST["ffn"], after=after,
        )

    n2_a, hid_a, ggug_a, keep, give, _, _ = ffn((2, 3))
    two_x = keep + swap(give, 1)
    n2_b, hid_b, ggug_b, two_keep, give, attc, mixed_own = ffn((0, 1), two_x)
    two_x = swap(two_x, 2)
    two_c = swap(give, 1)
    y_keep, y_give, z_keep, z_give, lo_keep, lo_give = call(
        ffn_dw_kernel, (sds((4, 288, 256), BF16),) * 4 + (sds((2, T, D), BF16),) * 2,
        n2_a.reshape(2 * T, D), ggug_a.reshape(2 * T, 1024), hid_a.reshape(2 * T, 512),
        n2_b.reshape(2 * T, D), ggug_b.reshape(2 * T, 1024), hid_b.reshape(2 * T, 512),
        *cots, wd, name="ffn_dw", vmem=20, cost=COST["ffn_dw"],
        scratch=(pltpu.VMEM((D, 1024), F32), pltpu.VMEM((512, D), F32)),
    )
    y_got, z_got = swap(y_give, 4), swap(z_give, 8)
    mixed_grad, g0, g1, g2, g3, wo_keep, *wo_gives = call(
        mid_kernel,
        (sds((T, D), F32),) + (sds((384, 128), BF16),) * 4
        + (sds((2, 8, 24, D), BF16),) + (sds((8, 24, D), BF16),) * 2,
        two_keep, two_c, two_x, mixed_own, cot_own, attc, wop, gains, name="mid", vmem=16,
        after=(y_give,), scratch=(pltpu.VMEM((D, D), F32),), cost=COST["mid"],
    )
    g1, g2, g3 = swap(g1, 1), swap(g2, 2), swap(g3, 3)
    wo_got = (swap(wo_gives[0], 1), swap(wo_gives[1], 1))
    lo_c = swap(later(lo_give, *()), 1)
    lo_sum = lo_keep[1] + lo_c[1]
    wo_sum = later(wo_keep[1] + wo_got[1], g1, g2, g3)
    wo_along = swap(wo_sum, 2)

    def attn_bwd(second, *after):
        mine = slice(2, 3) if second else slice(0, 2)
        count = 1 if second else 2
        return call(
            functools.partial(attn_bwd_kernel, second),
            (sds((TP, T, 256 if second else 384), BF16), sds((8, 128), F32)),
            qkv, *probs[mine], *inv_tots[mine], *out_ts[mine], g0, g1, g2, g3,
            name="attn_bwd", vmem=22, cost=COST["attn_bwd"][second], after=after,
            scratch=(
                pltpu.VMEM((count, TP, 128, T), BF16),
                pltpu.VMEM((count, TP, T, 128), BF16),
                pltpu.VMEM((count, TP, T, 128), BF16),
                pltpu.VMEM((count, 128, TP * T), BF16),
                pltpu.VMEM((count, TP, 1, T), F32),
                pltpu.VMEM((TP, T, T), BF16),
                pltpu.VMEM((128, TP * T), F32),
                pltpu.VMEM((TP * T, 128), F32),
                pltpu.VMEM((TP * T, 128), F32),
                pltpu.VMEM((3, 128, 128), F32),
                pltpu.VMEM((2, 8, 128), F32),
            ),
        )

    def chunks(n, chunk):
        return sds((n * chunk + (TAIL if chunk == SECOND else 0), 128), BF16)

    def stage(n, chunk, keep, got, name, *after):
        return call(
            functools.partial(stage_kernel, n, chunk), (chunks(n // 2, chunk),) * 2, keep, got,
            name=name, after=after, cost=COST[name],
        )

    da, ta = attn_bwd(0, *(wo_sum,))
    a_keep, a_give = call(
        first_dw_kernel, (chunks(4, FIRST),) * 2, n1.reshape(flat, D), da.reshape(flat, 384),
        name="first_dw", vmem=12, scratch=(pltpu.VMEM((D, 384), F32),),
    )
    a_got = swap(a_give, 4)
    y_keep, y_give, z_keep, z_give = call(
        ffn_second_kernel, (sds((2, 288, 256), BF16),) * 4, y_keep, y_got, z_keep, z_got,
        name="ffn_second", after=(a_give,),
    )
    y_got, z_got = swap(y_give, 8), swap(z_give, 16)
    db, tb = attn_bwd(1, y_give, *(lo_sum,))
    b_keep, b_give = call(
        second_dw_kernel, (chunks(4, SECOND),) * 2,
        n1.reshape(flat, D), db.reshape(flat, 256), wo_keep, wo_got[0], wo_along, ta, tb,
        name="second_dw", vmem=12,
        scratch=(
            pltpu.VMEM((D, 256), F32), pltpu.VMEM((8, 24, D), F32), pltpu.VMEM((SECOND, 128), F32),
        ),
    )
    b_got = swap(b_give, 4)
    one_keep, one_give = call(
        one_grad_kernel, (sds((2, T, D), BF16),) * 2, da, db, w_qkv, name="one_grad", vmem=16,
        after=(b_give,), cost=COST["one_grad"],
    )
    lo_x = swap(later(lo_sum, *()), 2)
    one_c = swap(one_give, 1)
    one_x = swap(later(one_keep[1] + one_c[1], *(lo_x,)), 2)
    a_keep, a_give = stage(4, FIRST, a_keep, a_got, "stage_y", b_give)
    a_got = swap(a_give, 8)
    y_give, z_give = call(
        ffn_third_kernel, (sds((288, 256), BF16),) * 2, y_keep, y_got, z_keep, z_got,
        name="ffn_third", after=(a_give,),
    )
    y_along, z_along = swap(y_give, 16), swap(z_give, 4)
    b_keep, b_give = stage(4, SECOND, b_keep, b_got, "stage_y", *(y_give,))
    b_got = swap(b_give, 8)
    a_keep, a_give = stage(2, FIRST, a_keep, a_got, "stage_z", b_give)
    a_got = swap(a_give, 16)
    b_keep, b_give = stage(2, SECOND, b_keep, b_got, "stage_z", *(a_give,))
    b_got = swap(b_give, 16)
    layer_out = mixed_own + lo_keep[0].astype(F32) + lo_c[0].astype(F32) + lo_x.astype(F32)
    tokens_grad, mark = call(
        close_kernel, (sds((T, D), F32), sds((8, 128), F32)), one_keep, one_c, one_x, mixed_grad, tok, gains,
        name="close", vmem=10, after=(a_got,),
    )
    dwd, *backs = call(
        first_back_kernel, (sds((64, D), F32),) + (sds((rows, 1408), BF16),) * 4,
        a_keep, a_got, y_keep, y_got, y_along, z_keep, z_got, z_along,
        name="first_back", after=(b_give,), cost=COST["first_back"],
        scratch=(pltpu.VMEM((FIRST, 128), F32), pltpu.VMEM((576, 256), F32)),
    )
    firsts = (backs[0], swap(backs[1], 1), swap(backs[2], 2), swap(backs[3], 3))
    dwo, *backs = call(
        second_back_kernel, (sds((rows, D), F32),) + (sds((rows, 384), BF16),) * 4, b_keep, b_got,
        name="second_back", after=(mark, *firsts[1:]), scratch=(pltpu.VMEM((SECOND, 128), F32),),
    )
    seconds = (backs[0], swap(backs[1], 1), swap(backs[2], 2), swap(backs[3], 3))
    dg, du, gg2 = call(
        first_final_kernel, (sds((rows, ff), F32),) * 2 + (sds((1, rows), F32),),
        *firsts, gain_cols, w_gate, w_up, name="first_final",
        scratch=(pltpu.VMEM((TP, rows, 1024), F32),),
    )
    dq, dk, dv, gg1, table_sum = call(
        second_final_kernel,
        (sds((rows, D), F32),) * 3 + (sds((1, rows), F32), sds((H, NB), F32)),
        *firsts, *seconds, gain_cols, w_query, w_key, w_value, name="second_final", after=(gg2,),
        scratch=(pltpu.VMEM((TP, rows, 640), F32),),
    )
    return (
        layer_out.astype(BF16)[None],
        tokens_grad[None],
        dq,
        dk,
        dv,
        dwo,
        gg1[0],
        table_sum.T,
        dg,
        du,
        dwd,
        gg2[0],
    )


KEY_BLOCK = 256
HIGHEST = lax.Precision.HIGHEST


def rms_norm(values, gain):
    return values * lax.rsqrt(jnp.mean(values * values, axis=-1, keepdims=True) + EPSILON) * gain


def split_heads(flat_rows):
    return flat_rows.reshape(flat_rows.shape[0], flat_rows.shape[1], H, DH)


def join_heads(per_head):
    return per_head.reshape(per_head.shape[0], per_head.shape[1], H * DH)


def project(left, matrix):
    return jnp.einsum("rtd,de->rte", left, matrix, preferred_element_type=jnp.float32)


def project_back(left, matrix):
    return jnp.einsum("rte,de->rtd", left, matrix, preferred_element_type=jnp.float32)


def weight_grad(left, right):
    return jnp.einsum("rtd,rte->de", left, right, preferred_element_type=jnp.float32)


def block_scores(queries, key_block, query_pos, key_pos, query_seg, key_seg, bias_table):
    raw_scores = jnp.einsum(
        "rqhd,rkhd->rhqk", queries, key_block, preferred_element_type=jnp.float32
    )
    buckets = bucket_of(key_pos[None, :] - query_pos[:, None])
    one_hot = (buckets[:, :, None] == jnp.arange(NB, dtype=jnp.int32)[None, None, :]).astype(
        jnp.float32
    )
    rel_term = jnp.einsum("qkb,bh->hqk", one_hot, bias_table, precision=HIGHEST)
    allowed = (query_seg[:, :, None] == key_seg[:, None, :])[:, None]
    return (raw_scores + rel_term[None], allowed, one_hot)


def absorb(
    running, queries, key_block, value_block, query_pos, key_pos, query_seg, key_seg, bias_table
):
    row_peak, row_total, weighted = running
    scores, allowed, unused = block_scores(
        queries, key_block, query_pos, key_pos, query_seg, key_seg, bias_table
    )
    block_peak = jnp.max(jnp.where(allowed, scores, MASKED), axis=-1)
    new_peak = jnp.maximum(row_peak, block_peak)
    weights = jnp.where(allowed, jnp.exp(scores - new_peak[..., None]), 0.0)
    factor = jnp.exp(row_peak - new_peak)
    row_total = row_total * factor + jnp.sum(weights, axis=-1)
    weighted = weighted * factor[..., None] + jnp.einsum(
        "rhqk,rkhd->rhqd",
        weights.astype(jnp.bfloat16),
        value_block,
        preferred_element_type=jnp.float32,
    )
    return (new_peak, row_total, weighted)


def pair_grads(
    queries,
    out_grad,
    log_total,
    row_delta,
    key_block,
    value_block,
    query_pos,
    key_pos,
    query_seg,
    key_seg,
    bias_table,
):
    scores, allowed, one_hot = block_scores(
        queries, key_block, query_pos, key_pos, query_seg, key_seg, bias_table
    )
    prob_map = jnp.where(allowed, jnp.exp(scores - log_total[..., None]), 0.0)
    prob_grad = jnp.einsum(
        "rqhd,rkhd->rhqk", out_grad, value_block, preferred_element_type=jnp.float32
    )
    score_grad = prob_map * (prob_grad - row_delta[..., None])
    score_low = score_grad.astype(jnp.bfloat16)
    query_grad = jnp.einsum(
        "rhqk,rkhd->rqhd", score_low, key_block, preferred_element_type=jnp.float32
    )
    key_grad = jnp.einsum("rhqk,rqhd->rkhd", score_low, queries, preferred_element_type=jnp.float32)
    value_grad = jnp.einsum(
        "rhqk,rqhd->rkhd",
        prob_map.astype(jnp.bfloat16),
        out_grad,
        preferred_element_type=jnp.float32,
    )
    table_grad = jnp.einsum("rhqk,qkb->bh", score_grad, one_hot, precision=HIGHEST)
    return (query_grad, key_grad, value_grad, table_grad)


def in_blocks(step_fn, running, pieces):
    length = pieces[0].shape[1]
    block_size = math.gcd(length, KEY_BLOCK)
    block_count = length // block_size
    stacked = tuple(
        (
            jnp.moveaxis(
                member.reshape((member.shape[0], block_count, block_size) + member.shape[2:]), 1, 0
            )
            for member in pieces
        )
    )
    starts = block_size * jnp.arange(block_count, dtype=jnp.int32)

    def scan_step(inner_state, item_pair):
        return (step_fn(inner_state, item_pair[0], item_pair[1]), None)

    running, unused = lax.scan(scan_step, running, (stacked, starts))
    return running


def local(
    tokens,
    segment_ids,
    w_query,
    w_key,
    w_value,
    w_attn_out,
    attn_gain,
    rel_bias,
    w_gate,
    w_up,
    w_down,
    ffn_gain,
    cotangent,
):
    row_count, local_len, unused_dim = tokens.shape
    my_block = lax.axis_index("blk")
    full_query, full_key, full_value, full_out, gain_one = (
        lax.all_gather(w_query, ("dp", "blk"), axis=0, tiled=True),
        lax.all_gather(w_key, ("dp", "blk"), axis=0, tiled=True),
        lax.all_gather(w_value, ("dp", "blk"), axis=0, tiled=True),
        lax.all_gather(w_attn_out, ("dp", "blk"), axis=0, tiled=True),
        lax.all_gather(attn_gain, ("dp", "blk"), axis=0, tiled=True),
    )
    full_gate, full_up, full_down, gain_two = (
        lax.all_gather(w_gate, ("dp", "blk"), axis=0, tiled=True),
        lax.all_gather(w_up, ("dp", "blk"), axis=0, tiled=True),
        lax.all_gather(w_down, ("dp", "blk"), axis=0, tiled=True),
        lax.all_gather(ffn_gain, ("dp", "blk"), axis=0, tiled=True),
    )
    row_segs = lax.all_gather(segment_ids, "blk", axis=1, tiled=True)
    bias_table = rel_bias.astype(jnp.float32)
    gain_one_f = gain_one.astype(jnp.float32)
    gain_two_f = gain_two.astype(jnp.float32)
    inputs = tokens.astype(jnp.float32)
    query_pos = my_block * local_len + jnp.arange(local_len, dtype=jnp.int32)
    normed_one = rms_norm(inputs, gain_one_f).astype(jnp.bfloat16)
    query_flat = project(normed_one, full_query).astype(jnp.bfloat16)
    key_flat = project(normed_one, full_key).astype(jnp.bfloat16)
    value_flat = project(normed_one, full_value).astype(jnp.bfloat16)
    queries = split_heads(query_flat)
    key_heads = split_heads(key_flat)
    value_heads = split_heads(value_flat)

    def forward_piece(running, pieces):

        def step_fn(inner_state, blocks, block_start):
            block_len = blocks[0].shape[1]
            key_pos = block_start + jnp.arange(block_len, dtype=jnp.int32)
            key_seg = lax.dynamic_slice_in_dim(row_segs, block_start, block_len, 1)
            return absorb(
                inner_state,
                queries,
                split_heads(blocks[0]),
                split_heads(blocks[1]),
                query_pos,
                key_pos,
                segment_ids,
                key_seg,
                bias_table,
            )

        return in_blocks(step_fn, running, pieces)

    stat_shape = (row_count, H, local_len)
    start_state = (
        jnp.full(stat_shape, MASKED, jnp.float32),
        jnp.zeros(stat_shape, jnp.float32),
        jnp.zeros(stat_shape + (DH,), jnp.float32),
    )
    row_peak, row_total, weighted = forward_piece(
        start_state,
        (
            lax.all_gather(key_flat, "blk", axis=1, tiled=True),
            lax.all_gather(value_flat, "blk", axis=1, tiled=True),
        ),
    )
    log_total = row_peak + jnp.log(row_total)
    attended_f = jnp.transpose(weighted / row_total[..., None], (0, 2, 1, 3))
    attended = join_heads(attended_f).astype(jnp.bfloat16)
    mixed_in = inputs + project(attended, full_out)
    normed_two = rms_norm(mixed_in, gain_two_f).astype(jnp.bfloat16)
    gate_act = project(normed_two, full_gate)
    up_act = project(normed_two, full_up)

    def gated(gate_in, up_in):
        return jax.nn.gelu(gate_in, approximate=True) * up_in

    hidden_f, gated_back = jax.vjp(gated, gate_act, up_act)
    hidden = hidden_f.astype(jnp.bfloat16)
    layer_out = (mixed_in + project(hidden, full_down)).astype(jnp.bfloat16)
    down_grad = weight_grad(hidden, cotangent)
    hidden_grad = project_back(cotangent, full_down)
    gate_grad, up_grad = gated_back(hidden_grad)
    gate_low = gate_grad.astype(jnp.bfloat16)
    up_low = up_grad.astype(jnp.bfloat16)
    gate_w_grad = weight_grad(normed_two, gate_low)
    up_w_grad = weight_grad(normed_two, up_low)
    two_grad = project_back(gate_low, full_gate) + project_back(up_low, full_up)
    unused_two, norm_two_back = jax.vjp(rms_norm, mixed_in, gain_two_f)
    mixed_part, gain_two_grad = norm_two_back(two_grad)
    mixed_grad = cotangent.astype(jnp.float32) + mixed_part
    mixed_low = mixed_grad.astype(jnp.bfloat16)
    out_w_grad = weight_grad(attended, mixed_low)
    attended_grad = project_back(mixed_low, full_out).astype(jnp.bfloat16)
    grad_heads = split_heads(attended_grad)
    row_delta = jnp.sum(
        jnp.transpose(grad_heads.astype(jnp.float32), (0, 2, 1, 3))
        * (weighted / row_total[..., None]),
        axis=-1,
    )
    zero_heads = jnp.zeros(queries.shape, jnp.float32)
    zero_table = jnp.zeros((NB, H), jnp.float32)

    def query_piece(running, pieces):

        def step_fn(inner_state, blocks, block_start):
            block_len = blocks[0].shape[1]
            key_pos = block_start + jnp.arange(block_len, dtype=jnp.int32)
            key_seg = lax.dynamic_slice_in_dim(row_segs, block_start, block_len, 1)
            pair_parts = pair_grads(
                queries,
                grad_heads,
                log_total,
                row_delta,
                split_heads(blocks[0]),
                split_heads(blocks[1]),
                query_pos,
                key_pos,
                segment_ids,
                key_seg,
                bias_table,
            )
            return inner_state + pair_parts[0]

        return in_blocks(step_fn, running, pieces)

    query_grad = join_heads(
        query_piece(
            zero_heads,
            (
                lax.all_gather(key_flat, "blk", axis=1, tiled=True),
                lax.all_gather(value_flat, "blk", axis=1, tiled=True),
            ),
        )
    )
    log_rows, delta_rows = (
        lax.all_gather(log_total, "blk", axis=2, tiled=True),
        lax.all_gather(row_delta, "blk", axis=2, tiled=True),
    )

    def key_piece(running, pieces):

        def step_fn(inner_state, blocks, block_start):
            block_len = blocks[0].shape[1]
            piece_pos = block_start + jnp.arange(block_len, dtype=jnp.int32)
            piece_seg = lax.dynamic_slice_in_dim(row_segs, block_start, block_len, 1)
            piece_log = lax.dynamic_slice_in_dim(log_rows, block_start, block_len, 2)
            piece_delta = lax.dynamic_slice_in_dim(delta_rows, block_start, block_len, 2)
            pair_parts = pair_grads(
                split_heads(blocks[0]),
                split_heads(blocks[1]),
                piece_log,
                piece_delta,
                key_heads,
                value_heads,
                piece_pos,
                query_pos,
                piece_seg,
                segment_ids,
                bias_table,
            )
            return (
                inner_state[0] + pair_parts[1],
                inner_state[1] + pair_parts[2],
                inner_state[2] + pair_parts[3],
            )

        return in_blocks(step_fn, running, pieces)

    key_grad, value_grad, table_grad = key_piece(
        (zero_heads, zero_heads, zero_table),
        (
            lax.all_gather(query_flat, "blk", axis=1, tiled=True),
            lax.all_gather(attended_grad, "blk", axis=1, tiled=True),
        ),
    )
    query_low = query_grad.astype(jnp.bfloat16)
    key_low = join_heads(key_grad).astype(jnp.bfloat16)
    value_low = join_heads(value_grad).astype(jnp.bfloat16)
    query_w_grad = weight_grad(normed_one, query_low)
    key_w_grad = weight_grad(normed_one, key_low)
    value_w_grad = weight_grad(normed_one, value_low)
    one_grad = (
        project_back(query_low, full_query)
        + project_back(key_low, full_key)
        + project_back(value_low, full_value)
    )
    unused_one, norm_one_back = jax.vjp(rms_norm, inputs, gain_one_f)
    input_part, gain_one_grad = norm_one_back(one_grad)
    tokens_grad = mixed_grad + input_part
    table_sum = lax.psum(table_grad, ("dp", "blk"))
    all_sums = (
        lax.psum_scatter(query_w_grad, ("dp", "blk"), scatter_dimension=0, tiled=True),
        lax.psum_scatter(key_w_grad, ("dp", "blk"), scatter_dimension=0, tiled=True),
        lax.psum_scatter(value_w_grad, ("dp", "blk"), scatter_dimension=0, tiled=True),
        lax.psum_scatter(out_w_grad, ("dp", "blk"), scatter_dimension=0, tiled=True),
        lax.psum_scatter(gain_one_grad, ("dp", "blk"), scatter_dimension=0, tiled=True),
        lax.psum_scatter(gate_w_grad, ("dp", "blk"), scatter_dimension=0, tiled=True),
        lax.psum_scatter(up_w_grad, ("dp", "blk"), scatter_dimension=0, tiled=True),
        lax.psum_scatter(down_grad, ("dp", "blk"), scatter_dimension=0, tiled=True),
        lax.psum_scatter(gain_two_grad, ("dp", "blk"), scatter_dimension=0, tiled=True),
    )
    return (
        layer_out,
        tokens_grad,
        all_sums[0],
        all_sums[1],
        all_sums[2],
        all_sums[3],
        all_sums[4],
        table_sum,
        all_sums[5],
        all_sums[6],
        all_sums[7],
        all_sums[8],
    )


def solution(mesh):
    whole = P(AXES, None)
    rows = P("dp", "blk", None)
    n_dp, n_blk = mesh.shape["dp"], mesh.shape["blk"]
    grouped = functools.partial(group_local, n_dp, n_blk)
    body = grouped if (n_dp, n_blk) == (8, TP) else local
    return jax.shard_map(
        body,
        mesh=mesh,
        in_specs=(
            rows, P("dp", "blk"), whole, whole, whole, whole, P(AXES), P(),
            whole, whole, whole, P(AXES), rows,
        ),
        out_specs=(
            rows, rows, whole, whole, whole, whole, P(AXES), P(), whole, whole, whole, P(AXES),
        ),
        check_vma=False,
    )
```

```python
import functools
import math

import jax
import jax.numpy as jnp
from jax import lax
from jax.experimental import pallas as pl
from jax.experimental.pallas import tpu as pltpu
from jax.sharding import PartitionSpec as P

D = 768
H = 12
DH = 64
NB = 32
THRESHOLDS = (12, 16, 23, 32, 46, 64, 91)
MASKED = -1e30
EPSILON = 1e-06
TP = 4
T = 256
HT = 3
F32 = jnp.float32
BF16 = jnp.bfloat16
MIB = 1 << 20


def dot(a, b):
    return lax.dot_general(a, b, (((1,), (0,)), ((), ())), preferred_element_type=F32)


def dot_nt(a, b):
    return lax.dot_general(a, b, (((1,), (1,)), ((), ())), preferred_element_type=F32)


def dot_tn(a, b):
    return lax.dot_general(a, b, (((0,), (0,)), ((), ())), preferred_element_type=F32)


def bucket_of(relative):
    distance = jnp.abs(relative)
    far = jnp.full(relative.shape, 8, jnp.int32)
    for threshold in THRESHOLDS:
        far = far + (distance >= threshold).astype(jnp.int32)
    return jnp.where(relative > 0, NB // 2, 0) + jnp.where(distance < 8, distance, far)


def call(
    kernel, out_shape, *args, scratch=(), smem=(), held=(), after=(), vmem=8, cost=0, name=None
):
    vspec = pl.BlockSpec(memory_space=pltpu.VMEM)
    sspec = pl.BlockSpec(memory_space=pltpu.SMEM)
    aspec = pl.BlockSpec(memory_space=pl.ANY)
    hspec = pl.BlockSpec(memory_space=pltpu.HBM)
    skip = len(after)

    def body(*refs):
        kernel(*refs[skip:])

    specs = [sspec if n in smem else hspec if n in held else vspec for n in range(len(args))]
    return pl.pallas_call(
        body,
        out_shape=out_shape,
        in_specs=[aspec] * skip + specs,
        out_specs=jax.tree.map(lambda _: vspec, out_shape),
        scratch_shapes=list(scratch),
        compiler_params=pltpu.CompilerParams(vmem_limit_bytes=vmem * MIB),
        cost_estimate=pl.CostEstimate(flops=cost * 1_150_000_000, bytes_accessed=0, transcendentals=0),
        name=name,
    )(*after, *args)


def sds(shape, dtype):
    return jax.ShapeDtypeStruct(shape, dtype)


def low_half(rows):
    return lax.broadcasted_iota(jnp.int32, (rows, 128), 1) < 64


def prep_kernel(
    wq, wk, wv, wg, wu, tok, seg, g1, g2, s0, s1, s2, s3, ts, gains, slabs, vq, vk, vv, vg, vu, sems
):
    j_me = lax.axis_index("blk")
    rows = wq.shape[0]
    pairs = ((wq, vq), (wk, vk), (wv, vv), (wg, vg), (wu, vu), (tok, ts.at[0:T]))
    copies = [pltpu.make_async_copy(a, b, sems.at[n]) for n, (a, b) in enumerate(pairs)]
    for copy in copies:
        copy.start()
    eye = lax.broadcasted_iota(jnp.int32, (rows, rows), 0) == lax.broadcasted_iota(
        jnp.int32, (rows, rows), 1
    )
    columns = []
    for n, ref in enumerate((g1, g2)):
        row = jnp.broadcast_to(ref[...].astype(F32).reshape(1, rows), (rows, rows))
        column = jnp.sum(jnp.where(eye, row, 0.0), axis=1, keepdims=True)
        columns.append(column)
        gains[n] = jnp.broadcast_to(column, (rows, 128))
    ids = jnp.broadcast_to(seg[...], (16, T))
    ts[T : T + 16, 0:T] = (ids // 2).astype(F32).astype(BF16)
    ts[T : T + 16, T : 2 * T] = (ids % 2).astype(F32).astype(BF16)
    ts[T : T + 16, 2 * T : 3 * T] = jnp.zeros((16, T), BF16)
    low = low_half(rows)
    lane = lax.broadcasted_iota(jnp.int32, (rows, 128), 1)
    spare = jnp.where(lane == 64, columns[0], jnp.where(lane == 65, columns[1], 0.0))
    for copy in copies:
        copy.wait()

    def tile(ref, index):
        return ref[:, 128 * index : 128 * index + 128].astype(F32)

    for j in range(TP):
        first, second = [], []
        for ref in (vq, vk, vv):
            at = 192 * j // 128
            a, b = tile(ref, at), tile(ref, at + 1)
            if j % 2:
                a, b = pltpu.roll(a, 64, 1), pltpu.roll(b, 64, 1)
                a = jnp.where(low, a, b)
            first.append(a)
            second.append(b)
        tiles = first + [
            jnp.where(low, second[0], pltpu.roll(second[1], 64, 1)),
            jnp.where(low, second[2], spare),
        ]
        for ref in (vg, vu):
            for t in range(4):
                a = tile(ref, 4 * t + j // 2)
                b = tile(ref, 4 * t + 2 + j // 2)
                if j % 2:
                    tiles.append(jnp.where(low, pltpu.roll(a, 64, 1), b))
                else:
                    tiles.append(jnp.where(low, a, pltpu.roll(b, 64, 1)))
        for n, v in enumerate(tiles):
            slabs[j ^ j_me, :, 128 * n : 128 * n + 128] = v.astype(BF16)
    for k, ref in enumerate((s0, s1, s2, s3)):
        ref[...] = slabs[k]


def pack_kernel(s0, s1, s2, s3, wo, first, whole, vo, sem):
    j = lax.axis_index("blk")
    rows = s0.shape[0]
    copy = pltpu.make_async_copy(wo, vo, sem)
    copy.start()
    for k, ref in enumerate((s0, s1, s2, s3)):
        whole[pl.ds(pl.multiple_of(rows * (j ^ k), 8), rows)] = ref[:, 0:640].astype(F32)
    first[0:96] = whole[...].astype(BF16)
    copy.wait()
    out = vo[...].astype(F32)
    rest = [out[8 * n : 8 * n + 8, 640:768] for n in range(3)]
    rest = jnp.concatenate(rest + [jnp.zeros((8, 256), F32)], axis=1)
    first[96:128] = jnp.concatenate([out[:, 0:640], rest], axis=0).astype(BF16)


def pack_more_kernel(s0, s1, s2, s3, wd, second, whole, vd, sem):
    j = lax.axis_index("blk")
    rows = s0.shape[0]
    copy = pltpu.make_async_copy(wd, vd, sem)
    copy.start()
    for k, ref in enumerate((s0, s1, s2, s3)):
        whole[pl.ds(pl.multiple_of(rows * (j ^ k), 8), rows)] = ref[:, 640:1664].astype(F32)
    for n in range(4):
        second[96 * n : 96 * n + 96] = whole[:, 256 * n : 256 * n + 256].astype(BF16)
    copy.wait()
    for n in range(3):
        second[384 + 64 * n : 448 + 64 * n] = vd[:, 256 * n : 256 * n + 256]


def stripes_kernel(p0, p1, p2, p3, p4, p5, p6, p7, out, whole):
    dp = lax.axis_index("dp")
    for n, ref in enumerate((p0, p1, p2, p3, p4, p5, p6, p7)):
        at = pl.ds(pl.multiple_of(24 * (dp ^ piece_at(n)), 8), 24)
        part = ref[96:128].astype(F32)
        whole[at, 0:640] = part[0:24]
        rest = [part[24:32, 128 * m : 128 * m + 128] for m in range(3)]
        whole[at, 640:768] = jnp.concatenate(rest, axis=0)
    out[...] = whole[...].astype(BF16)


def out_weight_kernel(p0, p1, p2, p3, out, whole):
    j = lax.axis_index("blk")
    for k, ref in enumerate((p0, p1, p2, p3)):
        rows = ref[...].astype(F32)
        for d in range(8):
            at = pl.multiple_of(24 * (TP * d + (j ^ k)), 8)
            whole[pl.ds(at, 24)] = rows[24 * d : 24 * d + 24]
    for k in range(TP):
        at = pl.multiple_of(192 * (j ^ k), 64)
        out[128 * k : 128 * k + 128] = whole[pl.ds(at, 128)].astype(BF16)
        out[512 + 64 * k : 576 + 64 * k] = whole[pl.ds(at + 128, 64)].astype(BF16)


def bias_kernel(table, out):
    j = lax.axis_index("blk")
    lane = lax.broadcasted_iota(jnp.int32, (8, 512), 1)
    for n in range(3):
        off = (n - 1) * T
        rel = jnp.where(lane < 256, off - lane, off + 512 - lane)
        bucket = bucket_of(rel)
        for h in range(HT):
            row = jnp.zeros((8, 512), F32)
            for b in range(NB):
                row = jnp.where(bucket == b, table[HT * j + h, b], row)
            wide = jnp.broadcast_to(row[0:1], (T, 512))
            out[h, n] = pltpu.roll(wide, 0, 1, stride=1, stride_axis=0)[:, :T]


def piece_at(n):
    return 2 * (n % 4) + n // 4


def qkv_kernel(
    t0, t1, t2, t3, p0, p1, p2, p3, p4, p5, p6, p7, tok, n1, qkv, w, gains, segq, segk
):
    j = lax.axis_index("blk")
    dp = lax.axis_index("dp")
    for k, ref in enumerate((t0, t1, t2, t3)):
        tok[j ^ k] = ref[0:T]
        parts = ref[T : T + 16].astype(F32)
        row = (2.0 * parts[:, 0:T] + parts[:, T : 2 * T])[0:8]
        segq[j ^ k] = row
        col = jnp.transpose(jnp.broadcast_to(row[0:1], (128, T)))
        segk[j ^ k, :, 0:128] = col
        segk[j ^ k, :, 128:256] = col
    for n, ref in enumerate((p0, p1, p2, p3, p4, p5, p6, p7)):
        w[pl.ds(pl.multiple_of(96 * (dp ^ piece_at(n)), 32), 96)] = ref[0:96]
    turned = jnp.transpose(w[:, 512:640].astype(F32))
    gains[...] = turned[64:72]

    def body(b, carry):
        x = tok[b].astype(F32)
        rstd = lax.rsqrt(jnp.mean(x * x, axis=-1, keepdims=True) + EPSILON)
        n = (x * rstd * gains[0:1]).astype(BF16)
        n1[b] = n
        y = dot(n, w[...])
        for t in range(5):
            qkv[t, b] = y[:, 128 * t : 128 * t + 128].astype(BF16)
        return carry

    lax.fori_loop(0, TP, body, 0)


def attn_fwd_kernel(h, table, bias, qkv, segq, segk, prob, inv_tot, out_t, qt, vt, sc):
    j_me = lax.axis_index("blk")
    rows_low = lax.broadcasted_iota(jnp.int32, (128, T), 0) < 64
    half = slice(64, 128) if h == 1 else slice(0, 64)
    for i in range(TP):
        if h < 2:
            q = jnp.transpose(qkv[0, i].astype(F32))
        else:
            q = jnp.transpose(pltpu.roll(qkv[3, i].astype(F32), 64, 1))
        qt[i] = jnp.where(rows_low == (h == 0), q, 0.0).astype(BF16)
        v = jnp.transpose(qkv[2 + 2 * (h // 2), i].astype(F32)).astype(BF16)
        vt[:, T * i : T * i + T] = v[half]

    tile = 1 + 2 * (h // 2)
    far = (table[HT * j_me + h, 15], table[HT * j_me + h, 31])
    for i in range(TP):
        peak = jnp.full((1, T), MASKED, F32)
        for j in range(TP):
            s = dot(qkv[tile, j], qt[i])
            if abs(j - i) <= 1:
                s = s + bias[h, j - i + 1]
            else:
                s = s + far[j > i]
            if i in (0, TP - 1) or j in (0, TP - 1):
                s = jnp.where(segk[j] == segq[i, 0:1], s, MASKED)
            sc[j] = s
            peak = jnp.maximum(peak, jnp.max(s, axis=0, keepdims=True))
        total = jnp.zeros((1, T), F32)
        for j in range(TP):
            p = jnp.exp(sc[j] - peak)
            total = total + jnp.sum(p, axis=0, keepdims=True)
            prob[i, j] = p.astype(BF16)
        inv = 1.0 / total
        inv_tot[i] = inv
        out_t[:, T * i : T * i + T] = dot(vt[...], prob[i].reshape(TP * T, T)) * inv


def join_kernel(o0, o1, o2, att):
    for b in range(TP):
        at = slice(T * b, T * b + T)
        both = jnp.concatenate([o0[:, at], o1[:, at]], axis=0)
        att[at, :] = jnp.transpose(both).astype(BF16)
    for b in range(2):
        both = [o2[:, T * c : T * c + T] for c in (b, b + 2)]
        att[1024 + T * b : 1280 + T * b, :] = jnp.transpose(jnp.concatenate(both, axis=0)).astype(BF16)


def put_pair(keep, give, k, value):
    @pl.when(k % 2 == 0)
    def _():
        keep[k // 2] = value

    @pl.when(k % 2 == 1)
    def _():
        give[k // 2] = value


def units_kernel(p0, p1, p2, p3, p4, p5, p6, p7, wgu, wd):
    dp = lax.axis_index("dp")
    for n, ref in enumerate((p0, p1, p2, p3, p4, p5, p6, p7)):
        at = dp ^ piece_at(n)
        rows = pl.ds(pl.multiple_of(96 * at, 32), 96)
        for m in range(4):
            wgu[rows, 256 * m : 256 * m + 256] = ref[96 * m : 96 * m + 96]
        rows = pl.ds(pl.multiple_of(64 * at, 64), 64)
        for m in range(3):
            wd[rows, 256 * m : 256 * m + 256] = ref[384 + 64 * m : 448 + 64 * m]


def ffn_kernel(
    ks, a0, a1, a2, a3, gains, wop, wgu, wd, tok, c0, c1,
    n2, hid, ggug, keep, give, attc, mixed_own,
):
    j = lax.axis_index("blk")
    low = low_half(T)
    refs = (a0, a1, a2, a3)
    for m, k in enumerate(ks):
        b = j ^ k
        half = b // 2
        for n, ref in enumerate(refs):
            attc[m, :, 128 * n : 128 * n + 128] = ref[pl.ds(pl.multiple_of(b * T, T), T)]
        rest = [
            ref[pl.ds(pl.multiple_of(1024 + (b % 2) * T, T), T)].astype(F32) for ref in refs
        ]
        for n in range(2):
            lo = pltpu.roll(rest[2 * n], 64 * half, 1)
            hi = pltpu.roll(rest[2 * n + 1], 64 * (1 - half), 1)
            attc[m, :, 512 + 128 * n : 640 + 128 * n] = jnp.where(low, lo, hi).astype(BF16)
        mixed = tok[b].astype(F32) + dot(attc[m], wop[...])
        if k == 0:
            mixed_own[...] = mixed
        rstd = lax.rsqrt(jnp.mean(mixed * mixed, axis=-1, keepdims=True) + EPSILON)
        n = (mixed * rstd * gains[1:2]).astype(BF16)
        n2[m] = n
        gate = dot(n, wgu[:, 0:512])
        up = dot(n, wgu[:, 512:1024])
        c = 0.7978845608028654
        sq = gate * gate
        th = jnp.tanh(c * gate * (1.0 + 0.044715 * sq))
        act = 0.5 * gate * (1.0 + th)
        slope = 0.5 * (1.0 + th) + 0.5 * gate * (1.0 - th * th) * (c * (1.0 + 3 * 0.044715 * sq))
        hid[m] = (act * up).astype(BF16)
        hg = dot_nt((c0, c1)[m][...], wd[...])
        ggug[m, :, 0:512] = (hg * up * slope).astype(BF16)
        ggug[m, :, 512:1024] = (hg * act).astype(BF16)
        (keep, give)[m][...] = dot_nt(ggug[m], wgu[...]).astype(BF16)


def mid_kernel(keep, rc, rx, mixed_own, cot, attc, wop, gains, mixed_grad, g0, g1, g2, g3, wo_keep, wo_one, wo_three, dw):
    j = lax.axis_index("blk")
    u = (keep[...].astype(F32) + rc[...].astype(F32) + rx[...].astype(F32)) * gains[1:2]
    mixed = mixed_own[...]
    rstd = lax.rsqrt(jnp.mean(mixed * mixed, axis=-1, keepdims=True) + EPSILON)
    n = mixed * rstd
    mg = cot[...].astype(F32) + rstd * (u - n * jnp.mean(u * n, axis=-1, keepdims=True))
    mixed_grad[...] = mg
    ml = mg.astype(BF16)
    ag = dot_nt(ml, wop[...])
    low = low_half(128)
    for k, ref in enumerate((g0, g1, g2, g3)):
        ref[0:256] = ag[:, 128 * k : 128 * k + 128].astype(BF16)
        rest = ag[:, 512 + 128 * (k // 2) : 640 + 128 * (k // 2)]
        top, bottom = rest[0:128], rest[128:256]
        if k % 2 == 0:
            v = jnp.where(low, top, pltpu.roll(bottom, 64, 1))
        else:
            v = jnp.where(low, pltpu.roll(top, 64, 1), bottom)
        ref[256:384] = v.astype(BF16)
    perm = dot_tn(attc[0], ml)
    for k in range(TP):
        at = pl.multiple_of(192 * (j ^ k), 64)
        dw[pl.ds(at, 128)] = perm[128 * k : 128 * k + 128]
        dw[pl.ds(at + 128, 64)] = perm[512 + 64 * k : 512 + 64 * k + 64]
    for k in range(TP):
        ref = (wo_keep.at[0], wo_one, wo_keep.at[1], wo_three)[k]
        for d in range(8):
            at = pl.multiple_of(24 * (TP * d + (j ^ k)), 8)
            ref[d] = dw[pl.ds(at, 24)].astype(BF16)


SLOTS = (0, 2, 1, 3)
FIRST = 3 * 96
SECOND = 2 * 96 + 6 * 24
TAIL = 16


def slots(body):
    dp = lax.axis_index("dp")
    for give in range(2):
        for slot, z in enumerate(SLOTS):
            body(give, slot, dp ^ (2 * z + give))


def ffn_dw_kernel(
    na, ga, ha, nb, gb, hb, c0, c1, c2, c3, wd, y_keep, y_give, z_keep, z_give, lo_keep, lo_give, dwgu, dwd
):
    for m in range(2):
        at = slice(512 * m, 512 * m + 512)
        dwgu[:, at] = dot_tn(na[...], ga[:, at]) + dot_tn(nb[...], gb[:, at])
    for m in range(3):
        at = slice(256 * m, 256 * m + 256)
        dwd[:, at] = (
            dot_tn(ha[0:T], c2[:, at])
            + dot_tn(ha[T : 2 * T], c3[:, at])
            + dot_tn(hb[0:T], c0[:, at])
            + dot_tn(hb[T : 2 * T], c1[:, at])
        )
    for n, ref in enumerate((hb, ha)):
        lo_keep[n] = dot(ref[0:T], wd[...]).astype(BF16)
        lo_give[n] = dot(ref[T : 2 * T], wd[...]).astype(BF16)

    def put(g, slot, owner):
        ref = y_give if g else y_keep
        a = pl.ds(pl.multiple_of(96 * owner, 32), 96)
        for m in range(3):
            ref[slot, 96 * m : 96 * m + 96] = dwgu[a, 256 * m : 256 * m + 256].astype(BF16)
        ref = z_give if slot > 1 else z_keep
        slot = 2 * (slot % 2) + g
        ref[slot, 0:96] = dwgu[a, 768:1024].astype(BF16)
        a = pl.ds(pl.multiple_of(64 * owner, 64), 64)
        for m in range(3):
            ref[slot, 96 + 64 * m : 160 + 64 * m] = dwd[a, 256 * m : 256 * m + 256].astype(BF16)

    slots(put)


def ffn_second_kernel(y_keep, y_got, z_keep, z_got, y_next, y_give, z_next, z_give):
    for keep, got, rest, give in ((y_keep, y_got, y_next, y_give), (z_keep, z_got, z_next, z_give)):
        rest[...] = (keep[0:2].astype(F32) + got[0:2].astype(F32)).astype(BF16)
        give[...] = (keep[2:4].astype(F32) + got[2:4].astype(F32)).astype(BF16)


def ffn_third_kernel(y_keep, y_got, z_keep, z_got, y_give, z_give):
    y_give[...] = (y_keep[1].astype(F32) + y_got[1].astype(F32)).astype(BF16)
    z_give[...] = (z_keep[1].astype(F32) + z_got[1].astype(F32)).astype(BF16)


def split(x):
    high = x.astype(BF16).astype(F32)
    return jnp.concatenate([high, x - high], axis=0).astype(BF16)


def first_dw_kernel(n1, dqkv, keep, give, dw):
    for t in range(3):
        at = slice(128 * t, 128 * t + 128)
        dw[:, at] = dot_tn(n1[...], dqkv[:, at])

    def put(g, slot, owner):
        ref = give if g else keep
        a = pl.ds(pl.multiple_of(96 * owner, 32), 96)
        for t in range(3):
            at = FIRST * slot + 96 * t
            ref[at : at + 96] = dw[a, 128 * t : 128 * t + 128].astype(BF16)

    slots(put)


def second_dw_kernel(n1, dqkv, wo_keep, wo_got, wo_along, ta, tb, keep, give, dw, wo, chunk):
    for t in range(2):
        at = slice(128 * t, 128 * t + 128)
        dw[:, at] = dot_tn(n1[...], dqkv[:, at])
    for d in range(8):
        wo[d] = wo_keep[0, d].astype(F32) + wo_got[d].astype(F32) + wo_along[d].astype(F32)

    def put(g, slot, owner):
        ref = give if g else keep
        a = pl.ds(pl.multiple_of(96 * owner, 32), 96)
        for t in range(2):
            chunk[96 * t : 96 * t + 96] = dw[a, 128 * t : 128 * t + 128]
        for t in range(6):
            chunk[192 + 24 * t : 216 + 24 * t] = wo[owner, :, 128 * t : 128 * t + 128]
        ref[SECOND * slot : SECOND * slot + SECOND] = chunk[...].astype(BF16)

    slots(put)
    for ref in (keep, give):
        ref[4 * SECOND : 4 * SECOND + 16] = split(ta[...] + tb[...])


def tail_of(ref, base):
    both = ref[base : base + 16].astype(F32)
    return both[0:8] + both[8:16]


def stage_kernel(n, chunk, keep, got, next_keep, next_give):
    half = n // 2 * chunk
    for at, ref in ((0, next_keep), (half, next_give)):
        here = slice(at, at + half)
        ref[0:half] = (keep[here].astype(F32) + got[here].astype(F32)).astype(BF16)
        if chunk == SECOND:
            ref[half : half + 16] = split(tail_of(keep, n * chunk) + tail_of(got, n * chunk))


def first_back_kernel(ka, ga, yk, yg, ya, zk, zg, za, dwd, b0, b1, b2, b3, total, ffn):
    j = lax.axis_index("blk")
    ffn[0:288] = yk[0].astype(F32) + yg[0].astype(F32) + ya[...].astype(F32)
    ffn[288:576] = zk[0].astype(F32) + zg[0].astype(F32) + za[...].astype(F32)
    for m in range(3):
        dwd[:, 256 * m : 256 * m + 256] = ffn[384 + 64 * m : 448 + 64 * m]
    total[...] = ka[...].astype(F32) + ga[...].astype(F32)
    for k, ref in enumerate((b0, b1, b2, b3)):
        for t in range(3):
            part = total[pl.ds(pl.multiple_of(96 * t + 24 * (j ^ k), 8), 24)]
            ref[:, 128 * t : 128 * t + 128] = part.astype(BF16)
        for m in range(4):
            part = ffn[pl.ds(pl.multiple_of(96 * m + 24 * (j ^ k), 8), 24)]
            ref[:, 384 + 256 * m : 640 + 256 * m] = part.astype(BF16)


def second_back_kernel(kb, gb, dwo, b0, b1, b2, b3, total):
    j = lax.axis_index("blk")
    total[...] = kb[0:SECOND].astype(F32) + gb[0:SECOND].astype(F32)
    parts = split(tail_of(kb, SECOND) + tail_of(gb, SECOND)).astype(F32)
    parts = jnp.concatenate([parts, jnp.zeros((8, 128), F32)], axis=0).astype(BF16)
    for t in range(6):
        at = 192 + 24 * t
        dwo[:, 128 * t : 128 * t + 128] = total[at : at + 24]
    for k, ref in enumerate((b0, b1, b2, b3)):
        for t in range(2):
            part = total[pl.ds(pl.multiple_of(96 * t + 24 * (j ^ k), 8), 24)]
            ref[:, 128 * t : 128 * t + 128] = part.astype(BF16)
        ref[:, 256:384] = parts


def attn_bwd_kernel(second, *refs):
    count = 1 if second else 2
    heads = range(HT - 1, HT) if second else range(2)
    qkv, refs = refs[0], refs[1:]
    probs, refs = refs[:count], refs[count:]
    invs, refs = refs[:count], refs[count:]
    outs, refs = refs[:count], refs[count:]
    (g0, g1, g2, g3, dqkv, table_grad,
     dotm, dom, qm, ktm, delta, dst, dq_acc, dk_acc, dv_acc, near, far) = refs
    j_me = lax.axis_index("blk")
    low = low_half(T)
    rows_low = lax.broadcasted_iota(jnp.int32, (128, T), 0) < 64

    for k, ref in enumerate((g0, g1, g2, g3)):
        b = j_me ^ k
        if second:
            rest = ref[256:384].astype(F32)
            rows = jnp.concatenate([rest, pltpu.roll(rest, 64, 1)], axis=0)
            turned = jnp.where(rows_low, jnp.transpose(rows) * invs[0][b], 0.0)
        else:
            turned = jnp.transpose(ref[0:256].astype(F32))
            turned = turned * jnp.where(rows_low, invs[0][b], invs[1][b])
        turned = turned.astype(BF16).astype(F32)
        back = jnp.transpose(turned)
        for n in range(count):
            dotm[n, b] = jnp.where(rows_low == (n == 0), turned, 0.0).astype(BF16)
            dom[n, b] = jnp.where(low == (n == 0), back, 0.0).astype(BF16)

    for i in range(TP):
        at = slice(T * i, T * i + T)
        if second:
            q = pltpu.roll(qkv[3, i].astype(F32), 64, 1)
            keys = jnp.transpose(q)
        else:
            q = qkv[0, i].astype(F32)
            keys = jnp.transpose(qkv[1, i].astype(F32))
        for n in range(count):
            g = dotm[n, i].astype(F32)[64 * n : 64 * n + 64]
            delta[n, i] = jnp.sum(outs[n][:, at] * g, axis=0, keepdims=True)
            qm[n, i] = jnp.where(low == (n == 0 and not second), q, 0.0).astype(BF16)
            ktm[n, :, at] = jnp.where(rows_low == (n == 0), keys, 0.0).astype(BF16)

    dq_acc[...] = jnp.zeros(dq_acc.shape, F32)
    dk_acc[...] = jnp.zeros(dk_acc.shape, F32)
    dv_acc[...] = jnp.zeros(dv_acc.shape, F32)
    table_grad[...] = jnp.zeros(table_grad.shape, F32)
    key_at = lax.broadcasted_iota(jnp.int32, (128, 128), 0)
    query_at = lax.broadcasted_iota(jnp.int32, (128, 128), 1)
    upper = query_at >= key_at
    turn = (key_at + query_at == 127).astype(F32)

    def diagonals(m):
        m = lax.dot_general(
            turn, m, (((1,), (0,)), ((), ())), precision=HIGHEST, preferred_element_type=F32
        )
        return jnp.sum(pltpu.roll(m, 1, 1, stride=1, stride_axis=0), axis=0, keepdims=True)

    row_id = lax.broadcasted_iota(jnp.int32, (NB, 128), 0)
    lane_id = lax.broadcasted_iota(jnp.int32, (NB, 128), 1)
    hot_neg = bucket_of(-lane_id) == row_id
    hot_pos = bucket_of(128 - lane_id) == row_id

    for n, prob in enumerate(probs):
        near[...] = jnp.zeros(near.shape, F32)
        far[...] = jnp.zeros(far.shape, F32)
        for i in range(TP):
            at = slice(T * i, T * i + T)
            row_delta = delta[n, i]
            for j in range(TP):
                dp = dot(qkv[2 + 2 * second, j], dotm[n, i])
                ds = prob[i, j].astype(F32) * (dp - row_delta)
                dst[j] = ds.astype(BF16)
                for a in range(2):
                    for c in range(2):
                        gap = 2 * (j - i) + a - c
                        part = ds[128 * a : 128 * a + 128, 128 * c : 128 * c + 128]
                        if abs(gap) <= 1:
                            near[gap + 1] += part
                        else:
                            far[int(gap > 0)] += jnp.sum(part.reshape(16, 8, 128), axis=0)
            d_all = dst[...].reshape(TP * T, T)
            dq_acc[:, at] += dot(ktm[n], d_all)
            dk_acc[...] += dot(d_all, qm[n, i])
            dv_acc[...] += dot(prob[i].reshape(TP * T, T), dom[n, i])
        before, diagonal, after = near[0], near[1], near[2]
        neg = jnp.where(upper, diagonal, before)
        pos = jnp.where(upper, after, diagonal)
        neg, pos = diagonals(neg), diagonals(pos)
        far_neg = jnp.sum(far[0], axis=0, keepdims=True) + jnp.sum(
            jnp.where(upper, before, 0.0), axis=0, keepdims=True
        )
        far_pos = jnp.sum(far[1], axis=0, keepdims=True) + jnp.sum(
            jnp.where(upper, 0.0, after), axis=0, keepdims=True
        )
        spread = (
            jnp.where(hot_neg, neg, 0.0)
            + jnp.where(hot_pos, pos, 0.0)
            + jnp.where(row_id == 15, far_neg, 0.0)
            + jnp.where(row_id == 31, far_pos, 0.0)
        )
        sums = jnp.sum(spread, axis=1, keepdims=True)
        sums = jnp.sum(jnp.where(lane_id == row_id, sums, 0.0), axis=0, keepdims=True)
        h = heads[n]
        table_grad[h : h + 1] = sums
    for i in range(TP):
        at = slice(T * i, T * i + T)
        dq = jnp.transpose(dq_acc[:, at])
        if second:
            parts = (dq + dk_acc[at], dv_acc[at])
        else:
            parts = (dq, dk_acc[at], dv_acc[at])
        for n, part in enumerate(parts):
            dqkv[i, :, 128 * n : 128 * n + 128] = part.astype(BF16)


def one_grad_kernel(da, db, w, keep, give):
    j = lax.axis_index("blk")

    def body(k, carry):
        total = dot_nt(da[j ^ k], w[:, 0:384]) + dot_nt(db[j ^ k], w[:, 384:640])
        put_pair(keep, give, k, total.astype(BF16))
        return carry

    lax.fori_loop(0, TP, body, 0)


def finish(parts, w, out, gain):
    total = jnp.zeros((w.shape[0], 128), F32)
    for n, part in enumerate(parts):
        at = slice(128 * n, 128 * n + 128)
        total = total + part * w[:, at].astype(F32)
        out[:, at] = part
    return jnp.sum(total, axis=1, keepdims=True) / gain


def put_row(ref, wide):
    rows = wide.shape[0]
    row_id = lax.broadcasted_iota(jnp.int32, (rows, 128), 0)
    eye = row_id == lax.broadcasted_iota(jnp.int32, (rows, 128), 1)
    ref[...] = jnp.sum(jnp.where(eye, wide, 0.0), axis=0, keepdims=True)[:, 0:rows]


def first_final_kernel(b0, b1, b2, b3, gains, wg, wu, dg, du, gg2, mark, src):
    mark[...] = jnp.zeros((8, 128), F32)
    j_me = lax.axis_index("blk")
    low = low_half(wg.shape[0])
    for k, ref in enumerate((b0, b1, b2, b3)):
        src[j_me ^ k] = ref[:, 384:1408].astype(F32)
    gain_grad = 0.0
    for n, (w, out) in enumerate(((wg, dg), (wu, du))):
        parts = [None] * 16
        for t in range(4):
            at = slice(512 * n + 128 * t, 512 * n + 128 * t + 128)
            for half in range(2):
                a, b = src[2 * half, :, at], src[2 * half + 1, :, at]
                parts[4 * t + half] = jnp.where(low, a, pltpu.roll(b, 64, 1))
                parts[4 * t + 2 + half] = jnp.where(low, pltpu.roll(a, 64, 1), b)
        gain_grad = gain_grad + finish(parts, w, out, gains[1])
    put_row(gg2, gain_grad)


def second_final_kernel(
    a0, a1, a2, a3, b0, b1, b2, b3, gains, wq, wk, wv, dq, dk, dv, gg1, table, src
):
    j_me = lax.axis_index("blk")
    low = low_half(wq.shape[0])
    heads = jnp.zeros((128, 128), F32)
    head_id = lax.broadcasted_iota(jnp.int32, (128, 128), 0)
    for k, (first, second) in enumerate(zip((a0, a1, a2, a3), (b0, b1, b2, b3))):
        src[j_me ^ k, :, 0:384] = first[:, 0:384].astype(F32)
        src[j_me ^ k, :, 384:640] = second[:, 0:256].astype(F32)
        parts = second[:, 256:384].astype(F32)
        for h in range(HT):
            row = parts[h : h + 1] + parts[8 + h : 9 + h]
            heads = jnp.where(head_id == HT * (j_me ^ k) + h, row, heads)
    table[...] = heads[0:H, 0:NB]

    def one(j, n):
        return src[j, :, 128 * n : 128 * n + 128]

    gain_grad = 0.0
    for n, (w, out) in enumerate(((wq, dq), (wk, dk), (wv, dv))):
        parts = []
        for j in range(0, TP, 2):
            rest = []
            for m in (j, j + 1):
                last = one(m, 4 if n == 2 else 3)
                rest.append(pltpu.roll(last, 64, 1) if n == 1 else last)
            mid = pltpu.roll(one(j + 1, n), 64, 1)
            parts += [
                one(j, n),
                jnp.where(low, rest[0], mid),
                jnp.where(low, mid, pltpu.roll(rest[1], 64, 1)),
            ]
        gain_grad = gain_grad + finish(parts, w, out, gains[0])
    put_row(gg1, gain_grad)


def close_kernel(keep, got, along, mixed_grad, tok, gains, tokens_grad, mark):
    mark[...] = jnp.zeros((8, 128), F32)
    x = tok[lax.axis_index("blk")].astype(F32)
    rstd = lax.rsqrt(jnp.mean(x * x, axis=-1, keepdims=True) + EPSILON)
    n = x * rstd
    u = (keep[0].astype(F32) + got[0].astype(F32) + along[...].astype(F32)) * gains[0:1]
    grad = rstd * (u - n * jnp.mean(u * n, axis=-1, keepdims=True))
    tokens_grad[...] = mixed_grad[...] + grad


AXES = ("dp", "blk")
COST = {"qkv": 0, "attn_fwd": (0, 0, 0), "units": 15, "ffn": 0, "ffn_dw": 0, "mid": 0, "attn_bwd": (0, 10), "one_grad": 40, "stage_y": 0, "stage_z": 10, "first_back": 0}


def group_local(
    n_dp, n_blk,
    tokens, segment_ids, w_query, w_key, w_value, w_attn_out, attn_gain, rel_bias,
    w_gate, w_up, w_down, ffn_gain, cotangent,
):
    n_dev = n_dp * n_blk

    def later(x, *others):
        return lax.optimization_barrier((x,) + others)[0]

    def swap(x, mask):
        return lax.ppermute(x, AXES, [(d, d ^ mask) for d in range(n_dev)])

    def share(x, *others):
        along = swap(x, 2)
        return (x, swap(x, 1), along, swap(later(along, *others), 1))

    def reduce_pair(keep, give):
        got = swap(give, 1)
        return got, swap(keep[1] + got[1], 2)

    def round_one(x):
        return lax.optimization_barrier((swap(x, 16), swap(x, 8), swap(x, 4)))

    def round_two(far, near):
        return lax.optimization_barrier((swap(far, 8), swap(near, 4), swap(far, 4)))

    def gathered(x, one, two, *others):
        far, near, other = one
        last, near_y, far_y = two
        return (x, near, far, last, other, near_y, far_y, swap(later(last, *others), 4))

    tok_own, cot_own = tokens[0], cotangent[0]
    rows, ff = w_query.shape[0], w_gate.shape[1]
    flat = TP * T
    table = rel_bias.astype(F32).T

    *slabs, tok_seg, gain_cols = call(
        prep_kernel,
        (sds((rows, 1664), BF16),) * TP + (sds((T + 16, D), BF16), sds((2, rows, 128), F32)),
        w_query, w_key, w_value, w_gate, w_up, tok_own, segment_ids, attn_gain, ffn_gain,
        name="prep", vmem=60, held=(0, 1, 2, 3, 4, 5),
        scratch=(
            pltpu.VMEM((TP, rows, 1664), BF16),
            *(pltpu.VMEM((rows, D), BF16),) * 3,
            *(pltpu.VMEM((rows, ff), BF16),) * 2,
            pltpu.SemaphoreType.DMA((6,)),
        ),
    )
    toks_x, toks_c = swap(tok_seg, 2), swap(tok_seg, 1)
    slabs = (slabs[0], swap(slabs[1], 1), swap(slabs[2], 2), swap(slabs[3], 3))
    first = call(
        pack_kernel, sds((128, 640), BF16), *slabs, w_attn_out,
        name="pack", vmem=30, held=(4,),
        scratch=(pltpu.VMEM((96, 640), F32), pltpu.VMEM((rows, D), BF16), pltpu.SemaphoreType.DMA),
    )
    second = call(
        pack_more_kernel, sds((576, 256), BF16), *slabs, w_down,
        name="pack_more", vmem=30, held=(4,), after=(first,),
        scratch=(pltpu.VMEM((96, 1024), F32), pltpu.VMEM((64, D), BF16), pltpu.SemaphoreType.DMA),
    )
    first_one = round_one(first)
    bias = call(
        bias_kernel, sds((HT, 3, T, T), F32), table, smem=(0,), name="bias", after=(second,)
    )
    far, near = lax.optimization_barrier(first_one + (second, bias))[:2]
    first_two = round_two(far, near)
    toks_r = swap(later(toks_x, *first_two), 1)
    firsts = gathered(first, first_one, first_two, *())
    toks = (tok_seg, toks_c, toks_x, toks_r)
    second_one = (
        swap(later(second, *first_one), 16),
        swap(later(second, *first_two), 8),
        swap(later(second, *first_two), 4),
    )

    tok, n1, qkv, w_qkv, gains, segq, segk = call(
        qkv_kernel,
        (
            sds((TP, T, D), BF16), sds((TP, T, D), BF16), sds((5, TP, T, 128), BF16),
            sds((D, 640), BF16), sds((8, D), F32), sds((TP, 8, T), F32), sds((TP, T, T), F32),
        ),
        *toks, *firsts, name="qkv", vmem=16, cost=COST["qkv"],
    )
    stripes = call(
        stripes_kernel, sds((192, D), BF16), *firsts, name="stripes", after=(segq,),
        scratch=(pltpu.VMEM((192, D), F32),),
    )
    stripes = share(stripes)
    wop = call(
        out_weight_kernel, sds((D, D), BF16), *stripes, name="out_weight",
        scratch=(pltpu.VMEM((D, D), F32),),
    )
    cots_x = swap(later(cot_own, *(gains,)), 2)
    heads = []
    for h in range(HT):
        heads.append(
            call(
                functools.partial(attn_fwd_kernel, h),
                (sds((TP, TP, T, T), BF16), sds((TP, 1, T), F32), sds((DH, flat), F32)),
                table, bias, qkv, segq, segk, smem=(0,), name="attn_fwd", vmem=14,
                cost=COST["attn_fwd"][h], after=((heads[-1][1],) if heads else ()) + ((cots_x,) if h == 2 else ()),
                scratch=(
                    pltpu.VMEM((TP, 128, T), BF16),
                    pltpu.VMEM((DH, flat), BF16),
                    pltpu.VMEM((TP, T, T), F32),
                ),
            )
        )
    probs, inv_tots, out_ts = zip(*heads)
    cots = (cot_own, swap(later(cot_own, inv_tots[2]), 1), cots_x, swap(later(cots_x, inv_tots[2]), 1))
    far, near = lax.optimization_barrier(second_one + (inv_tots[0],))[:2]
    second_two = round_two(far, near)
    seconds = gathered(second, second_one, second_two)
    att = call(join_kernel, sds((1536, 128), BF16), *out_ts, name="join")
    atts = share(att, wop)
    wgu, wd = call(
        units_kernel, (sds((D, 1024), BF16), sds((512, D), BF16)), *seconds, name="units",
        cost=COST["units"],
    )

    def ffn(ks, *after):
        return call(
            functools.partial(ffn_kernel, ks),
            (
                sds((2, T, D), BF16), sds((2, T, 512), BF16), sds((2, T, 1024), BF16),
                sds((T, D), BF16), sds((T, D), BF16), sds((2, T, D), BF16), sds((T, D), F32),
            ),
            *atts, gains, wop, wgu, wd, tok, cots[ks[0]], cots[ks[1]], name="ffn", vmem=24,
            cost=COST["ffn"], after=after,
        )

    n2_a, hid_a, ggug_a, keep, give, _, _ = ffn((2, 3))
    two_x = keep + swap(give, 1)
    n2_b, hid_b, ggug_b, two_keep, give, attc, mixed_own = ffn((0, 1), two_x)
    two_x = swap(two_x, 2)
    two_c = swap(give, 1)
    y_keep, y_give, z_keep, z_give, lo_keep, lo_give = call(
        ffn_dw_kernel, (sds((4, 288, 256), BF16),) * 4 + (sds((2, T, D), BF16),) * 2,
        n2_a.reshape(2 * T, D), ggug_a.reshape(2 * T, 1024), hid_a.reshape(2 * T, 512),
        n2_b.reshape(2 * T, D), ggug_b.reshape(2 * T, 1024), hid_b.reshape(2 * T, 512),
        *cots, wd, name="ffn_dw", vmem=20, cost=COST["ffn_dw"],
        scratch=(pltpu.VMEM((D, 1024), F32), pltpu.VMEM((512, D), F32)),
    )
    y_got, z_got = swap(y_give, 4), swap(z_give, 8)
    lo_c = swap(later(lo_give, *()), 1)
    lo_sum = lo_keep[1] + lo_c[1]
    mixed_grad, g0, g1, g2, g3, wo_keep, *wo_gives = call(
        mid_kernel,
        (sds((T, D), F32),) + (sds((384, 128), BF16),) * 4
        + (sds((2, 8, 24, D), BF16),) + (sds((8, 24, D), BF16),) * 2,
        two_keep, two_c, two_x, mixed_own, cot_own, attc, wop, gains, name="mid", vmem=16,
        after=(y_give, *()), scratch=(pltpu.VMEM((D, D), F32),), cost=COST["mid"],
    )
    g1, g2, g3 = swap(g1, 1), swap(g2, 2), swap(g3, 3)
    wo_got = (swap(wo_gives[0], 1), swap(wo_gives[1], 1))
    wo_sum = later(wo_keep[1] + wo_got[1], g1, g2, g3)
    wo_along = swap(wo_sum, 2)

    def attn_bwd(second, *after):
        mine = slice(2, 3) if second else slice(0, 2)
        count = 1 if second else 2
        return call(
            functools.partial(attn_bwd_kernel, second),
            (sds((TP, T, 256 if second else 384), BF16), sds((8, 128), F32)),
            qkv, *probs[mine], *inv_tots[mine], *out_ts[mine], g0, g1, g2, g3,
            name="attn_bwd", vmem=22, cost=COST["attn_bwd"][second], after=after,
            scratch=(
                pltpu.VMEM((count, TP, 128, T), BF16),
                pltpu.VMEM((count, TP, T, 128), BF16),
                pltpu.VMEM((count, TP, T, 128), BF16),
                pltpu.VMEM((count, 128, TP * T), BF16),
                pltpu.VMEM((count, TP, 1, T), F32),
                pltpu.VMEM((TP, T, T), BF16),
                pltpu.VMEM((128, TP * T), F32),
                pltpu.VMEM((TP * T, 128), F32),
                pltpu.VMEM((TP * T, 128), F32),
                pltpu.VMEM((3, 128, 128), F32),
                pltpu.VMEM((2, 8, 128), F32),
            ),
        )

    def chunks(n, chunk):
        return sds((n * chunk + (TAIL if chunk == SECOND else 0), 128), BF16)

    def stage(n, chunk, keep, got, name, *after):
        return call(
            functools.partial(stage_kernel, n, chunk), (chunks(n // 2, chunk),) * 2, keep, got,
            name=name, after=after, cost=COST[name],
        )

    da, ta = attn_bwd(0, *(wo_sum,))
    a_keep, a_give = call(
        first_dw_kernel, (chunks(4, FIRST),) * 2, n1.reshape(flat, D), da.reshape(flat, 384),
        name="first_dw", vmem=12, scratch=(pltpu.VMEM((D, 384), F32),),
    )
    a_got = swap(a_give, 4)
    y_keep, y_give, z_keep, z_give = call(
        ffn_second_kernel, (sds((2, 288, 256), BF16),) * 4, y_keep, y_got, z_keep, z_got,
        name="ffn_second", after=(a_give,),
    )
    y_got, z_got = swap(y_give, 8), swap(z_give, 16)
    db, tb = attn_bwd(1, y_give, *(lo_sum,))
    b_keep, b_give = call(
        second_dw_kernel, (chunks(4, SECOND),) * 2,
        n1.reshape(flat, D), db.reshape(flat, 256), wo_keep, wo_got[0], wo_along, ta, tb,
        name="second_dw", vmem=12,
        scratch=(
            pltpu.VMEM((D, 256), F32), pltpu.VMEM((8, 24, D), F32), pltpu.VMEM((SECOND, 128), F32),
        ),
    )
    b_got = swap(b_give, 4)
    one_keep, one_give = call(
        one_grad_kernel, (sds((2, T, D), BF16),) * 2, da, db, w_qkv, name="one_grad", vmem=16,
        after=(b_give,), cost=COST["one_grad"],
    )
    lo_x = swap(later(lo_sum, *(db,)), 2)
    one_c = swap(one_give, 1)
    one_x = swap(later(one_keep[1] + one_c[1], *(lo_x,)), 2)
    a_keep, a_give = stage(4, FIRST, a_keep, a_got, "stage_y", b_give)
    a_got = swap(a_give, 8)
    y_give, z_give = call(
        ffn_third_kernel, (sds((288, 256), BF16),) * 2, y_keep, y_got, z_keep, z_got,
        name="ffn_third", after=(a_give,),
    )
    y_along, z_along = swap(y_give, 16), swap(z_give, 4)
    b_keep, b_give = stage(4, SECOND, b_keep, b_got, "stage_y", *(y_give,))
    b_got = swap(b_give, 8)
    a_keep, a_give = stage(2, FIRST, a_keep, a_got, "stage_z", b_give)
    a_got = swap(a_give, 16)
    b_keep, b_give = stage(2, SECOND, b_keep, b_got, "stage_z", *(a_give,))
    b_got = swap(b_give, 16)
    layer_out = mixed_own + lo_keep[0].astype(F32) + lo_c[0].astype(F32) + lo_x.astype(F32)
    tokens_grad, mark = call(
        close_kernel, (sds((T, D), F32), sds((8, 128), F32)), one_keep, one_c, one_x, mixed_grad, tok, gains,
        name="close", vmem=10, after=(a_got,),
    )
    dwd, *backs = call(
        first_back_kernel, (sds((64, D), F32),) + (sds((rows, 1408), BF16),) * 4,
        a_keep, a_got, y_keep, y_got, y_along, z_keep, z_got, z_along,
        name="first_back", after=(b_give,), cost=COST["first_back"],
        scratch=(pltpu.VMEM((FIRST, 128), F32), pltpu.VMEM((576, 256), F32)),
    )
    firsts = (backs[0], swap(backs[1], 1), swap(backs[2], 2), swap(backs[3], 3))
    dwo, *backs = call(
        second_back_kernel, (sds((rows, D), F32),) + (sds((rows, 384), BF16),) * 4, b_keep, b_got,
        name="second_back", after=(mark, *firsts[1:]), scratch=(pltpu.VMEM((SECOND, 128), F32),),
    )
    seconds = (backs[0], swap(backs[1], 1), swap(backs[2], 2), swap(backs[3], 3))
    dg, du, gg2, mark = call(
        first_final_kernel,
        (sds((rows, ff), F32),) * 2 + (sds((1, rows), F32), sds((8, 128), F32)),
        *firsts, gain_cols, w_gate, w_up, name="first_final",
        scratch=(pltpu.VMEM((TP, rows, 1024), F32),),
    )
    dq, dk, dv, gg1, table_sum = call(
        second_final_kernel,
        (sds((rows, D), F32),) * 3 + (sds((1, rows), F32), sds((H, NB), F32)),
        *firsts, *seconds, gain_cols, w_query, w_key, w_value, name="second_final", after=(mark,),
        scratch=(pltpu.VMEM((TP, rows, 640), F32),),
    )
    return (
        layer_out.astype(BF16)[None],
        tokens_grad[None],
        dq,
        dk,
        dv,
        dwo,
        gg1[0],
        table_sum.T,
        dg,
        du,
        dwd,
        gg2[0],
    )


KEY_BLOCK = 256
HIGHEST = lax.Precision.HIGHEST


def rms_norm(values, gain):
    return values * lax.rsqrt(jnp.mean(values * values, axis=-1, keepdims=True) + EPSILON) * gain


def split_heads(flat_rows):
    return flat_rows.reshape(flat_rows.shape[0], flat_rows.shape[1], H, DH)


def join_heads(per_head):
    return per_head.reshape(per_head.shape[0], per_head.shape[1], H * DH)


def project(left, matrix):
    return jnp.einsum("rtd,de->rte", left, matrix, preferred_element_type=jnp.float32)


def project_back(left, matrix):
    return jnp.einsum("rte,de->rtd", left, matrix, preferred_element_type=jnp.float32)


def weight_grad(left, right):
    return jnp.einsum("rtd,rte->de", left, right, preferred_element_type=jnp.float32)


def block_scores(queries, key_block, query_pos, key_pos, query_seg, key_seg, bias_table):
    raw_scores = jnp.einsum(
        "rqhd,rkhd->rhqk", queries, key_block, preferred_element_type=jnp.float32
    )
    buckets = bucket_of(key_pos[None, :] - query_pos[:, None])
    one_hot = (buckets[:, :, None] == jnp.arange(NB, dtype=jnp.int32)[None, None, :]).astype(
        jnp.float32
    )
    rel_term = jnp.einsum("qkb,bh->hqk", one_hot, bias_table, precision=HIGHEST)
    allowed = (query_seg[:, :, None] == key_seg[:, None, :])[:, None]
    return (raw_scores + rel_term[None], allowed, one_hot)


def absorb(
    running, queries, key_block, value_block, query_pos, key_pos, query_seg, key_seg, bias_table
):
    row_peak, row_total, weighted = running
    scores, allowed, unused = block_scores(
        queries, key_block, query_pos, key_pos, query_seg, key_seg, bias_table
    )
    block_peak = jnp.max(jnp.where(allowed, scores, MASKED), axis=-1)
    new_peak = jnp.maximum(row_peak, block_peak)
    weights = jnp.where(allowed, jnp.exp(scores - new_peak[..., None]), 0.0)
    factor = jnp.exp(row_peak - new_peak)
    row_total = row_total * factor + jnp.sum(weights, axis=-1)
    weighted = weighted * factor[..., None] + jnp.einsum(
        "rhqk,rkhd->rhqd",
        weights.astype(jnp.bfloat16),
        value_block,
        preferred_element_type=jnp.float32,
    )
    return (new_peak, row_total, weighted)


def pair_grads(
    queries,
    out_grad,
    log_total,
    row_delta,
    key_block,
    value_block,
    query_pos,
    key_pos,
    query_seg,
    key_seg,
    bias_table,
):
    scores, allowed, one_hot = block_scores(
        queries, key_block, query_pos, key_pos, query_seg, key_seg, bias_table
    )
    prob_map = jnp.where(allowed, jnp.exp(scores - log_total[..., None]), 0.0)
    prob_grad = jnp.einsum(
        "rqhd,rkhd->rhqk", out_grad, value_block, preferred_element_type=jnp.float32
    )
    score_grad = prob_map * (prob_grad - row_delta[..., None])
    score_low = score_grad.astype(jnp.bfloat16)
    query_grad = jnp.einsum(
        "rhqk,rkhd->rqhd", score_low, key_block, preferred_element_type=jnp.float32
    )
    key_grad = jnp.einsum("rhqk,rqhd->rkhd", score_low, queries, preferred_element_type=jnp.float32)
    value_grad = jnp.einsum(
        "rhqk,rqhd->rkhd",
        prob_map.astype(jnp.bfloat16),
        out_grad,
        preferred_element_type=jnp.float32,
    )
    table_grad = jnp.einsum("rhqk,qkb->bh", score_grad, one_hot, precision=HIGHEST)
    return (query_grad, key_grad, value_grad, table_grad)


def in_blocks(step_fn, running, pieces):
    length = pieces[0].shape[1]
    block_size = math.gcd(length, KEY_BLOCK)
    block_count = length // block_size
    stacked = tuple(
        (
            jnp.moveaxis(
                member.reshape((member.shape[0], block_count, block_size) + member.shape[2:]), 1, 0
            )
            for member in pieces
        )
    )
    starts = block_size * jnp.arange(block_count, dtype=jnp.int32)

    def scan_step(inner_state, item_pair):
        return (step_fn(inner_state, item_pair[0], item_pair[1]), None)

    running, unused = lax.scan(scan_step, running, (stacked, starts))
    return running


def local(
    tokens,
    segment_ids,
    w_query,
    w_key,
    w_value,
    w_attn_out,
    attn_gain,
    rel_bias,
    w_gate,
    w_up,
    w_down,
    ffn_gain,
    cotangent,
):
    row_count, local_len, unused_dim = tokens.shape
    my_block = lax.axis_index("blk")
    full_query, full_key, full_value, full_out, gain_one = (
        lax.all_gather(w_query, ("dp", "blk"), axis=0, tiled=True),
        lax.all_gather(w_key, ("dp", "blk"), axis=0, tiled=True),
        lax.all_gather(w_value, ("dp", "blk"), axis=0, tiled=True),
        lax.all_gather(w_attn_out, ("dp", "blk"), axis=0, tiled=True),
        lax.all_gather(attn_gain, ("dp", "blk"), axis=0, tiled=True),
    )
    full_gate, full_up, full_down, gain_two = (
        lax.all_gather(w_gate, ("dp", "blk"), axis=0, tiled=True),
        lax.all_gather(w_up, ("dp", "blk"), axis=0, tiled=True),
        lax.all_gather(w_down, ("dp", "blk"), axis=0, tiled=True),
        lax.all_gather(ffn_gain, ("dp", "blk"), axis=0, tiled=True),
    )
    row_segs = lax.all_gather(segment_ids, "blk", axis=1, tiled=True)
    bias_table = rel_bias.astype(jnp.float32)
    gain_one_f = gain_one.astype(jnp.float32)
    gain_two_f = gain_two.astype(jnp.float32)
    inputs = tokens.astype(jnp.float32)
    query_pos = my_block * local_len + jnp.arange(local_len, dtype=jnp.int32)
    normed_one = rms_norm(inputs, gain_one_f).astype(jnp.bfloat16)
    query_flat = project(normed_one, full_query).astype(jnp.bfloat16)
    key_flat = project(normed_one, full_key).astype(jnp.bfloat16)
    value_flat = project(normed_one, full_value).astype(jnp.bfloat16)
    queries = split_heads(query_flat)
    key_heads = split_heads(key_flat)
    value_heads = split_heads(value_flat)

    def forward_piece(running, pieces):

        def step_fn(inner_state, blocks, block_start):
            block_len = blocks[0].shape[1]
            key_pos = block_start + jnp.arange(block_len, dtype=jnp.int32)
            key_seg = lax.dynamic_slice_in_dim(row_segs, block_start, block_len, 1)
            return absorb(
                inner_state,
                queries,
                split_heads(blocks[0]),
                split_heads(blocks[1]),
                query_pos,
                key_pos,
                segment_ids,
                key_seg,
                bias_table,
            )

        return in_blocks(step_fn, running, pieces)

    stat_shape = (row_count, H, local_len)
    start_state = (
        jnp.full(stat_shape, MASKED, jnp.float32),
        jnp.zeros(stat_shape, jnp.float32),
        jnp.zeros(stat_shape + (DH,), jnp.float32),
    )
    row_peak, row_total, weighted = forward_piece(
        start_state,
        (
            lax.all_gather(key_flat, "blk", axis=1, tiled=True),
            lax.all_gather(value_flat, "blk", axis=1, tiled=True),
        ),
    )
    log_total = row_peak + jnp.log(row_total)
    attended_f = jnp.transpose(weighted / row_total[..., None], (0, 2, 1, 3))
    attended = join_heads(attended_f).astype(jnp.bfloat16)
    mixed_in = inputs + project(attended, full_out)
    normed_two = rms_norm(mixed_in, gain_two_f).astype(jnp.bfloat16)
    gate_act = project(normed_two, full_gate)
    up_act = project(normed_two, full_up)

    def gated(gate_in, up_in):
        return jax.nn.gelu(gate_in, approximate=True) * up_in

    hidden_f, gated_back = jax.vjp(gated, gate_act, up_act)
    hidden = hidden_f.astype(jnp.bfloat16)
    layer_out = (mixed_in + project(hidden, full_down)).astype(jnp.bfloat16)
    down_grad = weight_grad(hidden, cotangent)
    hidden_grad = project_back(cotangent, full_down)
    gate_grad, up_grad = gated_back(hidden_grad)
    gate_low = gate_grad.astype(jnp.bfloat16)
    up_low = up_grad.astype(jnp.bfloat16)
    gate_w_grad = weight_grad(normed_two, gate_low)
    up_w_grad = weight_grad(normed_two, up_low)
    two_grad = project_back(gate_low, full_gate) + project_back(up_low, full_up)
    unused_two, norm_two_back = jax.vjp(rms_norm, mixed_in, gain_two_f)
    mixed_part, gain_two_grad = norm_two_back(two_grad)
    mixed_grad = cotangent.astype(jnp.float32) + mixed_part
    mixed_low = mixed_grad.astype(jnp.bfloat16)
    out_w_grad = weight_grad(attended, mixed_low)
    attended_grad = project_back(mixed_low, full_out).astype(jnp.bfloat16)
    grad_heads = split_heads(attended_grad)
    row_delta = jnp.sum(
        jnp.transpose(grad_heads.astype(jnp.float32), (0, 2, 1, 3))
        * (weighted / row_total[..., None]),
        axis=-1,
    )
    zero_heads = jnp.zeros(queries.shape, jnp.float32)
    zero_table = jnp.zeros((NB, H), jnp.float32)

    def query_piece(running, pieces):

        def step_fn(inner_state, blocks, block_start):
            block_len = blocks[0].shape[1]
            key_pos = block_start + jnp.arange(block_len, dtype=jnp.int32)
            key_seg = lax.dynamic_slice_in_dim(row_segs, block_start, block_len, 1)
            pair_parts = pair_grads(
                queries,
                grad_heads,
                log_total,
                row_delta,
                split_heads(blocks[0]),
                split_heads(blocks[1]),
                query_pos,
                key_pos,
                segment_ids,
                key_seg,
                bias_table,
            )
            return inner_state + pair_parts[0]

        return in_blocks(step_fn, running, pieces)

    query_grad = join_heads(
        query_piece(
            zero_heads,
            (
                lax.all_gather(key_flat, "blk", axis=1, tiled=True),
                lax.all_gather(value_flat, "blk", axis=1, tiled=True),
            ),
        )
    )
    log_rows, delta_rows = (
        lax.all_gather(log_total, "blk", axis=2, tiled=True),
        lax.all_gather(row_delta, "blk", axis=2, tiled=True),
    )

    def key_piece(running, pieces):

        def step_fn(inner_state, blocks, block_start):
            block_len = blocks[0].shape[1]
            piece_pos = block_start + jnp.arange(block_len, dtype=jnp.int32)
            piece_seg = lax.dynamic_slice_in_dim(row_segs, block_start, block_len, 1)
            piece_log = lax.dynamic_slice_in_dim(log_rows, block_start, block_len, 2)
            piece_delta = lax.dynamic_slice_in_dim(delta_rows, block_start, block_len, 2)
            pair_parts = pair_grads(
                split_heads(blocks[0]),
                split_heads(blocks[1]),
                piece_log,
                piece_delta,
                key_heads,
                value_heads,
                piece_pos,
                query_pos,
                piece_seg,
                segment_ids,
                bias_table,
            )
            return (
                inner_state[0] + pair_parts[1],
                inner_state[1] + pair_parts[2],
                inner_state[2] + pair_parts[3],
            )

        return in_blocks(step_fn, running, pieces)

    key_grad, value_grad, table_grad = key_piece(
        (zero_heads, zero_heads, zero_table),
        (
            lax.all_gather(query_flat, "blk", axis=1, tiled=True),
            lax.all_gather(attended_grad, "blk", axis=1, tiled=True),
        ),
    )
    query_low = query_grad.astype(jnp.bfloat16)
    key_low = join_heads(key_grad).astype(jnp.bfloat16)
    value_low = join_heads(value_grad).astype(jnp.bfloat16)
    query_w_grad = weight_grad(normed_one, query_low)
    key_w_grad = weight_grad(normed_one, key_low)
    value_w_grad = weight_grad(normed_one, value_low)
    one_grad = (
        project_back(query_low, full_query)
        + project_back(key_low, full_key)
        + project_back(value_low, full_value)
    )
    unused_one, norm_one_back = jax.vjp(rms_norm, inputs, gain_one_f)
    input_part, gain_one_grad = norm_one_back(one_grad)
    tokens_grad = mixed_grad + input_part
    table_sum = lax.psum(table_grad, ("dp", "blk"))
    all_sums = (
        lax.psum_scatter(query_w_grad, ("dp", "blk"), scatter_dimension=0, tiled=True),
        lax.psum_scatter(key_w_grad, ("dp", "blk"), scatter_dimension=0, tiled=True),
        lax.psum_scatter(value_w_grad, ("dp", "blk"), scatter_dimension=0, tiled=True),
        lax.psum_scatter(out_w_grad, ("dp", "blk"), scatter_dimension=0, tiled=True),
        lax.psum_scatter(gain_one_grad, ("dp", "blk"), scatter_dimension=0, tiled=True),
        lax.psum_scatter(gate_w_grad, ("dp", "blk"), scatter_dimension=0, tiled=True),
        lax.psum_scatter(up_w_grad, ("dp", "blk"), scatter_dimension=0, tiled=True),
        lax.psum_scatter(down_grad, ("dp", "blk"), scatter_dimension=0, tiled=True),
        lax.psum_scatter(gain_two_grad, ("dp", "blk"), scatter_dimension=0, tiled=True),
    )
    return (
        layer_out,
        tokens_grad,
        all_sums[0],
        all_sums[1],
        all_sums[2],
        all_sums[3],
        all_sums[4],
        table_sum,
        all_sums[5],
        all_sums[6],
        all_sums[7],
        all_sums[8],
    )


def solution(mesh):
    whole = P(AXES, None)
    rows = P("dp", "blk", None)
    n_dp, n_blk = mesh.shape["dp"], mesh.shape["blk"]
    grouped = functools.partial(group_local, n_dp, n_blk)
    body = grouped if (n_dp, n_blk) == (8, TP) else local
    return jax.shard_map(
        body,
        mesh=mesh,
        in_specs=(
            rows, P("dp", "blk"), whole, whole, whole, whole, P(AXES), P(),
            whole, whole, whole, P(AXES), rows,
        ),
        out_specs=(
            rows, rows, whole, whole, whole, whole, P(AXES), P(), whole, whole, whole, P(AXES),
        ),
        check_vma=False,
    )
```

```python
import functools
import math

import jax
import jax.numpy as jnp
from jax import lax
from jax.experimental import pallas as pl
from jax.experimental.pallas import tpu as pltpu
from jax.sharding import PartitionSpec as P

D = 768
H = 12
DH = 64
NB = 32
THRESHOLDS = (12, 16, 23, 32, 46, 64, 91)
MASKED = -1e30
EPSILON = 1e-06
TP = 4
T = 256
HT = 3
F32 = jnp.float32
BF16 = jnp.bfloat16
MIB = 1 << 20


def dot(a, b):
    return lax.dot_general(a, b, (((1,), (0,)), ((), ())), preferred_element_type=F32)


def dot_nt(a, b):
    return lax.dot_general(a, b, (((1,), (1,)), ((), ())), preferred_element_type=F32)


def dot_tn(a, b):
    return lax.dot_general(a, b, (((0,), (0,)), ((), ())), preferred_element_type=F32)


def bucket_of(relative):
    distance = jnp.abs(relative)
    far = jnp.full(relative.shape, 8, jnp.int32)
    for threshold in THRESHOLDS:
        far = far + (distance >= threshold).astype(jnp.int32)
    return jnp.where(relative > 0, NB // 2, 0) + jnp.where(distance < 8, distance, far)


def call(
    kernel, out_shape, *args, scratch=(), smem=(), held=(), after=(), vmem=8, cost=0, name=None
):
    vspec = pl.BlockSpec(memory_space=pltpu.VMEM)
    sspec = pl.BlockSpec(memory_space=pltpu.SMEM)
    aspec = pl.BlockSpec(memory_space=pl.ANY)
    hspec = pl.BlockSpec(memory_space=pltpu.HBM)
    skip = len(after)

    def body(*refs):
        kernel(*refs[skip:])

    specs = [sspec if n in smem else hspec if n in held else vspec for n in range(len(args))]
    return pl.pallas_call(
        body,
        out_shape=out_shape,
        in_specs=[aspec] * skip + specs,
        out_specs=jax.tree.map(lambda _: vspec, out_shape),
        scratch_shapes=list(scratch),
        compiler_params=pltpu.CompilerParams(vmem_limit_bytes=vmem * MIB),
        cost_estimate=pl.CostEstimate(flops=cost * 1_150_000_000, bytes_accessed=0, transcendentals=0),
        name=name,
    )(*after, *args)


def sds(shape, dtype):
    return jax.ShapeDtypeStruct(shape, dtype)


def low_half(rows):
    return lax.broadcasted_iota(jnp.int32, (rows, 128), 1) < 64


def prep_kernel(
    wq, wk, wv, wg, wu, tok, seg, g1, g2, s0, s1, s2, s3, ts, gains, slabs, vq, vk, vv, vg, vu, sems
):
    j_me = lax.axis_index("blk")
    rows = wq.shape[0]
    pairs = ((wq, vq), (wk, vk), (wv, vv), (wg, vg), (wu, vu), (tok, ts.at[0:T]))
    copies = [pltpu.make_async_copy(a, b, sems.at[n]) for n, (a, b) in enumerate(pairs)]
    for copy in copies:
        copy.start()
    eye = lax.broadcasted_iota(jnp.int32, (rows, rows), 0) == lax.broadcasted_iota(
        jnp.int32, (rows, rows), 1
    )
    columns = []
    for n, ref in enumerate((g1, g2)):
        row = jnp.broadcast_to(ref[...].astype(F32).reshape(1, rows), (rows, rows))
        column = jnp.sum(jnp.where(eye, row, 0.0), axis=1, keepdims=True)
        columns.append(column)
        gains[n] = jnp.broadcast_to(column, (rows, 128))
    ids = jnp.broadcast_to(seg[...], (16, T))
    ts[T : T + 16, 0:T] = (ids // 2).astype(F32).astype(BF16)
    ts[T : T + 16, T : 2 * T] = (ids % 2).astype(F32).astype(BF16)
    ts[T : T + 16, 2 * T : 3 * T] = jnp.zeros((16, T), BF16)
    low = low_half(rows)
    lane = lax.broadcasted_iota(jnp.int32, (rows, 128), 1)
    spare = jnp.where(lane == 64, columns[0], jnp.where(lane == 65, columns[1], 0.0))
    for copy in copies:
        copy.wait()

    def tile(ref, index):
        return ref[:, 128 * index : 128 * index + 128].astype(F32)

    for j in range(TP):
        first, second = [], []
        for ref in (vq, vk, vv):
            at = 192 * j // 128
            a, b = tile(ref, at), tile(ref, at + 1)
            if j % 2:
                a, b = pltpu.roll(a, 64, 1), pltpu.roll(b, 64, 1)
                a = jnp.where(low, a, b)
            first.append(a)
            second.append(b)
        tiles = first + [
            jnp.where(low, second[0], pltpu.roll(second[1], 64, 1)),
            jnp.where(low, second[2], spare),
        ]
        for ref in (vg, vu):
            for t in range(4):
                a = tile(ref, 4 * t + j // 2)
                b = tile(ref, 4 * t + 2 + j // 2)
                if j % 2:
                    tiles.append(jnp.where(low, pltpu.roll(a, 64, 1), b))
                else:
                    tiles.append(jnp.where(low, a, pltpu.roll(b, 64, 1)))
        for n, v in enumerate(tiles):
            slabs[j ^ j_me, :, 128 * n : 128 * n + 128] = v.astype(BF16)
    for k, ref in enumerate((s0, s1, s2, s3)):
        ref[...] = slabs[k]


def pack_kernel(s0, s1, s2, s3, wo, first, whole, vo, sem):
    j = lax.axis_index("blk")
    rows = s0.shape[0]
    copy = pltpu.make_async_copy(wo, vo, sem)
    copy.start()
    for k, ref in enumerate((s0, s1, s2, s3)):
        whole[pl.ds(pl.multiple_of(rows * (j ^ k), 8), rows)] = ref[:, 0:640].astype(F32)
    first[0:96] = whole[...].astype(BF16)
    copy.wait()
    out = vo[...].astype(F32)
    rest = [out[8 * n : 8 * n + 8, 640:768] for n in range(3)]
    rest = jnp.concatenate(rest + [jnp.zeros((8, 256), F32)], axis=1)
    first[96:128] = jnp.concatenate([out[:, 0:640], rest], axis=0).astype(BF16)


def pack_more_kernel(s0, s1, s2, s3, wd, second, whole, vd, sem):
    j = lax.axis_index("blk")
    rows = s0.shape[0]
    copy = pltpu.make_async_copy(wd, vd, sem)
    copy.start()
    for k, ref in enumerate((s0, s1, s2, s3)):
        whole[pl.ds(pl.multiple_of(rows * (j ^ k), 8), rows)] = ref[:, 640:1664].astype(F32)
    for n in range(4):
        second[96 * n : 96 * n + 96] = whole[:, 256 * n : 256 * n + 256].astype(BF16)
    copy.wait()
    for n in range(3):
        second[384 + 64 * n : 448 + 64 * n] = vd[:, 256 * n : 256 * n + 256]


def stripes_kernel(p0, p1, p2, p3, p4, p5, p6, p7, out, whole):
    dp = lax.axis_index("dp")
    for n, ref in enumerate((p0, p1, p2, p3, p4, p5, p6, p7)):
        at = pl.ds(pl.multiple_of(24 * (dp ^ piece_at(n)), 8), 24)
        part = ref[96:128].astype(F32)
        whole[at, 0:640] = part[0:24]
        rest = [part[24:32, 128 * m : 128 * m + 128] for m in range(3)]
        whole[at, 640:768] = jnp.concatenate(rest, axis=0)
    out[...] = whole[...].astype(BF16)


def out_weight_kernel(p0, p1, p2, p3, out, whole):
    j = lax.axis_index("blk")
    for k, ref in enumerate((p0, p1, p2, p3)):
        rows = ref[...].astype(F32)
        for d in range(8):
            at = pl.multiple_of(24 * (TP * d + (j ^ k)), 8)
            whole[pl.ds(at, 24)] = rows[24 * d : 24 * d + 24]
    for k in range(TP):
        at = pl.multiple_of(192 * (j ^ k), 64)
        out[128 * k : 128 * k + 128] = whole[pl.ds(at, 128)].astype(BF16)
        out[512 + 64 * k : 576 + 64 * k] = whole[pl.ds(at + 128, 64)].astype(BF16)


def bias_kernel(table, out):
    j = lax.axis_index("blk")
    lane = lax.broadcasted_iota(jnp.int32, (8, 512), 1)
    for n in range(3):
        off = (n - 1) * T
        rel = jnp.where(lane < 256, off - lane, off + 512 - lane)
        bucket = bucket_of(rel)
        for h in range(HT):
            row = jnp.zeros((8, 512), F32)
            for b in range(NB):
                row = jnp.where(bucket == b, table[HT * j + h, b], row)
            wide = jnp.broadcast_to(row[0:1], (T, 512))
            out[h, n] = pltpu.roll(wide, 0, 1, stride=1, stride_axis=0)[:, :T]


def piece_at(n):
    return 2 * (n % 4) + n // 4


def qkv_kernel(
    t0, t1, t2, t3, p0, p1, p2, p3, p4, p5, p6, p7, tok, n1, qkv, w, gains, segq, segk
):
    j = lax.axis_index("blk")
    dp = lax.axis_index("dp")
    for k, ref in enumerate((t0, t1, t2, t3)):
        tok[j ^ k] = ref[0:T]
        parts = ref[T : T + 16].astype(F32)
        row = (2.0 * parts[:, 0:T] + parts[:, T : 2 * T])[0:8]
        segq[j ^ k] = row
        col = jnp.transpose(jnp.broadcast_to(row[0:1], (128, T)))
        segk[j ^ k, :, 0:128] = col
        segk[j ^ k, :, 128:256] = col
    for n, ref in enumerate((p0, p1, p2, p3, p4, p5, p6, p7)):
        w[pl.ds(pl.multiple_of(96 * (dp ^ piece_at(n)), 32), 96)] = ref[0:96]
    turned = jnp.transpose(w[:, 512:640].astype(F32))
    gains[...] = turned[64:72]

    def body(b, carry):
        x = tok[b].astype(F32)
        rstd = lax.rsqrt(jnp.mean(x * x, axis=-1, keepdims=True) + EPSILON)
        n = (x * rstd * gains[0:1]).astype(BF16)
        n1[b] = n
        y = dot(n, w[...])
        for t in range(5):
            qkv[t, b] = y[:, 128 * t : 128 * t + 128].astype(BF16)
        return carry

    lax.fori_loop(0, TP, body, 0)


def attn_fwd_kernel(h, table, bias, qkv, segq, segk, prob, inv_tot, out_t, qt, vt, sc):
    j_me = lax.axis_index("blk")
    rows_low = lax.broadcasted_iota(jnp.int32, (128, T), 0) < 64
    half = slice(64, 128) if h == 1 else slice(0, 64)
    for i in range(TP):
        if h < 2:
            q = jnp.transpose(qkv[0, i].astype(F32))
        else:
            q = jnp.transpose(pltpu.roll(qkv[3, i].astype(F32), 64, 1))
        qt[i] = jnp.where(rows_low == (h == 0), q, 0.0).astype(BF16)
        v = jnp.transpose(qkv[2 + 2 * (h // 2), i].astype(F32)).astype(BF16)
        vt[:, T * i : T * i + T] = v[half]

    tile = 1 + 2 * (h // 2)
    far = (table[HT * j_me + h, 15], table[HT * j_me + h, 31])
    for i in range(TP):
        peak = jnp.full((1, T), MASKED, F32)
        for j in range(TP):
            s = dot(qkv[tile, j], qt[i])
            if abs(j - i) <= 1:
                s = s + bias[h, j - i + 1]
            else:
                s = s + far[j > i]
            if i in (0, TP - 1) or j in (0, TP - 1):
                s = jnp.where(segk[j] == segq[i, 0:1], s, MASKED)
            sc[j] = s
            peak = jnp.maximum(peak, jnp.max(s, axis=0, keepdims=True))
        total = jnp.zeros((1, T), F32)
        for j in range(TP):
            p = jnp.exp(sc[j] - peak)
            total = total + jnp.sum(p, axis=0, keepdims=True)
            prob[i, j] = p.astype(BF16)
        inv = 1.0 / total
        inv_tot[i] = inv
        out_t[:, T * i : T * i + T] = dot(vt[...], prob[i].reshape(TP * T, T)) * inv


def join_kernel(o0, o1, o2, att):
    for b in range(TP):
        at = slice(T * b, T * b + T)
        both = jnp.concatenate([o0[:, at], o1[:, at]], axis=0)
        att[at, :] = jnp.transpose(both).astype(BF16)
    for b in range(2):
        both = [o2[:, T * c : T * c + T] for c in (b, b + 2)]
        att[1024 + T * b : 1280 + T * b, :] = jnp.transpose(jnp.concatenate(both, axis=0)).astype(BF16)


def put_pair(keep, give, k, value):
    @pl.when(k % 2 == 0)
    def _():
        keep[k // 2] = value

    @pl.when(k % 2 == 1)
    def _():
        give[k // 2] = value


def units_kernel(p0, p1, p2, p3, p4, p5, p6, p7, wgu, wd):
    dp = lax.axis_index("dp")
    for n, ref in enumerate((p0, p1, p2, p3, p4, p5, p6, p7)):
        at = dp ^ piece_at(n)
        rows = pl.ds(pl.multiple_of(96 * at, 32), 96)
        for m in range(4):
            wgu[rows, 256 * m : 256 * m + 256] = ref[96 * m : 96 * m + 96]
        rows = pl.ds(pl.multiple_of(64 * at, 64), 64)
        for m in range(3):
            wd[rows, 256 * m : 256 * m + 256] = ref[384 + 64 * m : 448 + 64 * m]


def ffn_kernel(
    ks, a0, a1, a2, a3, gains, wop, wgu, wd, tok, c0, c1,
    n2, hid, ggug, keep, give, attc, mixed_own,
):
    j = lax.axis_index("blk")
    low = low_half(T)
    refs = (a0, a1, a2, a3)
    for m, k in enumerate(ks):
        b = j ^ k
        half = b // 2
        for n, ref in enumerate(refs):
            attc[m, :, 128 * n : 128 * n + 128] = ref[pl.ds(pl.multiple_of(b * T, T), T)]
        rest = [
            ref[pl.ds(pl.multiple_of(1024 + (b % 2) * T, T), T)].astype(F32) for ref in refs
        ]
        for n in range(2):
            lo = pltpu.roll(rest[2 * n], 64 * half, 1)
            hi = pltpu.roll(rest[2 * n + 1], 64 * (1 - half), 1)
            attc[m, :, 512 + 128 * n : 640 + 128 * n] = jnp.where(low, lo, hi).astype(BF16)
        mixed = tok[b].astype(F32) + dot(attc[m], wop[...])
        if k == 0:
            mixed_own[...] = mixed
        rstd = lax.rsqrt(jnp.mean(mixed * mixed, axis=-1, keepdims=True) + EPSILON)
        n = (mixed * rstd * gains[1:2]).astype(BF16)
        n2[m] = n
        gate = dot(n, wgu[:, 0:512])
        up = dot(n, wgu[:, 512:1024])
        c = 0.7978845608028654
        sq = gate * gate
        th = jnp.tanh(c * gate * (1.0 + 0.044715 * sq))
        act = 0.5 * gate * (1.0 + th)
        slope = 0.5 * (1.0 + th) + 0.5 * gate * (1.0 - th * th) * (c * (1.0 + 3 * 0.044715 * sq))
        hid[m] = (act * up).astype(BF16)
        hg = dot_nt((c0, c1)[m][...], wd[...])
        ggug[m, :, 0:512] = (hg * up * slope).astype(BF16)
        ggug[m, :, 512:1024] = (hg * act).astype(BF16)
        (keep, give)[m][...] = dot_nt(ggug[m], wgu[...]).astype(BF16)


def mid_kernel(keep, rc, rx, mixed_own, cot, attc, wop, gains, mixed_grad, g0, g1, g2, g3, wo_keep, wo_one, wo_three, dw):
    j = lax.axis_index("blk")
    u = (keep[...].astype(F32) + rc[...].astype(F32) + rx[...].astype(F32)) * gains[1:2]
    mixed = mixed_own[...]
    rstd = lax.rsqrt(jnp.mean(mixed * mixed, axis=-1, keepdims=True) + EPSILON)
    n = mixed * rstd
    mg = cot[...].astype(F32) + rstd * (u - n * jnp.mean(u * n, axis=-1, keepdims=True))
    mixed_grad[...] = mg
    ml = mg.astype(BF16)
    ag = dot_nt(ml, wop[...])
    low = low_half(128)
    for k, ref in enumerate((g0, g1, g2, g3)):
        ref[0:256] = ag[:, 128 * k : 128 * k + 128].astype(BF16)
        rest = ag[:, 512 + 128 * (k // 2) : 640 + 128 * (k // 2)]
        top, bottom = rest[0:128], rest[128:256]
        if k % 2 == 0:
            v = jnp.where(low, top, pltpu.roll(bottom, 64, 1))
        else:
            v = jnp.where(low, pltpu.roll(top, 64, 1), bottom)
        ref[256:384] = v.astype(BF16)
    perm = dot_tn(attc[0], ml)
    for k in range(TP):
        at = pl.multiple_of(192 * (j ^ k), 64)
        dw[pl.ds(at, 128)] = perm[128 * k : 128 * k + 128]
        dw[pl.ds(at + 128, 64)] = perm[512 + 64 * k : 512 + 64 * k + 64]
    for k in range(TP):
        ref = (wo_keep.at[0], wo_one, wo_keep.at[1], wo_three)[k]
        for d in range(8):
            at = pl.multiple_of(24 * (TP * d + (j ^ k)), 8)
            ref[d] = dw[pl.ds(at, 24)].astype(BF16)


SLOTS = (0, 2, 1, 3)
FIRST = 3 * 96
SECOND = 2 * 96 + 6 * 24
TAIL = 16


def slots(body):
    dp = lax.axis_index("dp")
    for give in range(2):
        for slot, z in enumerate(SLOTS):
            body(give, slot, dp ^ (2 * z + give))


def ffn_dw_kernel(
    na, ga, ha, nb, gb, hb, c0, c1, c2, c3, wd, y_keep, y_give, z_keep, z_give, lo_keep, lo_give, dwgu, dwd
):
    for m in range(2):
        at = slice(512 * m, 512 * m + 512)
        dwgu[:, at] = dot_tn(na[...], ga[:, at]) + dot_tn(nb[...], gb[:, at])
    for m in range(3):
        at = slice(256 * m, 256 * m + 256)
        dwd[:, at] = (
            dot_tn(ha[0:T], c2[:, at])
            + dot_tn(ha[T : 2 * T], c3[:, at])
            + dot_tn(hb[0:T], c0[:, at])
            + dot_tn(hb[T : 2 * T], c1[:, at])
        )
    for n, ref in enumerate((hb, ha)):
        lo_keep[n] = dot(ref[0:T], wd[...]).astype(BF16)
        lo_give[n] = dot(ref[T : 2 * T], wd[...]).astype(BF16)

    def put(g, slot, owner):
        ref = y_give if g else y_keep
        a = pl.ds(pl.multiple_of(96 * owner, 32), 96)
        for m in range(3):
            ref[slot, 96 * m : 96 * m + 96] = dwgu[a, 256 * m : 256 * m + 256].astype(BF16)
        ref = z_give if slot > 1 else z_keep
        slot = 2 * (slot % 2) + g
        ref[slot, 0:96] = dwgu[a, 768:1024].astype(BF16)
        a = pl.ds(pl.multiple_of(64 * owner, 64), 64)
        for m in range(3):
            ref[slot, 96 + 64 * m : 160 + 64 * m] = dwd[a, 256 * m : 256 * m + 256].astype(BF16)

    slots(put)


def ffn_second_kernel(y_keep, y_got, z_keep, z_got, y_next, y_give, z_next, z_give):
    for keep, got, rest, give in ((y_keep, y_got, y_next, y_give), (z_keep, z_got, z_next, z_give)):
        rest[...] = (keep[0:2].astype(F32) + got[0:2].astype(F32)).astype(BF16)
        give[...] = (keep[2:4].astype(F32) + got[2:4].astype(F32)).astype(BF16)


def ffn_third_kernel(y_keep, y_got, z_keep, z_got, y_give, z_give):
    y_give[...] = (y_keep[1].astype(F32) + y_got[1].astype(F32)).astype(BF16)
    z_give[...] = (z_keep[1].astype(F32) + z_got[1].astype(F32)).astype(BF16)


def split(x):
    high = x.astype(BF16).astype(F32)
    return jnp.concatenate([high, x - high], axis=0).astype(BF16)


def first_dw_kernel(n1, dqkv, keep, give, dw):
    for t in range(3):
        at = slice(128 * t, 128 * t + 128)
        dw[:, at] = dot_tn(n1[...], dqkv[:, at])

    def put(g, slot, owner):
        ref = give if g else keep
        a = pl.ds(pl.multiple_of(96 * owner, 32), 96)
        for t in range(3):
            at = FIRST * slot + 96 * t
            ref[at : at + 96] = dw[a, 128 * t : 128 * t + 128].astype(BF16)

    slots(put)


def second_dw_kernel(n1, dqkv, wo_keep, wo_got, wo_along, ta, tb, keep, give, dw, wo, chunk):
    for t in range(2):
        at = slice(128 * t, 128 * t + 128)
        dw[:, at] = dot_tn(n1[...], dqkv[:, at])
    for d in range(8):
        wo[d] = wo_keep[0, d].astype(F32) + wo_got[d].astype(F32) + wo_along[d].astype(F32)

    def put(g, slot, owner):
        ref = give if g else keep
        a = pl.ds(pl.multiple_of(96 * owner, 32), 96)
        for t in range(2):
            chunk[96 * t : 96 * t + 96] = dw[a, 128 * t : 128 * t + 128]
        for t in range(6):
            chunk[192 + 24 * t : 216 + 24 * t] = wo[owner, :, 128 * t : 128 * t + 128]
        ref[SECOND * slot : SECOND * slot + SECOND] = chunk[...].astype(BF16)

    slots(put)
    for ref in (keep, give):
        ref[4 * SECOND : 4 * SECOND + 16] = split(ta[...] + tb[...])


def tail_of(ref, base):
    both = ref[base : base + 16].astype(F32)
    return both[0:8] + both[8:16]


def stage_kernel(n, chunk, keep, got, next_keep, next_give):
    half = n // 2 * chunk
    for at, ref in ((0, next_keep), (half, next_give)):
        here = slice(at, at + half)
        ref[0:half] = (keep[here].astype(F32) + got[here].astype(F32)).astype(BF16)
        if chunk == SECOND:
            ref[half : half + 16] = split(tail_of(keep, n * chunk) + tail_of(got, n * chunk))


def first_back_kernel(ka, ga, yk, yg, ya, zk, zg, za, dwd, b0, b1, b2, b3, total, ffn):
    j = lax.axis_index("blk")
    ffn[0:288] = yk[0].astype(F32) + yg[0].astype(F32) + ya[...].astype(F32)
    ffn[288:576] = zk[0].astype(F32) + zg[0].astype(F32) + za[...].astype(F32)
    for m in range(3):
        dwd[:, 256 * m : 256 * m + 256] = ffn[384 + 64 * m : 448 + 64 * m]
    total[...] = ka[...].astype(F32) + ga[...].astype(F32)
    for k, ref in enumerate((b0, b1, b2, b3)):
        for t in range(3):
            part = total[pl.ds(pl.multiple_of(96 * t + 24 * (j ^ k), 8), 24)]
            ref[:, 128 * t : 128 * t + 128] = part.astype(BF16)
        for m in range(4):
            part = ffn[pl.ds(pl.multiple_of(96 * m + 24 * (j ^ k), 8), 24)]
            ref[:, 384 + 256 * m : 640 + 256 * m] = part.astype(BF16)


def second_back_kernel(kb, gb, dwo, b0, b1, b2, b3, total):
    j = lax.axis_index("blk")
    total[...] = kb[0:SECOND].astype(F32) + gb[0:SECOND].astype(F32)
    parts = split(tail_of(kb, SECOND) + tail_of(gb, SECOND)).astype(F32)
    parts = jnp.concatenate([parts, jnp.zeros((8, 128), F32)], axis=0).astype(BF16)
    for t in range(6):
        at = 192 + 24 * t
        dwo[:, 128 * t : 128 * t + 128] = total[at : at + 24]
    for k, ref in enumerate((b0, b1, b2, b3)):
        for t in range(2):
            part = total[pl.ds(pl.multiple_of(96 * t + 24 * (j ^ k), 8), 24)]
            ref[:, 128 * t : 128 * t + 128] = part.astype(BF16)
        ref[:, 256:384] = parts


def attn_bwd_kernel(second, *refs):
    count = 1 if second else 2
    heads = range(HT - 1, HT) if second else range(2)
    qkv, refs = refs[0], refs[1:]
    probs, refs = refs[:count], refs[count:]
    invs, refs = refs[:count], refs[count:]
    outs, refs = refs[:count], refs[count:]
    (g0, g1, g2, g3, dqkv, table_grad,
     dotm, dom, qm, ktm, delta, dst, dq_acc, dk_acc, dv_acc, near, far) = refs
    j_me = lax.axis_index("blk")
    low = low_half(T)
    rows_low = lax.broadcasted_iota(jnp.int32, (128, T), 0) < 64

    for k, ref in enumerate((g0, g1, g2, g3)):
        b = j_me ^ k
        if second:
            rest = ref[256:384].astype(F32)
            rows = jnp.concatenate([rest, pltpu.roll(rest, 64, 1)], axis=0)
            turned = jnp.where(rows_low, jnp.transpose(rows) * invs[0][b], 0.0)
        else:
            turned = jnp.transpose(ref[0:256].astype(F32))
            turned = turned * jnp.where(rows_low, invs[0][b], invs[1][b])
        turned = turned.astype(BF16).astype(F32)
        back = jnp.transpose(turned)
        for n in range(count):
            dotm[n, b] = jnp.where(rows_low == (n == 0), turned, 0.0).astype(BF16)
            dom[n, b] = jnp.where(low == (n == 0), back, 0.0).astype(BF16)

    for i in range(TP):
        at = slice(T * i, T * i + T)
        if second:
            q = pltpu.roll(qkv[3, i].astype(F32), 64, 1)
            keys = jnp.transpose(q)
        else:
            q = qkv[0, i].astype(F32)
            keys = jnp.transpose(qkv[1, i].astype(F32))
        for n in range(count):
            g = dotm[n, i].astype(F32)[64 * n : 64 * n + 64]
            delta[n, i] = jnp.sum(outs[n][:, at] * g, axis=0, keepdims=True)
            qm[n, i] = jnp.where(low == (n == 0 and not second), q, 0.0).astype(BF16)
            ktm[n, :, at] = jnp.where(rows_low == (n == 0), keys, 0.0).astype(BF16)

    dq_acc[...] = jnp.zeros(dq_acc.shape, F32)
    dk_acc[...] = jnp.zeros(dk_acc.shape, F32)
    dv_acc[...] = jnp.zeros(dv_acc.shape, F32)
    table_grad[...] = jnp.zeros(table_grad.shape, F32)
    key_at = lax.broadcasted_iota(jnp.int32, (128, 128), 0)
    query_at = lax.broadcasted_iota(jnp.int32, (128, 128), 1)
    upper = query_at >= key_at
    turn = (key_at + query_at == 127).astype(F32)

    def diagonals(m):
        m = lax.dot_general(
            turn, m, (((1,), (0,)), ((), ())), precision=HIGHEST, preferred_element_type=F32
        )
        return jnp.sum(pltpu.roll(m, 1, 1, stride=1, stride_axis=0), axis=0, keepdims=True)

    row_id = lax.broadcasted_iota(jnp.int32, (NB, 128), 0)
    lane_id = lax.broadcasted_iota(jnp.int32, (NB, 128), 1)
    hot_neg = bucket_of(-lane_id) == row_id
    hot_pos = bucket_of(128 - lane_id) == row_id

    for n, prob in enumerate(probs):
        near[...] = jnp.zeros(near.shape, F32)
        far[...] = jnp.zeros(far.shape, F32)
        for i in range(TP):
            at = slice(T * i, T * i + T)
            row_delta = delta[n, i]
            for j in range(TP):
                dp = dot(qkv[2 + 2 * second, j], dotm[n, i])
                ds = prob[i, j].astype(F32) * (dp - row_delta)
                dst[j] = ds.astype(BF16)
                for a in range(2):
                    for c in range(2):
                        gap = 2 * (j - i) + a - c
                        part = ds[128 * a : 128 * a + 128, 128 * c : 128 * c + 128]
                        if abs(gap) <= 1:
                            near[gap + 1] += part
                        else:
                            far[int(gap > 0)] += jnp.sum(part.reshape(16, 8, 128), axis=0)
            d_all = dst[...].reshape(TP * T, T)
            dq_acc[:, at] += dot(ktm[n], d_all)
            dk_acc[...] += dot(d_all, qm[n, i])
            dv_acc[...] += dot(prob[i].reshape(TP * T, T), dom[n, i])
        before, diagonal, after = near[0], near[1], near[2]
        neg = jnp.where(upper, diagonal, before)
        pos = jnp.where(upper, after, diagonal)
        neg, pos = diagonals(neg), diagonals(pos)
        far_neg = jnp.sum(far[0], axis=0, keepdims=True) + jnp.sum(
            jnp.where(upper, before, 0.0), axis=0, keepdims=True
        )
        far_pos = jnp.sum(far[1], axis=0, keepdims=True) + jnp.sum(
            jnp.where(upper, 0.0, after), axis=0, keepdims=True
        )
        spread = (
            jnp.where(hot_neg, neg, 0.0)
            + jnp.where(hot_pos, pos, 0.0)
            + jnp.where(row_id == 15, far_neg, 0.0)
            + jnp.where(row_id == 31, far_pos, 0.0)
        )
        sums = jnp.sum(spread, axis=1, keepdims=True)
        sums = jnp.sum(jnp.where(lane_id == row_id, sums, 0.0), axis=0, keepdims=True)
        h = heads[n]
        table_grad[h : h + 1] = sums
    for i in range(TP):
        at = slice(T * i, T * i + T)
        dq = jnp.transpose(dq_acc[:, at])
        if second:
            parts = (dq + dk_acc[at], dv_acc[at])
        else:
            parts = (dq, dk_acc[at], dv_acc[at])
        for n, part in enumerate(parts):
            dqkv[i, :, 128 * n : 128 * n + 128] = part.astype(BF16)


def one_grad_kernel(da, db, w, keep, give):
    j = lax.axis_index("blk")

    def body(k, carry):
        total = dot_nt(da[j ^ k], w[:, 0:384]) + dot_nt(db[j ^ k], w[:, 384:640])
        put_pair(keep, give, k, total.astype(BF16))
        return carry

    lax.fori_loop(0, TP, body, 0)


def finish(parts, w, out, gain):
    total = jnp.zeros((w.shape[0], 128), F32)
    for n, part in enumerate(parts):
        at = slice(128 * n, 128 * n + 128)
        total = total + part * w[:, at].astype(F32)
        out[:, at] = part
    return jnp.sum(total, axis=1, keepdims=True) / gain


def put_row(ref, wide):
    rows = wide.shape[0]
    row_id = lax.broadcasted_iota(jnp.int32, (rows, 128), 0)
    eye = row_id == lax.broadcasted_iota(jnp.int32, (rows, 128), 1)
    ref[...] = jnp.sum(jnp.where(eye, wide, 0.0), axis=0, keepdims=True)[:, 0:rows]


def first_final_kernel(b0, b1, b2, b3, gains, wg, wu, dg, du, gg2, mark, src):
    mark[...] = jnp.zeros((8, 128), F32)
    j_me = lax.axis_index("blk")
    low = low_half(wg.shape[0])
    for k, ref in enumerate((b0, b1, b2, b3)):
        src[j_me ^ k] = ref[:, 384:1408].astype(F32)
    gain_grad = 0.0
    for n, (w, out) in enumerate(((wg, dg), (wu, du))):
        parts = [None] * 16
        for t in range(4):
            at = slice(512 * n + 128 * t, 512 * n + 128 * t + 128)
            for half in range(2):
                a, b = src[2 * half, :, at], src[2 * half + 1, :, at]
                parts[4 * t + half] = jnp.where(low, a, pltpu.roll(b, 64, 1))
                parts[4 * t + 2 + half] = jnp.where(low, pltpu.roll(a, 64, 1), b)
        gain_grad = gain_grad + finish(parts, w, out, gains[1])
    put_row(gg2, gain_grad)


def second_final_kernel(
    a0, a1, a2, a3, b0, b1, b2, b3, gains, wq, wk, wv, dq, dk, dv, gg1, table, src
):
    j_me = lax.axis_index("blk")
    low = low_half(wq.shape[0])
    heads = jnp.zeros((128, 128), F32)
    head_id = lax.broadcasted_iota(jnp.int32, (128, 128), 0)
    for k, (first, second) in enumerate(zip((a0, a1, a2, a3), (b0, b1, b2, b3))):
        src[j_me ^ k, :, 0:384] = first[:, 0:384].astype(F32)
        src[j_me ^ k, :, 384:640] = second[:, 0:256].astype(F32)
        parts = second[:, 256:384].astype(F32)
        for h in range(HT):
            row = parts[h : h + 1] + parts[8 + h : 9 + h]
            heads = jnp.where(head_id == HT * (j_me ^ k) + h, row, heads)
    table[...] = heads[0:H, 0:NB]

    def one(j, n):
        return src[j, :, 128 * n : 128 * n + 128]

    gain_grad = 0.0
    for n, (w, out) in enumerate(((wq, dq), (wk, dk), (wv, dv))):
        parts = []
        for j in range(0, TP, 2):
            rest = []
            for m in (j, j + 1):
                last = one(m, 4 if n == 2 else 3)
                rest.append(pltpu.roll(last, 64, 1) if n == 1 else last)
            mid = pltpu.roll(one(j + 1, n), 64, 1)
            parts += [
                one(j, n),
                jnp.where(low, rest[0], mid),
                jnp.where(low, mid, pltpu.roll(rest[1], 64, 1)),
            ]
        gain_grad = gain_grad + finish(parts, w, out, gains[0])
    put_row(gg1, gain_grad)


def close_kernel(keep, got, along, mixed_grad, tok, gains, tokens_grad, mark):
    mark[...] = jnp.zeros((8, 128), F32)
    x = tok[lax.axis_index("blk")].astype(F32)
    rstd = lax.rsqrt(jnp.mean(x * x, axis=-1, keepdims=True) + EPSILON)
    n = x * rstd
    u = (keep[0].astype(F32) + got[0].astype(F32) + along[...].astype(F32)) * gains[0:1]
    grad = rstd * (u - n * jnp.mean(u * n, axis=-1, keepdims=True))
    tokens_grad[...] = mixed_grad[...] + grad


AXES = ("dp", "blk")
COST = {"qkv": 0, "attn_fwd": (0, 0, 0), "units": 15, "ffn": 0, "ffn_dw": 0, "mid": 0, "attn_bwd": (0, 10), "one_grad": 40, "stage_y": 0, "stage_z": 10, "first_back": 0}


def group_local(
    n_dp, n_blk,
    tokens, segment_ids, w_query, w_key, w_value, w_attn_out, attn_gain, rel_bias,
    w_gate, w_up, w_down, ffn_gain, cotangent,
):
    n_dev = n_dp * n_blk

    def later(x, *others):
        return lax.optimization_barrier((x,) + others)[0]

    def swap(x, mask):
        return lax.ppermute(x, AXES, [(d, d ^ mask) for d in range(n_dev)])

    def share(x, *others):
        along = swap(x, 2)
        return (x, swap(x, 1), along, swap(later(along, *others), 1))

    def reduce_pair(keep, give):
        got = swap(give, 1)
        return got, swap(keep[1] + got[1], 2)

    def round_one(x):
        other, near, far = lax.optimization_barrier((swap(x, 4), swap(x, 8), swap(x, 16)))
        return far, near, other

    def round_two(far, near):
        return lax.optimization_barrier((swap(far, 8), swap(near, 4), swap(far, 4)))

    def gathered(x, one, two, *others):
        far, near, other = one
        last, near_y, far_y = two
        return (x, near, far, last, other, near_y, far_y, swap(later(last, *others), 4))

    tok_own, cot_own = tokens[0], cotangent[0]
    rows, ff = w_query.shape[0], w_gate.shape[1]
    flat = TP * T
    table = rel_bias.astype(F32).T

    *slabs, tok_seg, gain_cols = call(
        prep_kernel,
        (sds((rows, 1664), BF16),) * TP + (sds((T + 16, D), BF16), sds((2, rows, 128), F32)),
        w_query, w_key, w_value, w_gate, w_up, tok_own, segment_ids, attn_gain, ffn_gain,
        name="prep", vmem=60, held=(0, 1, 2, 3, 4, 5),
        scratch=(
            pltpu.VMEM((TP, rows, 1664), BF16),
            *(pltpu.VMEM((rows, D), BF16),) * 3,
            *(pltpu.VMEM((rows, ff), BF16),) * 2,
            pltpu.SemaphoreType.DMA((6,)),
        ),
    )
    toks_x, toks_c = swap(tok_seg, 2), swap(tok_seg, 1)
    slabs = (slabs[0], swap(slabs[1], 1), swap(slabs[2], 2), swap(slabs[3], 3))
    first = call(
        pack_kernel, sds((128, 640), BF16), *slabs, w_attn_out,
        name="pack", vmem=30, held=(4,),
        scratch=(pltpu.VMEM((96, 640), F32), pltpu.VMEM((rows, D), BF16), pltpu.SemaphoreType.DMA),
    )
    second = call(
        pack_more_kernel, sds((576, 256), BF16), *slabs, w_down,
        name="pack_more", vmem=30, held=(4,), after=(first,),
        scratch=(pltpu.VMEM((96, 1024), F32), pltpu.VMEM((64, D), BF16), pltpu.SemaphoreType.DMA),
    )
    first_one = round_one(first)
    bias = call(
        bias_kernel, sds((HT, 3, T, T), F32), table, smem=(0,), name="bias", after=(second,)
    )
    near, far = lax.optimization_barrier((*first_one[::-1], second, bias))[1:3]
    first_two = round_two(far, near)
    toks_r = swap(later(toks_x, *first_two), 1)
    firsts = gathered(first, first_one, first_two, *())
    toks = (tok_seg, toks_c, toks_x, toks_r)
    second_one = (
        swap(later(second, *first_one), 16),
        swap(later(second, *first_two), 8),
        swap(later(second, *first_two), 4),
    )

    tok, n1, qkv, w_qkv, gains, segq, segk = call(
        qkv_kernel,
        (
            sds((TP, T, D), BF16), sds((TP, T, D), BF16), sds((5, TP, T, 128), BF16),
            sds((D, 640), BF16), sds((8, D), F32), sds((TP, 8, T), F32), sds((TP, T, T), F32),
        ),
        *toks, *firsts, name="qkv", vmem=16, cost=COST["qkv"],
    )
    stripes = call(
        stripes_kernel, sds((192, D), BF16), *firsts, name="stripes", after=(segq,),
        scratch=(pltpu.VMEM((192, D), F32),),
    )
    stripes = share(stripes)
    wop = call(
        out_weight_kernel, sds((D, D), BF16), *stripes, name="out_weight",
        scratch=(pltpu.VMEM((D, D), F32),),
    )
    cots_x = swap(later(cot_own, *(gains,)), 2)
    heads = []
    for h in range(HT):
        heads.append(
            call(
                functools.partial(attn_fwd_kernel, h),
                (sds((TP, TP, T, T), BF16), sds((TP, 1, T), F32), sds((DH, flat), F32)),
                table, bias, qkv, segq, segk, smem=(0,), name="attn_fwd", vmem=14,
                cost=COST["attn_fwd"][h], after=((heads[-1][1],) if heads else ()) + ((cots_x,) if h == 2 else ()),
                scratch=(
                    pltpu.VMEM((TP, 128, T), BF16),
                    pltpu.VMEM((DH, flat), BF16),
                    pltpu.VMEM((TP, T, T), F32),
                ),
            )
        )
    probs, inv_tots, out_ts = zip(*heads)
    cots = (cot_own, swap(later(cot_own, inv_tots[2]), 1), cots_x, swap(later(cots_x, inv_tots[2]), 1))
    far, near = lax.optimization_barrier(second_one + (inv_tots[0],))[:2]
    second_two = round_two(far, near)
    seconds = gathered(second, second_one, second_two)
    att = call(join_kernel, sds((1536, 128), BF16), *out_ts, name="join")
    atts = share(att, wop)
    wgu, wd = call(
        units_kernel, (sds((D, 1024), BF16), sds((512, D), BF16)), *seconds, name="units",
        cost=COST["units"],
    )

    def ffn(ks, *after):
        return call(
            functools.partial(ffn_kernel, ks),
            (
                sds((2, T, D), BF16), sds((2, T, 512), BF16), sds((2, T, 1024), BF16),
                sds((T, D), BF16), sds((T, D), BF16), sds((2, T, D), BF16), sds((T, D), F32),
            ),
            *atts, gains, wop, wgu, wd, tok, cots[ks[0]], cots[ks[1]], name="ffn", vmem=24,
            cost=COST["ffn"], after=after,
        )

    n2_a, hid_a, ggug_a, keep, give, _, _ = ffn((2, 3))
    two_x = keep + swap(give, 1)
    n2_b, hid_b, ggug_b, two_keep, give, attc, mixed_own = ffn((0, 1), two_x)
    two_x = swap(two_x, 2)
    two_c = swap(give, 1)
    y_keep, y_give, z_keep, z_give, lo_keep, lo_give = call(
        ffn_dw_kernel, (sds((4, 288, 256), BF16),) * 4 + (sds((2, T, D), BF16),) * 2,
        n2_a.reshape(2 * T, D), ggug_a.reshape(2 * T, 1024), hid_a.reshape(2 * T, 512),
        n2_b.reshape(2 * T, D), ggug_b.reshape(2 * T, 1024), hid_b.reshape(2 * T, 512),
        *cots, wd, name="ffn_dw", vmem=20, cost=COST["ffn_dw"],
        scratch=(pltpu.VMEM((D, 1024), F32), pltpu.VMEM((512, D), F32)),
    )
    y_got, z_got = swap(y_give, 4), swap(z_give, 8)
    lo_c = swap(later(lo_give, *()), 1)
    lo_sum = lo_keep[1] + lo_c[1]
    mixed_grad, g0, g1, g2, g3, wo_keep, *wo_gives = call(
        mid_kernel,
        (sds((T, D), F32),) + (sds((384, 128), BF16),) * 4
        + (sds((2, 8, 24, D), BF16),) + (sds((8, 24, D), BF16),) * 2,
        two_keep, two_c, two_x, mixed_own, cot_own, attc, wop, gains, name="mid", vmem=16,
        after=(y_give, *()), scratch=(pltpu.VMEM((D, D), F32),), cost=COST["mid"],
    )
    g1, g2, g3 = swap(g1, 1), swap(g2, 2), swap(g3, 3)
    wo_got = (swap(later(wo_gives[0], g1), 1), swap(later(wo_gives[1], g1), 1))
    wo_sum = later(wo_keep[1] + wo_got[1], g1, g2, g3)
    wo_along = swap(wo_sum, 2)

    def attn_bwd(second, *after):
        mine = slice(2, 3) if second else slice(0, 2)
        count = 1 if second else 2
        return call(
            functools.partial(attn_bwd_kernel, second),
            (sds((TP, T, 256 if second else 384), BF16), sds((8, 128), F32)),
            qkv, *probs[mine], *inv_tots[mine], *out_ts[mine], g0, g1, g2, g3,
            name="attn_bwd", vmem=22, cost=COST["attn_bwd"][second], after=after,
            scratch=(
                pltpu.VMEM((count, TP, 128, T), BF16),
                pltpu.VMEM((count, TP, T, 128), BF16),
                pltpu.VMEM((count, TP, T, 128), BF16),
                pltpu.VMEM((count, 128, TP * T), BF16),
                pltpu.VMEM((count, TP, 1, T), F32),
                pltpu.VMEM((TP, T, T), BF16),
                pltpu.VMEM((128, TP * T), F32),
                pltpu.VMEM((TP * T, 128), F32),
                pltpu.VMEM((TP * T, 128), F32),
                pltpu.VMEM((3, 128, 128), F32),
                pltpu.VMEM((2, 8, 128), F32),
            ),
        )

    def chunks(n, chunk):
        return sds((n * chunk + (TAIL if chunk == SECOND else 0), 128), BF16)

    def stage(n, chunk, keep, got, name, *after):
        return call(
            functools.partial(stage_kernel, n, chunk), (chunks(n // 2, chunk),) * 2, keep, got,
            name=name, after=after, cost=COST[name],
        )

    da, ta = attn_bwd(0, *(wo_sum,))
    a_keep, a_give = call(
        first_dw_kernel, (chunks(4, FIRST),) * 2, n1.reshape(flat, D), da.reshape(flat, 384),
        name="first_dw", vmem=12, scratch=(pltpu.VMEM((D, 384), F32),),
    )
    a_got = swap(a_give, 4)
    y_keep, y_give, z_keep, z_give = call(
        ffn_second_kernel, (sds((2, 288, 256), BF16),) * 4, y_keep, y_got, z_keep, z_got,
        name="ffn_second", after=(a_give,),
    )
    y_got, z_got = swap(y_give, 8), swap(z_give, 16)
    db, tb = attn_bwd(1, y_give, *(lo_sum,))
    b_keep, b_give = call(
        second_dw_kernel, (chunks(4, SECOND),) * 2,
        n1.reshape(flat, D), db.reshape(flat, 256), wo_keep, wo_got[0], wo_along, ta, tb,
        name="second_dw", vmem=12,
        scratch=(
            pltpu.VMEM((D, 256), F32), pltpu.VMEM((8, 24, D), F32), pltpu.VMEM((SECOND, 128), F32),
        ),
    )
    b_got = swap(b_give, 4)
    one_keep, one_give = call(
        one_grad_kernel, (sds((2, T, D), BF16),) * 2, da, db, w_qkv, name="one_grad", vmem=16,
        after=(b_give,), cost=COST["one_grad"],
    )
    lo_x = swap(later(lo_sum, *(db,)), 2)
    one_c = swap(one_give, 1)
    one_x = swap(later(one_keep[1] + one_c[1], *(lo_x,)), 2)
    a_keep, a_give = stage(4, FIRST, a_keep, a_got, "stage_y", b_give)
    a_got = swap(a_give, 8)
    y_give, z_give = call(
        ffn_third_kernel, (sds((288, 256), BF16),) * 2, y_keep, y_got, z_keep, z_got,
        name="ffn_third", after=(a_give,),
    )
    y_along, z_along = swap(y_give, 16), swap(z_give, 4)
    b_keep, b_give = stage(4, SECOND, b_keep, b_got, "stage_y", *(y_give,))
    b_got = swap(b_give, 8)
    a_keep, a_give = stage(2, FIRST, a_keep, a_got, "stage_z", b_give)
    a_got = swap(a_give, 16)
    b_keep, b_give = stage(2, SECOND, b_keep, b_got, "stage_z", *(a_give,))
    b_got = swap(b_give, 16)
    layer_out = mixed_own + lo_keep[0].astype(F32) + lo_c[0].astype(F32) + lo_x.astype(F32)
    tokens_grad, mark = call(
        close_kernel, (sds((T, D), F32), sds((8, 128), F32)), one_keep, one_c, one_x, mixed_grad, tok, gains,
        name="close", vmem=10, after=(a_got,),
    )
    dwd, *backs = call(
        first_back_kernel, (sds((64, D), F32),) + (sds((rows, 1408), BF16),) * 4,
        a_keep, a_got, y_keep, y_got, y_along, z_keep, z_got, z_along,
        name="first_back", after=(b_give,), cost=COST["first_back"],
        scratch=(pltpu.VMEM((FIRST, 128), F32), pltpu.VMEM((576, 256), F32)),
    )
    firsts = (backs[0], swap(backs[1], 1), swap(backs[2], 2), swap(backs[3], 3))
    dwo, *backs = call(
        second_back_kernel, (sds((rows, D), F32),) + (sds((rows, 384), BF16),) * 4, b_keep, b_got,
        name="second_back", after=(mark, *firsts[1:]), scratch=(pltpu.VMEM((SECOND, 128), F32),),
    )
    seconds = (backs[0], swap(backs[1], 1), swap(backs[2], 2), swap(backs[3], 3))
    dg, du, gg2, mark = call(
        first_final_kernel,
        (sds((rows, ff), F32),) * 2 + (sds((1, rows), F32), sds((8, 128), F32)),
        *firsts, gain_cols, w_gate, w_up, name="first_final",
        scratch=(pltpu.VMEM((TP, rows, 1024), F32),),
    )
    dq, dk, dv, gg1, table_sum = call(
        second_final_kernel,
        (sds((rows, D), F32),) * 3 + (sds((1, rows), F32), sds((H, NB), F32)),
        *firsts, *seconds, gain_cols, w_query, w_key, w_value, name="second_final", after=(mark,),
        scratch=(pltpu.VMEM((TP, rows, 640), F32),),
    )
    return (
        layer_out.astype(BF16)[None],
        tokens_grad[None],
        dq,
        dk,
        dv,
        dwo,
        gg1[0],
        table_sum.T,
        dg,
        du,
        dwd,
        gg2[0],
    )


KEY_BLOCK = 256
HIGHEST = lax.Precision.HIGHEST


def rms_norm(values, gain):
    return values * lax.rsqrt(jnp.mean(values * values, axis=-1, keepdims=True) + EPSILON) * gain


def split_heads(flat_rows):
    return flat_rows.reshape(flat_rows.shape[0], flat_rows.shape[1], H, DH)


def join_heads(per_head):
    return per_head.reshape(per_head.shape[0], per_head.shape[1], H * DH)


def project(left, matrix):
    return jnp.einsum("rtd,de->rte", left, matrix, preferred_element_type=jnp.float32)


def project_back(left, matrix):
    return jnp.einsum("rte,de->rtd", left, matrix, preferred_element_type=jnp.float32)


def weight_grad(left, right):
    return jnp.einsum("rtd,rte->de", left, right, preferred_element_type=jnp.float32)


def block_scores(queries, key_block, query_pos, key_pos, query_seg, key_seg, bias_table):
    raw_scores = jnp.einsum(
        "rqhd,rkhd->rhqk", queries, key_block, preferred_element_type=jnp.float32
    )
    buckets = bucket_of(key_pos[None, :] - query_pos[:, None])
    one_hot = (buckets[:, :, None] == jnp.arange(NB, dtype=jnp.int32)[None, None, :]).astype(
        jnp.float32
    )
    rel_term = jnp.einsum("qkb,bh->hqk", one_hot, bias_table, precision=HIGHEST)
    allowed = (query_seg[:, :, None] == key_seg[:, None, :])[:, None]
    return (raw_scores + rel_term[None], allowed, one_hot)


def absorb(
    running, queries, key_block, value_block, query_pos, key_pos, query_seg, key_seg, bias_table
):
    row_peak, row_total, weighted = running
    scores, allowed, unused = block_scores(
        queries, key_block, query_pos, key_pos, query_seg, key_seg, bias_table
    )
    block_peak = jnp.max(jnp.where(allowed, scores, MASKED), axis=-1)
    new_peak = jnp.maximum(row_peak, block_peak)
    weights = jnp.where(allowed, jnp.exp(scores - new_peak[..., None]), 0.0)
    factor = jnp.exp(row_peak - new_peak)
    row_total = row_total * factor + jnp.sum(weights, axis=-1)
    weighted = weighted * factor[..., None] + jnp.einsum(
        "rhqk,rkhd->rhqd",
        weights.astype(jnp.bfloat16),
        value_block,
        preferred_element_type=jnp.float32,
    )
    return (new_peak, row_total, weighted)


def pair_grads(
    queries,
    out_grad,
    log_total,
    row_delta,
    key_block,
    value_block,
    query_pos,
    key_pos,
    query_seg,
    key_seg,
    bias_table,
):
    scores, allowed, one_hot = block_scores(
        queries, key_block, query_pos, key_pos, query_seg, key_seg, bias_table
    )
    prob_map = jnp.where(allowed, jnp.exp(scores - log_total[..., None]), 0.0)
    prob_grad = jnp.einsum(
        "rqhd,rkhd->rhqk", out_grad, value_block, preferred_element_type=jnp.float32
    )
    score_grad = prob_map * (prob_grad - row_delta[..., None])
    score_low = score_grad.astype(jnp.bfloat16)
    query_grad = jnp.einsum(
        "rhqk,rkhd->rqhd", score_low, key_block, preferred_element_type=jnp.float32
    )
    key_grad = jnp.einsum("rhqk,rqhd->rkhd", score_low, queries, preferred_element_type=jnp.float32)
    value_grad = jnp.einsum(
        "rhqk,rqhd->rkhd",
        prob_map.astype(jnp.bfloat16),
        out_grad,
        preferred_element_type=jnp.float32,
    )
    table_grad = jnp.einsum("rhqk,qkb->bh", score_grad, one_hot, precision=HIGHEST)
    return (query_grad, key_grad, value_grad, table_grad)


def in_blocks(step_fn, running, pieces):
    length = pieces[0].shape[1]
    block_size = math.gcd(length, KEY_BLOCK)
    block_count = length // block_size
    stacked = tuple(
        (
            jnp.moveaxis(
                member.reshape((member.shape[0], block_count, block_size) + member.shape[2:]), 1, 0
            )
            for member in pieces
        )
    )
    starts = block_size * jnp.arange(block_count, dtype=jnp.int32)

    def scan_step(inner_state, item_pair):
        return (step_fn(inner_state, item_pair[0], item_pair[1]), None)

    running, unused = lax.scan(scan_step, running, (stacked, starts))
    return running


def local(
    tokens,
    segment_ids,
    w_query,
    w_key,
    w_value,
    w_attn_out,
    attn_gain,
    rel_bias,
    w_gate,
    w_up,
    w_down,
    ffn_gain,
    cotangent,
):
    row_count, local_len, unused_dim = tokens.shape
    my_block = lax.axis_index("blk")
    full_query, full_key, full_value, full_out, gain_one = (
        lax.all_gather(w_query, ("dp", "blk"), axis=0, tiled=True),
        lax.all_gather(w_key, ("dp", "blk"), axis=0, tiled=True),
        lax.all_gather(w_value, ("dp", "blk"), axis=0, tiled=True),
        lax.all_gather(w_attn_out, ("dp", "blk"), axis=0, tiled=True),
        lax.all_gather(attn_gain, ("dp", "blk"), axis=0, tiled=True),
    )
    full_gate, full_up, full_down, gain_two = (
        lax.all_gather(w_gate, ("dp", "blk"), axis=0, tiled=True),
        lax.all_gather(w_up, ("dp", "blk"), axis=0, tiled=True),
        lax.all_gather(w_down, ("dp", "blk"), axis=0, tiled=True),
        lax.all_gather(ffn_gain, ("dp", "blk"), axis=0, tiled=True),
    )
    row_segs = lax.all_gather(segment_ids, "blk", axis=1, tiled=True)
    bias_table = rel_bias.astype(jnp.float32)
    gain_one_f = gain_one.astype(jnp.float32)
    gain_two_f = gain_two.astype(jnp.float32)
    inputs = tokens.astype(jnp.float32)
    query_pos = my_block * local_len + jnp.arange(local_len, dtype=jnp.int32)
    normed_one = rms_norm(inputs, gain_one_f).astype(jnp.bfloat16)
    query_flat = project(normed_one, full_query).astype(jnp.bfloat16)
    key_flat = project(normed_one, full_key).astype(jnp.bfloat16)
    value_flat = project(normed_one, full_value).astype(jnp.bfloat16)
    queries = split_heads(query_flat)
    key_heads = split_heads(key_flat)
    value_heads = split_heads(value_flat)

    def forward_piece(running, pieces):

        def step_fn(inner_state, blocks, block_start):
            block_len = blocks[0].shape[1]
            key_pos = block_start + jnp.arange(block_len, dtype=jnp.int32)
            key_seg = lax.dynamic_slice_in_dim(row_segs, block_start, block_len, 1)
            return absorb(
                inner_state,
                queries,
                split_heads(blocks[0]),
                split_heads(blocks[1]),
                query_pos,
                key_pos,
                segment_ids,
                key_seg,
                bias_table,
            )

        return in_blocks(step_fn, running, pieces)

    stat_shape = (row_count, H, local_len)
    start_state = (
        jnp.full(stat_shape, MASKED, jnp.float32),
        jnp.zeros(stat_shape, jnp.float32),
        jnp.zeros(stat_shape + (DH,), jnp.float32),
    )
    row_peak, row_total, weighted = forward_piece(
        start_state,
        (
            lax.all_gather(key_flat, "blk", axis=1, tiled=True),
            lax.all_gather(value_flat, "blk", axis=1, tiled=True),
        ),
    )
    log_total = row_peak + jnp.log(row_total)
    attended_f = jnp.transpose(weighted / row_total[..., None], (0, 2, 1, 3))
    attended = join_heads(attended_f).astype(jnp.bfloat16)
    mixed_in = inputs + project(attended, full_out)
    normed_two = rms_norm(mixed_in, gain_two_f).astype(jnp.bfloat16)
    gate_act = project(normed_two, full_gate)
    up_act = project(normed_two, full_up)

    def gated(gate_in, up_in):
        return jax.nn.gelu(gate_in, approximate=True) * up_in

    hidden_f, gated_back = jax.vjp(gated, gate_act, up_act)
    hidden = hidden_f.astype(jnp.bfloat16)
    layer_out = (mixed_in + project(hidden, full_down)).astype(jnp.bfloat16)
    down_grad = weight_grad(hidden, cotangent)
    hidden_grad = project_back(cotangent, full_down)
    gate_grad, up_grad = gated_back(hidden_grad)
    gate_low = gate_grad.astype(jnp.bfloat16)
    up_low = up_grad.astype(jnp.bfloat16)
    gate_w_grad = weight_grad(normed_two, gate_low)
    up_w_grad = weight_grad(normed_two, up_low)
    two_grad = project_back(gate_low, full_gate) + project_back(up_low, full_up)
    unused_two, norm_two_back = jax.vjp(rms_norm, mixed_in, gain_two_f)
    mixed_part, gain_two_grad = norm_two_back(two_grad)
    mixed_grad = cotangent.astype(jnp.float32) + mixed_part
    mixed_low = mixed_grad.astype(jnp.bfloat16)
    out_w_grad = weight_grad(attended, mixed_low)
    attended_grad = project_back(mixed_low, full_out).astype(jnp.bfloat16)
    grad_heads = split_heads(attended_grad)
    row_delta = jnp.sum(
        jnp.transpose(grad_heads.astype(jnp.float32), (0, 2, 1, 3))
        * (weighted / row_total[..., None]),
        axis=-1,
    )
    zero_heads = jnp.zeros(queries.shape, jnp.float32)
    zero_table = jnp.zeros((NB, H), jnp.float32)

    def query_piece(running, pieces):

        def step_fn(inner_state, blocks, block_start):
            block_len = blocks[0].shape[1]
            key_pos = block_start + jnp.arange(block_len, dtype=jnp.int32)
            key_seg = lax.dynamic_slice_in_dim(row_segs, block_start, block_len, 1)
            pair_parts = pair_grads(
                queries,
                grad_heads,
                log_total,
                row_delta,
                split_heads(blocks[0]),
                split_heads(blocks[1]),
                query_pos,
                key_pos,
                segment_ids,
                key_seg,
                bias_table,
            )
            return inner_state + pair_parts[0]

        return in_blocks(step_fn, running, pieces)

    query_grad = join_heads(
        query_piece(
            zero_heads,
            (
                lax.all_gather(key_flat, "blk", axis=1, tiled=True),
                lax.all_gather(value_flat, "blk", axis=1, tiled=True),
            ),
        )
    )
    log_rows, delta_rows = (
        lax.all_gather(log_total, "blk", axis=2, tiled=True),
        lax.all_gather(row_delta, "blk", axis=2, tiled=True),
    )

    def key_piece(running, pieces):

        def step_fn(inner_state, blocks, block_start):
            block_len = blocks[0].shape[1]
            piece_pos = block_start + jnp.arange(block_len, dtype=jnp.int32)
            piece_seg = lax.dynamic_slice_in_dim(row_segs, block_start, block_len, 1)
            piece_log = lax.dynamic_slice_in_dim(log_rows, block_start, block_len, 2)
            piece_delta = lax.dynamic_slice_in_dim(delta_rows, block_start, block_len, 2)
            pair_parts = pair_grads(
                split_heads(blocks[0]),
                split_heads(blocks[1]),
                piece_log,
                piece_delta,
                key_heads,
                value_heads,
                piece_pos,
                query_pos,
                piece_seg,
                segment_ids,
                bias_table,
            )
            return (
                inner_state[0] + pair_parts[1],
                inner_state[1] + pair_parts[2],
                inner_state[2] + pair_parts[3],
            )

        return in_blocks(step_fn, running, pieces)

    key_grad, value_grad, table_grad = key_piece(
        (zero_heads, zero_heads, zero_table),
        (
            lax.all_gather(query_flat, "blk", axis=1, tiled=True),
            lax.all_gather(attended_grad, "blk", axis=1, tiled=True),
        ),
    )
    query_low = query_grad.astype(jnp.bfloat16)
    key_low = join_heads(key_grad).astype(jnp.bfloat16)
    value_low = join_heads(value_grad).astype(jnp.bfloat16)
    query_w_grad = weight_grad(normed_one, query_low)
    key_w_grad = weight_grad(normed_one, key_low)
    value_w_grad = weight_grad(normed_one, value_low)
    one_grad = (
        project_back(query_low, full_query)
        + project_back(key_low, full_key)
        + project_back(value_low, full_value)
    )
    unused_one, norm_one_back = jax.vjp(rms_norm, inputs, gain_one_f)
    input_part, gain_one_grad = norm_one_back(one_grad)
    tokens_grad = mixed_grad + input_part
    table_sum = lax.psum(table_grad, ("dp", "blk"))
    all_sums = (
        lax.psum_scatter(query_w_grad, ("dp", "blk"), scatter_dimension=0, tiled=True),
        lax.psum_scatter(key_w_grad, ("dp", "blk"), scatter_dimension=0, tiled=True),
        lax.psum_scatter(value_w_grad, ("dp", "blk"), scatter_dimension=0, tiled=True),
        lax.psum_scatter(out_w_grad, ("dp", "blk"), scatter_dimension=0, tiled=True),
        lax.psum_scatter(gain_one_grad, ("dp", "blk"), scatter_dimension=0, tiled=True),
        lax.psum_scatter(gate_w_grad, ("dp", "blk"), scatter_dimension=0, tiled=True),
        lax.psum_scatter(up_w_grad, ("dp", "blk"), scatter_dimension=0, tiled=True),
        lax.psum_scatter(down_grad, ("dp", "blk"), scatter_dimension=0, tiled=True),
        lax.psum_scatter(gain_two_grad, ("dp", "blk"), scatter_dimension=0, tiled=True),
    )
    return (
        layer_out,
        tokens_grad,
        all_sums[0],
        all_sums[1],
        all_sums[2],
        all_sums[3],
        all_sums[4],
        table_sum,
        all_sums[5],
        all_sums[6],
        all_sums[7],
        all_sums[8],
    )


def solution(mesh):
    whole = P(AXES, None)
    rows = P("dp", "blk", None)
    n_dp, n_blk = mesh.shape["dp"], mesh.shape["blk"]
    grouped = functools.partial(group_local, n_dp, n_blk)
    body = grouped if (n_dp, n_blk) == (8, TP) else local
    return jax.shard_map(
        body,
        mesh=mesh,
        in_specs=(
            rows, P("dp", "blk"), whole, whole, whole, whole, P(AXES), P(),
            whole, whole, whole, P(AXES), rows,
        ),
        out_specs=(
            rows, rows, whole, whole, whole, whole, P(AXES), P(), whole, whole, whole, P(AXES),
        ),
        check_vma=False,
    )
```
